32 devices in a mesh: dp: 2 (over core), expert: 16 (over z, y, x).
Axes of the slice: x: 2, y: 2, z: 4, core: 2. Of those that a mesh axis runs over, the one named last changes fastest.
Arguments:
- tokens: bfloat16 [32768, 1024], P(('dp', 'expert')), may hold values from -6 to 6
- cotangent: bfloat16 [32768, 1024], P(('dp', 'expert')), may hold values from -6 to 6
- segment_ids: int32 [32, 1024], P(('dp', 'expert')), may hold values from 0 to 7, never falling along the last dimension, each value on 1 to 512 neighbouring positions
- expert_ids: int32 [32768, 1], P(('dp', 'expert')), may hold values from 0 to 15; in each aligned block of 1024 rows (0 to 1023, 1024 to 2047, ...) at most 96 rows name the same one
- qkv_weight: bfloat16 [3, 1024, 1024], P(None, None, 'dp'), may hold values from -0.1875 to 0.1875
- proj_weight: bfloat16 [1024, 1024], P('dp'), may hold values from -0.75 to 0.75
- proj_bias: bfloat16 [1024], replicated, may hold values from -1 to 1
- pre_gain: bfloat16 [1024], replicated, may hold values from 0.5 to 1.5
- pre_shift: bfloat16 [1024], replicated, may hold values from -1 to 1
- mid_gain: bfloat16 [1024], replicated, may hold values from 0.5 to 1.5
- mid_shift: bfloat16 [1024], replicated, may hold values from -1 to 1
- up_weight: bfloat16 [16, 4096, 1024], P('expert', 'dp'), may hold values from -0.1875 to 0.1875
- up_bias: bfloat16 [16, 4096], P('expert', 'dp'), may hold values from -1.5 to 1.5
- down_weight: bfloat16 [16, 4096, 1024], P('expert', 'dp'), may hold values from -0.09375 to 0.09375
- down_bias: bfloat16 [16, 1024], P('expert'), may hold values from -1 to 1
Outputs:
- output: bfloat16 [32768, 1024], P(('dp', 'expert'))
- input_grad: float32 [32768, 1024], P(('dp', 'expert'))
- qkv_grad: float32 [3, 1024, 1024], P(None, None, 'dp')
- proj_grad: float32 [1024, 1024], P('dp')
- projbias_grad: float32 [1024], replicated
- pregain_grad: float32 [1024], replicated
- before_offset_gradient: float32 [1024], replicated
- midgain_grad: float32 [1024], replicated
- midshift_grad: float32 [1024], replicated
- up_grad: float32 [16, 4096, 1024], P('expert', 'dp')
- upbias_grad: float32 [16, 4096], P('expert', 'dp')
- down_grad: float32 [16, 4096, 1024], P('expert', 'dp')
- downbias_grad: float32 [16, 1024], P('expert')
The draws below stay inside these ranges and needn't reach their ends.
Inputs may be any that keep to these rules, and one draw needn't show every extreme that they name: `expert_ids`: in the rows of one device (each aligned block of 1024 rows) no expert is named more than 96 times, a bound that some block reaches. `segment_ids`: along each sequence of 1024 positions the ids never fall; a document holds at most 512 positions.
All inputs are finite; a program needn't handle non-finite values.
Results may differ from the reference program's by a relative error of at most 0.017.
Values may be sent and summed in bfloat16 or wider, within the bound.
A program may use at most 320 MiB of HBM per device.

```python
import math
import jax
import jax.numpy as jnp
import numpy as np
from jax import lax

D = 1024
HEADS = 16
HEAD_DIM = 64
FF = 4096
EXP_DEV = 1
SEQ = 1024
DOCS = 8
EXPERTS = 16
TOK_DEV = 1024
TOKENS = 32768
SEQS = 32
CAP = 96
N_DP = 2
N_EXPERT = 16


def shard_levels(rng, dims, shards, least, top_value):
    level = 1.0
    for axis_at, shards_of in shards:
        steps = jax.random.uniform(jax.random.fold_in(jax.random.fold_in(rng, 6), axis_at), (shards_of,), jnp.float32, least / len(shards), top_value / len(shards))
        level = level * jnp.repeat(jnp.exp(steps), dims[axis_at] // shards_of).reshape((-1,) + (1,) * (len(dims) - 1 - axis_at))
    return level


def split_up(amount, total, limit, lean):
    portions = [(1 << 20) // math.isqrt(standing ** lean) + 1 for standing in range(2, amount + 1)]
    spare, given = total - limit - (amount - 1), [1] * (amount - 1)
    while spare > 0:
        movable = [i for i in range(amount - 1) if given[i] < limit]
        whole, remaining = sum([portions[i] for i in movable]), spare
        for i in movable:
            more = min(limit - given[i], max(1, remaining * portions[i] // whole), spare)
            given[i] = given[i] + more
            spare = spare - more
    return np.array([limit] + given)


def ragged(stream_key, number_of, total, limit, skew):
    if number_of == 2:
        one = jax.random.randint(stream_key, (), max(1, total - limit), min(limit, total - 1) + 1)
        return jnp.stack([one, total - one])
    lengths = jnp.asarray(split_up(number_of, total, limit, skew), jnp.int32)
    pairs = (number_of - 1) // 2
    donor, taker = lengths[1:1 + 2 * pairs:2], lengths[2:2 + 2 * pairs:2]
    margin = jnp.minimum(donor - 1, limit - taker)
    shifted = jax.random.randint(jax.random.fold_in(stream_key, 1), (pairs,), 0, 1 << 20) % (margin + 1)
    lengths = lengths.at[1:1 + 2 * pairs:2].set(donor - shifted).at[2:2 + 2 * pairs:2].set(taker + shifted)
    return lengths[jax.random.permutation(jax.random.fold_in(stream_key, 2), number_of)]


def assign_block(key, own, number, rows, count, top, most, skew):
    sequence = jax.random.permutation(key, count)
    crowded, ordinary = portions_of(count, rows * top, most, skew, True), portions_of(count, rows * top, most, skew, False)
    places = jnp.arange(count)

    def named(sizes, rotation):
        used = int((sizes > 0).sum())
        fixed = max(1, used // 4)
        passed = fixed + (places - fixed + rotation * (used - fixed)) % max(1, count - fixed)
        return jnp.zeros((count,), jnp.int32).at[sequence[jnp.where(places < fixed, places, passed)]].set(jnp.asarray(sizes, jnp.int32))

    sizes = jnp.where(number % 4 == 0, named(crowded, number // 4), named(ordinary, number - number // 4 - 1))
    mixed = jax.random.permutation(jax.random.fold_in(own, 3), count)
    donor, sink = mixed[0:count // 2 * 2:2], mixed[1:count // 2 * 2:2]
    slack = jnp.minimum(sizes[donor] - 1, most - sizes[sink]) // 2
    slack = jnp.where((donor == sequence[0]) | (sink == sequence[0]) | (sizes[sink] == 0), 0, jnp.maximum(slack, 0))
    passed = jax.random.randint(jax.random.fold_in(own, 4), (count // 2,), 0, 1 << 20) % (slack + 1)
    sizes = sizes.at[donor].add(-passed).at[sink].add(passed)
    members = jnp.searchsorted(jnp.cumsum(sizes), jnp.arange(rows * top), side="right").astype(jnp.int32)
    table = members.reshape(top, rows).T
    table = table[jax.random.permutation(jax.random.fold_in(own, 1), rows)]
    rotation = jax.random.randint(jax.random.fold_in(own, 2), (rows, 1), 0, top)
    return jnp.take_along_axis(table, (jnp.arange(top)[None, :] + rotation) % top, axis=1)


def portions_of(count, total, limit, slope, full):
    weights = [(1 << 20) // math.isqrt(rank ** slope) + 1 for rank in range(1, count + 1)]
    largest = limit if full else min(limit, max(-(-total // count), total * weights[0] // sum(weights)))
    least = 1 if total - largest >= count - 1 else 0
    counts, surplus = [largest] + [least] * (count - 1), total - largest - least * (count - 1)
    while surplus > 0:
        free = [i for i in range(1, count) if counts[i] < largest] or [i for i in range(1, count) if counts[i] < limit]
        mass, left = sum([weights[i] for i in free]), surplus
        for i in free:
            more = min(limit - counts[i], max(1, left * weights[i] // mass), surplus)
            counts[i] = counts[i] + more
            surplus = surplus - more
    return np.array(counts)


def scatter_about(rng, shape, scale, bound, cuts=(), kind=jnp.bfloat16):
    values = scale * jax.random.normal(rng, shape, jnp.float32)
    if cuts:
        values = values * shard_levels(rng, shape, cuts, -0.22, 0.18)
    return jnp.clip(values, -bound, bound).astype(kind)


def setup_inputs(seed: int = 0) -> dict:
    key_of = jax.random.split(jax.random.key(seed), 16)
    tokens = scatter_about(key_of[0], (TOKENS, D), 1.0, 6.0, ((0, 32),))
    cotangent = scatter_about(key_of[1], (TOKENS, D), 1.0, 6.0, ((0, 32),))
    segment_ids = jax.vmap(lambda own: jnp.searchsorted(jnp.cumsum(ragged(own, DOCS, SEQ, SEQ // 2, 1)), jnp.arange(SEQ), side="right"))(jax.random.split(key_of[2], SEQS)).reshape((SEQS, SEQ)).astype(jnp.int32)
    expert_ids_keys = jax.random.split(jax.random.fold_in(key_of[3], 1), TOKENS // TOK_DEV)
    expert_ids_turns = jax.random.permutation(jax.random.fold_in(key_of[3], 3), TOKENS // TOK_DEV)
    expert_ids = jax.vmap(lambda own, number: assign_block(jax.random.fold_in(key_of[3], 2), own, number, TOK_DEV, EXPERTS, 1, CAP, 1))(expert_ids_keys, expert_ids_turns).reshape((TOKENS, 1))
    qkv_weight = scatter_about(key_of[4], (3, D, D), D ** -0.5, 0.1875, ((2, 2),))
    proj_weight = scatter_about(key_of[5], (D, D), (D // 16) ** -0.5, 0.75, ((0, 2),))
    proj_bias = scatter_about(key_of[6], (D,), 0.2, 1.0)
    pre_gain = jnp.clip(1.0 + 0.1 * jax.random.normal(key_of[7], (D,), jnp.float32), 0.5, 1.5).astype(jnp.bfloat16)
    pre_shift = scatter_about(key_of[8], (D,), 0.2, 1.0)
    mid_gain = jnp.clip(1.0 + 0.1 * jax.random.normal(key_of[9], (D,), jnp.float32), 0.5, 1.5).astype(jnp.bfloat16)
    mid_shift = scatter_about(key_of[10], (D,), 0.2, 1.0)
    up_weight = scatter_about(key_of[11], (EXPERTS, FF, D), D ** -0.5, 0.1875, ((0, 16), (1, 2)))
    up_bias = scatter_about(key_of[12], (EXPERTS, FF), 0.3, 1.5, ((0, 16), (1, 2)))
    down_weight = scatter_about(key_of[13], (EXPERTS, FF, D), FF ** -0.5, 0.09375, ((0, 16), (1, 2)))
    down_bias = scatter_about(key_of[14], (EXPERTS, D), 0.2, 1.0, ((0, 16),))
    return dict(tokens=tokens, cotangent=cotangent, segment_ids=segment_ids, expert_ids=expert_ids, qkv_weight=qkv_weight, proj_weight=proj_weight, proj_bias=proj_bias, pre_gain=pre_gain, pre_shift=pre_shift, mid_gain=mid_gain, mid_shift=mid_shift, up_weight=up_weight, up_bias=up_bias, down_weight=down_weight, down_bias=down_bias)


epsilon = 1e-05
highest = lax.Precision.HIGHEST

@jax.custom_vjp
def low(v):
    return lax.optimization_barrier(v.astype(jnp.bfloat16)).astype(jnp.float32)

@jax.custom_vjp
def low_back(v):
    return v

def low_keep(v):
    return (low(v), None)

def low_pass(kept, grad):
    return (grad,)

def back_keep(v):
    return (v, None)

def back_low(kept, grad):
    return (low(grad),)
low.defvjp(low_keep, low_pass)
low_back.defvjp(back_keep, back_low)

def layer_norm(values, gain_vec, shift_vec):
    centre = values - lax.optimization_barrier(jnp.mean(values, axis=-1, keepdims=True))
    variance = lax.optimization_barrier(jnp.mean(centre * centre, axis=-1, keepdims=True))
    return centre * lax.rsqrt(variance + epsilon) * gain_vec + shift_vec

def attend(pieces):
    query_rows, key_rows, value_rows, seg_row = pieces
    scaling = HEAD_DIM ** (-0.5)
    raw_scores = jnp.einsum('qhd,khd->hqk', query_rows, key_rows, precision=highest) * scaling
    places = jnp.arange(SEQ, dtype=jnp.int32)
    allowed = (seg_row[:, None] == seg_row[None, :]) & (places[None, :] <= places[:, None])
    scores = low_back(jnp.where(allowed[None], raw_scores, -1e+30))
    row_top = lax.optimization_barrier(jnp.max(scores, axis=-1, keepdims=True))
    weights = jnp.exp(scores - row_top)
    attn_probs = weights / lax.optimization_barrier(jnp.sum(weights, axis=-1, keepdims=True))
    return jnp.einsum('hqk,khd->qhd', low(attn_probs), value_rows, precision=highest)

def expert_ffn(pieces):
    rows_in, up_mat, up_vec, down_mat, down_vec = pieces
    hidden = low_back(jnp.einsum('rd,fd->rf', rows_in, up_mat, precision=highest) + up_vec)
    active = low(jax.nn.gelu(hidden, approximate=True))
    return jnp.dot(active, down_mat, precision=highest) + down_vec

def reference(tokens, cotangent, segment_ids, expert_ids, qkv_weight, proj_weight, proj_bias, pre_gain, pre_shift, mid_gain, mid_shift, up_weight, up_bias, down_weight, down_bias):
    devices = N_DP * N_EXPERT
    experts = EXP_DEV * N_EXPERT
    capacity = 3 * TOK_DEV // (2 * experts)
    ids_flat = expert_ids.reshape(-1).astype(jnp.int32)
    owners = ids_flat.reshape(devices, TOK_DEV)
    onehot = (owners[:, :, None] == jnp.arange(experts, dtype=jnp.int32)[None, None, :]).astype(jnp.int32)
    slot_rank = lax.optimization_barrier(jnp.sum(jnp.cumsum(onehot, axis=1) * onehot, axis=-1)) - 1
    source = jnp.arange(devices * TOK_DEV, dtype=jnp.int32) // TOK_DEV
    target = (ids_flat * (devices * capacity) + source * capacity + slot_rank.reshape(-1)).astype(jnp.int32)
    segments = segment_ids.astype(jnp.int32)

    def forward(inputs, qkv_mat, proj_mat, proj_vec, gain_pre, shift_pre, gain_mid, shift_mid, up_mat, up_vec, down_mat, down_vec):
        normed_pre = low(layer_norm(inputs, gain_pre, shift_pre))
        head_rows = low_back(low(jnp.einsum('td,cde->cte', normed_pre, qkv_mat, precision=highest)))
        shaped = head_rows.reshape(3, -1, SEQ, HEADS, HEAD_DIM)
        attended = lax.map(jax.checkpoint(attend), (shaped[0], shaped[1], shaped[2], segments))
        attended = low_back(low(attended.reshape(-1, D)))
        branch = low_back(jnp.dot(attended, proj_mat, precision=highest) + proj_vec)
        middle = inputs + branch
        normed_mid = low_back(low(layer_norm(middle, gain_mid, shift_mid)))
        buffer = jnp.zeros((experts * devices * capacity, D), jnp.float32).at[target].set(normed_mid)
        buffer = buffer.reshape(experts, devices * capacity, D)
        expert_rows = lax.map(jax.checkpoint(expert_ffn), (buffer, up_mat, up_vec, down_mat, down_vec))
        expert_rows = low_back(low(expert_rows)).reshape(-1, D)
        return middle + expert_rows[target]
    floats = [array.astype(jnp.float32) for array in (tokens, qkv_weight, proj_weight, proj_bias, pre_gain, pre_shift, mid_gain, mid_shift, up_weight, up_bias, down_weight, down_bias)]
    result, pullback = jax.vjp(forward, *floats)
    grads = pullback(cotangent.astype(jnp.float32))
    return (result.astype(jnp.bfloat16), grads[0], grads[1], grads[2], grads[3], grads[4], grads[5], grads[6], grads[7], grads[8], grads[9], grads[10], grads[11])
```

```python
import functools

import jax
import jax.numpy as jnp
from jax import lax
from jax.experimental import pallas as pl
from jax.experimental.pallas import tpu as pltpu
from jax.sharding import PartitionSpec as P

HEAD_DIM = 64
SEQ = 1024
DOC_MAX = 512
EPS = 1e-05
QB = 256
CHUNKS = 3
BF = jnp.bfloat16
F32 = jnp.float32
MESH = pl.DeviceIdType.MESH
VMEM_LIMIT = 60 * 1024 * 1024

BLOCKS = SEQ // QB
START = [max(0, i * QB - DOC_MAX) for i in range(BLOCKS)]
WIDTH = [(i + 1) * QB - START[i] for i in range(BLOCKS)]
OFFSET = [sum(WIDTH[:i]) for i in range(BLOCKS)]
BAND = sum(WIDTH)


def dot(a, b):
    return jnp.dot(a, b, preferred_element_type=F32)


def dot_nt(a, b):
    return lax.dot_general(a, b, (((1,), (1,)), ((), ())), preferred_element_type=F32)


def dot_tn(a, b):
    return lax.dot_general(a, b, (((0,), (0,)), ((), ())), preferred_element_type=F32)


def params(**kw):
    return pltpu.CompilerParams(vmem_limit_bytes=VMEM_LIMIT, **kw)


def cost(flops, nbytes, trans=0):
    return pl.CostEstimate(flops=int(flops), bytes_accessed=int(nbytes), transcendentals=int(trans))


ANY = pl.BlockSpec(memory_space=pl.ANY)


def whole(shape):
    return pl.BlockSpec(shape, lambda *_: (0,) * len(shape))


class SideRoute:
    def __init__(self, n, pairs, sems):
        self.n, self.pairs = n, pairs
        self.send, self.recv, self.local = sems

    def copies(self):
        me = lax.axis_index("expert")
        for j, (src, dst) in enumerate(self.pairs):
            for d in range(1, self.n):
                there = lax.rem(me + d, self.n)
                yield pltpu.make_async_remote_copy(
                    src(there), dst(me), self.send.at[j, d], self.recv.at[j, d],
                    device_id={"expert": there}, device_id_type=MESH,
                )

    def own(self):
        me = lax.axis_index("expert")
        for j, (src, dst) in enumerate(self.pairs):
            yield pltpu.make_async_copy(src(me), dst(me), self.local.at[j])

    def start(self):
        me = lax.axis_index("expert")
        barrier = pltpu.get_barrier_semaphore()
        for d in range(1, self.n):
            pl.semaphore_signal(
                barrier, inc=1, device_id={"expert": lax.rem(me + d, self.n)}, device_id_type=MESH
            )
        pl.semaphore_wait(barrier, self.n - 1)
        for c in self.copies():
            c.start()
        for c in self.own():
            c.start()

    def wait(self):
        for c in self.own():
            c.wait()
        for c in self.copies():
            c.wait()


def route_sems(n, count):
    return [
        pltpu.SemaphoreType.DMA((count, n)),
        pltpu.SemaphoreType.DMA((count, n)),
        pltpu.SemaphoreType.DMA((count,)),
    ]


def slots_kernel(cc, rows, ids_ref, val_ref, tcol_ref, trow_ref, out_ref, row_s):
    step = pl.program_id(0)
    tokens = ids_ref.shape[0]

    @pl.when(step == 0)
    def _():
        ids = ids_ref[...]
        hot = (ids == lax.broadcasted_iota(jnp.int32, (tokens, 128), 1)).astype(F32)
        lower = (
            lax.broadcasted_iota(jnp.int32, (tokens, tokens), 0)
            >= lax.broadcasted_iota(jnp.int32, (tokens, tokens), 1)
        ).astype(F32).astype(BF)
        counts = dot(lower, hot.astype(BF))
        rank = jnp.sum(counts * hot, axis=1, keepdims=True) - 1.0
        chunk = jnp.floor((rank + 0.5) * (1.0 / cc))
        place = chunk * rows + ids.astype(F32) * cc + (rank - chunk * cc)
        place = jnp.broadcast_to(place, (tokens, 128))
        tcol_ref[...] = place.astype(jnp.int32)
        flat = jnp.transpose(place)[0:8, :].astype(jnp.int32)
        trow_ref[...] = flat
        row_s[...] = flat

    block = out_ref.shape[0]
    hot = (
        lax.broadcasted_iota(jnp.int32, (block, tokens), 0) + step * block == row_s[0:1, :]
    ).astype(F32).astype(BF)
    out_ref[...] = dot(hot, val_ref[...]).astype(BF)


def slots_call(ids, values, cc, rows):
    tokens, width = values.shape
    total = CHUNKS * rows
    block = 256
    return pl.pallas_call(
        functools.partial(slots_kernel, cc, rows),
        grid=(total // block,),
        in_specs=[whole((tokens, 1)), whole((tokens, width))],
        out_specs=[
            whole((tokens, 128)),
            whole((8, tokens)),
            pl.BlockSpec((block, width), lambda i: (i, 0)),
        ],
        out_shape=[
            jax.ShapeDtypeStruct((tokens, 128), jnp.int32),
            jax.ShapeDtypeStruct((8, tokens), jnp.int32),
            jax.ShapeDtypeStruct((total, width), BF),
        ],
        scratch_shapes=[pltpu.VMEM((8, tokens), jnp.int32)],
        compiler_params=params(),
        cost_estimate=cost(2 * total * tokens * width, 8e6),
        name="slots",
    )(ids, values)


def unit_of(values):
    centre = values - jnp.mean(values, axis=-1, keepdims=True)
    inverse = lax.rsqrt(jnp.mean(centre * centre, axis=-1, keepdims=True) + EPS)
    return centre * inverse, inverse


def heads_kernel(x_ref, own_ref, oth_ref, gain_ref, shift_ref, norm_ref, out_ref, norm_s):
    step = pl.program_id(0)
    tokens = x_ref.shape[0]

    @pl.when(step == 0)
    def _():
        gain, shift = gain_ref[...].astype(F32), shift_ref[...].astype(F32)

        def body(b, _):
            at = pl.ds(b * 128, 128)
            unit, _ = unit_of(x_ref[at, :].astype(F32))
            low = (unit * gain + shift).astype(BF)
            norm_s[at, :] = low
            norm_ref[at, :] = low
            return 0

        lax.fori_loop(0, tokens // 128, body, 0)

    @pl.when(step < 3)
    def _():
        out_ref[0] = dot(norm_s[...], own_ref[0]).astype(BF)

    @pl.when(step >= 3)
    def _():
        out_ref[0] = dot(norm_s[...], oth_ref[0]).astype(BF)


def heads_call(x, own, oth, gain, shift):
    tokens, width = x.shape
    half = own.shape[2]
    return pl.pallas_call(
        heads_kernel,
        grid=(6,),
        in_specs=[
            whole((tokens, width)),
            pl.BlockSpec((1, width, half), lambda i: (jnp.minimum(i, 2), 0, 0)),
            pl.BlockSpec((1, width, half), lambda i: (jnp.maximum(i - 3, 0), 0, 0)),
            whole((1, width)),
            whole((1, width)),
        ],
        out_specs=[whole((tokens, width)), pl.BlockSpec((1, tokens, half), lambda i: (i, 0, 0))],
        out_shape=[
            jax.ShapeDtypeStruct((tokens, width), BF),
            jax.ShapeDtypeStruct((6, tokens, half), BF),
        ],
        scratch_shapes=[pltpu.VMEM((tokens, width), BF)],
        compiler_params=params(),
        cost_estimate=cost(2 * tokens * width * 6 * half, 18e6),
        name="head_rows",
    )(x, own, oth, gain, shift)


def lane_pick(width, first):
    lanes = lax.broadcasted_iota(jnp.int32, (1, width), 1)
    return (lanes < HEAD_DIM) if first else (lanes >= HEAD_DIM)


def attend_kernel(
    n, pairs, x_ref, seg_ref, q_ref, k_ref, v_ref, own_ref, oth_ref, pbias_ref, gain_ref, shift_ref,
    trow_ref, cot_ref, att_ref, prob_ref, mid_ref, slot_ref, arr_ref, bias_s, low_s, send, recv, local,
):
    step = pl.program_id(0)
    tokens = x_ref.shape[0]
    route = SideRoute(
        n, [(lambda e: cot_ref.at[:, e], lambda e: arr_ref.at[:, e])], (send, recv, local)
    )

    @pl.when(step == 0)
    def _():
        route.start()
        seg = seg_ref[...].astype(F32)
        seg_col = jnp.transpose(jnp.broadcast_to(seg, (128, tokens)))
        for i in range(BLOCKS):
            w, s = WIDTH[i], START[i]
            rows = lax.broadcasted_iota(jnp.int32, (QB, w), 0) + i * QB
            keys = lax.broadcasted_iota(jnp.int32, (QB, w), 1) + s
            same = seg_col[i * QB:(i + 1) * QB, 0:1] == seg[:, s:s + w]
            bias_s[:, OFFSET[i]:OFFSET[i] + w] = jnp.where(same & (keys <= rows), 0.0, -1e30)

    @pl.when(step < pairs)
    def _():
        query = q_ref[0] * BF(HEAD_DIM ** -0.5)
        for i in range(BLOCKS):
            w, s = WIDTH[i], START[i]
            keys, values = k_ref[0, s:s + w, :], v_ref[0, s:s + w, :]
            bias = bias_s[:, OFFSET[i]:OFFSET[i] + w]
            parts = []
            for j in range(2):
                q = jnp.where(lane_pick(128, j == 0), query[i * QB:(i + 1) * QB], BF(0))
                scores = dot_nt(q, keys) + bias
                top = jnp.max(scores, axis=-1, keepdims=True)
                weights = jnp.exp(scores - top)
                probs = (weights * (1.0 / jnp.sum(weights, axis=-1, keepdims=True))).astype(BF)
                prob_ref[j, :, OFFSET[i]:OFFSET[i] + w] = probs
                parts.append(dot(probs, values))
            both = jnp.where(lane_pick(128, True), parts[0], parts[1])
            att_ref[i * QB:(i + 1) * QB, pl.ds(pl.multiple_of(step * 128, 128), 128)] = both.astype(BF)

    @pl.when(step == pairs)
    def _():
        pbias = pbias_ref[...].astype(F32)
        gain, shift = gain_ref[...].astype(F32), shift_ref[...].astype(F32)
        half = own_ref.shape[0]

        def body(b, _):
            at = pl.ds(b * 128, 128)
            branch = dot(att_ref[at, 0:half], own_ref[...]) + dot(att_ref[at, half:2 * half], oth_ref[...])
            middle = x_ref[at, :].astype(F32) + branch + pbias
            mid_ref[at, :] = middle
            unit, _ = unit_of(middle)
            low_s[at, :] = (unit * gain + shift).astype(BF)
            return 0

        lax.fori_loop(0, tokens // 128, body, 0)

        def place(b, _):
            hot = (
                lax.broadcasted_iota(jnp.int32, (256, tokens), 0) + b * 256 == trow_ref[0:1, :]
            ).astype(F32).astype(BF)
            slot_ref[pl.ds(b * 256, 256), :] = dot(hot, low_s[...]).astype(BF)
            return 0

        lax.fori_loop(0, slot_ref.shape[0] // 256, place, 0)
        route.wait()


def attend_call(n, x, seg, head_rows, proj_own, proj_oth, pbias, gain, shift, trow, cot_slots):
    tokens, width = x.shape
    half = proj_own.shape[0]
    pairs = width // 128
    per = half // 128
    slots = cot_slots.shape[1] * cot_slots.shape[2] * CHUNKS

    def head(c):
        def index(h):
            h = jnp.minimum(h, pairs - 1)
            return (3 * (h // per) + c, 0, h % per)

        return pl.BlockSpec((1, tokens, 128), index)

    return pl.pallas_call(
        functools.partial(attend_kernel, n, pairs),
        grid=(pairs + 1,),
        in_specs=[
            whole((tokens, width)), whole((1, tokens)), head(0), head(1), head(2),
            whole((half, width)), whole((half, width)), whole((1, width)), whole((1, width)),
            whole((1, width)), whole((8, tokens)), ANY,
        ],
        out_specs=[
            whole((tokens, width)),
            pl.BlockSpec((2, QB, BAND), lambda h: (jnp.minimum(h, pairs - 1), 0, 0)),
            whole((tokens, width)),
            whole((slots, width)),
            ANY,
        ],
        out_shape=[
            jax.ShapeDtypeStruct((tokens, width), BF),
            jax.ShapeDtypeStruct((2 * pairs, QB, BAND), BF),
            jax.ShapeDtypeStruct((tokens, width), F32),
            jax.ShapeDtypeStruct((slots, width), BF),
            jax.ShapeDtypeStruct(cot_slots.shape, BF),
        ],
        scratch_shapes=[
            pltpu.VMEM((QB, BAND), F32), pltpu.VMEM((tokens, width), BF), *route_sems(n, 1),
        ],
        compiler_params=params(collective_id=1, has_side_effects=True),
        cost_estimate=cost(2e10, 5e7),
        name="attend",
    )(x, seg, head_rows, head_rows, head_rows, proj_own, proj_oth, pbias, gain, shift, trow, cot_slots)


def route_kernel(n, chunk, src_ref, dst_ref, send, recv, local):
    route = SideRoute(
        n, [(lambda e: src_ref.at[chunk, e], lambda e: dst_ref.at[e])], (send, recv, local)
    )
    route.start()
    route.wait()


def route_call(n, src, chunk, cid):
    return pl.pallas_call(
        functools.partial(route_kernel, n, chunk),
        in_specs=[ANY],
        out_specs=ANY,
        out_shape=jax.ShapeDtypeStruct(src.shape[1:], BF),
        scratch_shapes=route_sems(n, 1),
        compiler_params=params(collective_id=cid, has_side_effects=True),
        name="route",
    )(src)


GELU_C = 0.7978845608028654
GELU_A = 0.044715


def expert_kernel(
    n, has_mid, has_back, tiles, x_ref, c_ref, uo_ref, ut_ref, do_ref, dt_ref, bo_ref, bt_ref, db_ref, *rest
):
    rest = list(rest)
    pairs = []
    mid_src = rest.pop(0) if has_mid is not None else None
    back_src = rest.pop(0) if has_back else None
    act_ref, gh_ref, ub_ref, y_ref, dx_ref = rest[:5]
    rest = rest[5:]
    mid_dst = rest.pop(0) if has_mid is not None else None
    back_dst = rest.pop(0) if has_back else None
    y_s, dx_s = rest[:2]
    sems = rest[2:]
    if has_mid is not None:
        pairs.append((lambda e: mid_src.at[has_mid, e], lambda e: mid_dst.at[e]))
    if has_back:
        pairs.append((lambda e: back_src.at[e], lambda e: back_dst.at[e]))
    route = SideRoute(n, pairs, sems)
    step = pl.program_id(0)

    @pl.when(step == 0)
    def _():
        route.start()
        y_s[...] = jnp.broadcast_to(db_ref[...].astype(F32), y_s.shape)
        dx_s[...] = jnp.zeros_like(dx_s)

    def work(up_ref, down_ref, b_ref):
        rows, cot = x_ref[...], c_ref[0]
        up, down = up_ref[...], down_ref[...]
        h = dot_nt(rows, up) + b_ref[...].astype(F32)
        g = dot_nt(cot, down)
        sq = h * h
        t = jnp.tanh(GELU_C * (h + GELU_A * (sq * h)))
        act = ((0.5 * h) * (1.0 + t)).astype(BF)
        act_ref[...] = act
        slope = 0.5 * (1.0 + t) + (0.5 * h) * ((1.0 - t * t) * (GELU_C * (1.0 + (3.0 * GELU_A) * sq)))
        gh = (g * slope).astype(BF)
        gh_ref[...] = gh
        ub_ref[...] = jnp.broadcast_to(jnp.sum(gh.astype(F32), axis=0, keepdims=True), ub_ref.shape)
        y_s[...] += dot(act, down)
        dx_s[...] += dot(gh, up)

    @pl.when(step < tiles // 2)
    def _():
        work(uo_ref, do_ref, bo_ref)

    @pl.when(step >= tiles // 2)
    def _():
        work(ut_ref, dt_ref, bt_ref)

    @pl.when(step == tiles - 1)
    def _():
        y_ref[...] = y_s[...].astype(BF)
        dx_ref[...] = dx_s[...].astype(BF)
        route.wait()


def expert_call(n, chunk, rows, cot, up, down, bias, down_bias, mid=None, mid_chunk=None, back=None, cid=0):
    up_own, up_oth = up
    down_own, down_oth = down
    b_own, b_oth = bias
    r, width = rows.shape
    hid = up_own.shape[0]
    ft = 512
    own_tiles = hid // ft
    tiles = 2 * own_tiles

    def first(i):
        return jnp.minimum(i, own_tiles - 1)

    def second(i):
        return jnp.maximum(i - own_tiles, 0)

    in_specs = [
        whole((r, width)),
        pl.BlockSpec((1, r, width), lambda i: (chunk, 0, 0)),
        pl.BlockSpec((ft, width), lambda i: (first(i), 0)),
        pl.BlockSpec((ft, width), lambda i: (second(i), 0)),
        pl.BlockSpec((ft, width), lambda i: (first(i), 0)),
        pl.BlockSpec((ft, width), lambda i: (second(i), 0)),
        pl.BlockSpec((1, ft), lambda i: (0, first(i))),
        pl.BlockSpec((1, ft), lambda i: (0, second(i))),
        whole((1, width)),
    ]
    args = [rows, cot, up_own, up_oth, down_own, down_oth, b_own, b_oth, down_bias]
    out_specs = [
        pl.BlockSpec((r, ft), lambda i: (0, i)),
        pl.BlockSpec((r, ft), lambda i: (0, i)),
        pl.BlockSpec((8, ft), lambda i: (0, i)),
        whole((r, width)),
        whole((r, width)),
    ]
    out_shape = [
        jax.ShapeDtypeStruct((r, 2 * hid), BF),
        jax.ShapeDtypeStruct((r, 2 * hid), BF),
        jax.ShapeDtypeStruct((8, 2 * hid), F32),
        jax.ShapeDtypeStruct((r, width), BF),
        jax.ShapeDtypeStruct((r, width), BF),
    ]
    count = 0
    if mid is not None:
        in_specs.append(ANY)
        args.append(mid)
        out_specs.append(ANY)
        out_shape.append(jax.ShapeDtypeStruct(mid.shape[1:], BF))
        count += 1
    if back is not None:
        in_specs.append(ANY)
        args.append(back)
        out_specs.append(ANY)
        out_shape.append(jax.ShapeDtypeStruct(back.shape, BF))
        count += 1
    return pl.pallas_call(
        functools.partial(expert_kernel, n, mid_chunk if mid is not None else None, back is not None, tiles),
        grid=(tiles,),
        in_specs=in_specs,
        out_specs=out_specs,
        out_shape=out_shape,
        scratch_shapes=[pltpu.VMEM((r, width), F32), pltpu.VMEM((r, width), F32), *route_sems(n, count)],
        compiler_params=params(collective_id=cid, has_side_effects=True),
        cost_estimate=cost(8 * r * width * 2 * hid, 3e7),
        name="experts",
    )(*args)


def wgrad_oth_kernel(n, tiles, a0, a1, a2, g0, g1, g2, c_ref, x0, x1, x2, back_src, do_ref, up_ref, cb_ref, back_dst, *sems):
    route = SideRoute(n, [(lambda e: back_src.at[e], lambda e: back_dst.at[e])], sems)
    step = pl.program_id(0)

    @pl.when(step == 0)
    def _():
        route.start()
        total = jnp.zeros((1, c_ref.shape[2]), F32)
        for c in range(CHUNKS):
            total = total + jnp.sum(c_ref[c].astype(F32), axis=0, keepdims=True)
        cb_ref[...] = jnp.broadcast_to(total, cb_ref.shape)

    @pl.when(step < tiles)
    def _():
        s = dot_tn(a0[...], c_ref[0]) + dot_tn(a1[...], c_ref[1]) + dot_tn(a2[...], c_ref[2])
        do_ref[...] = s.astype(BF)

    @pl.when(step >= tiles)
    def _():
        s = dot_tn(g0[...], x0[...]) + dot_tn(g1[...], x1[...]) + dot_tn(g2[...], x2[...])
        up_ref[...] = s.astype(BF)

    @pl.when(step == 2 * tiles - 1)
    def _():
        route.wait()


def wgrad_oth_call(n, acts, ghs, cot, rows, back, cid):
    r, width = rows[0].shape
    hid = acts[0].shape[1] // 2
    ft = 512
    tiles = hid // ft

    def first(i):
        return jnp.minimum(i, tiles - 1)

    def second(i):
        return jnp.maximum(i - tiles, 0)

    a_spec = pl.BlockSpec((r, ft), lambda i: (0, tiles + first(i)))
    g_spec = pl.BlockSpec((r, ft), lambda i: (0, tiles + second(i)))
    return pl.pallas_call(
        functools.partial(wgrad_oth_kernel, n, tiles),
        grid=(2 * tiles,),
        in_specs=[a_spec] * 3 + [g_spec] * 3 + [whole(cot.shape)] + [whole((r, width))] * 3 + [ANY],
        out_specs=[
            pl.BlockSpec((ft, width), lambda i: (first(i), 0)),
            pl.BlockSpec((ft, width), lambda i: (second(i), 0)),
            whole((8, width)),
            ANY,
        ],
        out_shape=[
            jax.ShapeDtypeStruct((hid, width), BF),
            jax.ShapeDtypeStruct((hid, width), BF),
            jax.ShapeDtypeStruct((8, width), F32),
            jax.ShapeDtypeStruct(back.shape, BF),
        ],
        scratch_shapes=route_sems(n, 1),
        compiler_params=params(collective_id=cid, has_side_effects=True),
        cost_estimate=cost(4 * 3 * r * hid * width, 4e7),
        name="weight_grads_other",
    )(*acts, *ghs, cot, *rows, back)


def wgrad_own_kernel(tiles, a0, a1, a2, g0, g1, g2, c_ref, x0, x1, x2, rd_ref, ru_ref, do_ref, up_ref):
    step = pl.program_id(0)

    @pl.when(step < tiles)
    def _():
        s = dot_tn(a0[...], c_ref[0]) + dot_tn(a1[...], c_ref[1]) + dot_tn(a2[...], c_ref[2])
        do_ref[...] = s + rd_ref[...].astype(F32)

    @pl.when(step >= tiles)
    def _():
        s = dot_tn(g0[...], x0[...]) + dot_tn(g1[...], x1[...]) + dot_tn(g2[...], x2[...])
        up_ref[...] = s + ru_ref[...].astype(F32)


def wgrad_own_call(acts, ghs, cot, rows, got_down, got_up):
    r, width = rows[0].shape
    hid = acts[0].shape[1] // 2
    ft = 512
    tiles = hid // ft

    def first(i):
        return jnp.minimum(i, tiles - 1)

    def second(i):
        return jnp.maximum(i - tiles, 0)

    a_spec = pl.BlockSpec((r, ft), lambda i: (0, first(i)))
    g_spec = pl.BlockSpec((r, ft), lambda i: (0, second(i)))
    d_spec = pl.BlockSpec((ft, width), lambda i: (first(i), 0))
    u_spec = pl.BlockSpec((ft, width), lambda i: (second(i), 0))
    return pl.pallas_call(
        functools.partial(wgrad_own_kernel, tiles),
        grid=(2 * tiles,),
        in_specs=[a_spec] * 3 + [g_spec] * 3 + [whole(cot.shape)] + [whole((r, width))] * 3 + [d_spec, u_spec],
        out_specs=[d_spec, u_spec],
        out_shape=[jax.ShapeDtypeStruct((hid, width), F32), jax.ShapeDtypeStruct((hid, width), F32)],
        compiler_params=params(),
        cost_estimate=cost(4 * 3 * r * hid * width, 6e7),
        name="weight_grads_own",
    )(*acts, *ghs, cot, *rows, got_down, got_up)


def gather_rows(tcol, parts):
    rows = parts[0].shape[0]
    total = None
    for c, part in enumerate(parts):
        hot = (
            lax.broadcasted_iota(jnp.int32, (tcol.shape[0], rows), 1) + c * rows == tcol[:, 0:1]
        ).astype(F32).astype(BF)
        term = dot(hot, part[...])
        total = term if total is None else total + term
    return total


def middle_back_kernel(
    n, blocks, tcol_ref, g0, g1, g2, mid_ref, cot_ref, gain_ref, own_ref, oth_ref, att_ref, y_src,
    gmid_ref, gatt_ref, pg_own, pg_oth, small_ref, y_dst, gb_s, send, recv, local,
):
    route = SideRoute(n, [(lambda e: y_src.at[e], lambda e: y_dst.at[e])], (send, recv, local))
    step = pl.program_id(0)
    half = own_ref.shape[0]
    tb, width = mid_ref.shape

    @pl.when(step == 0)
    def _():
        route.start()
        small_ref[...] = jnp.zeros_like(small_ref)

    grad = gather_rows(tcol_ref[...], (g0, g1, g2))
    grad = grad.astype(BF).astype(F32)
    unit, inverse = unit_of(mid_ref[...])
    scaled = grad * gain_ref[...].astype(F32)
    inner = jnp.mean(scaled, axis=-1, keepdims=True)
    along = jnp.mean(scaled * unit, axis=-1, keepdims=True)
    gmid = cot_ref[...].astype(F32) + inverse * (scaled - inner - unit * along)
    gmid_ref[...] = gmid
    gb = gmid.astype(BF)
    gb_s[pl.ds(pl.multiple_of(step * tb, tb), tb), :] = gb
    small_ref[0:1, :] += jnp.sum(grad * unit, axis=0, keepdims=True)
    small_ref[1:2, :] += jnp.sum(grad, axis=0, keepdims=True)
    small_ref[2:3, :] += jnp.sum(gb.astype(F32), axis=0, keepdims=True)
    gatt_ref[:, 0:half] = dot_nt(gb, own_ref[...]).astype(BF)
    gatt_ref[:, half:2 * half] = dot_nt(gb, oth_ref[...]).astype(BF)

    @pl.when(step == blocks - 1)
    def _():
        pg_own[...] = dot_tn(att_ref[:, 0:half], gb_s[...])
        pg_oth[...] = dot_tn(att_ref[:, half:2 * half], gb_s[...]).astype(BF)
        route.wait()


def middle_back_call(n, tcol, grads, middle, cot, gain, proj_own, proj_oth, att, y, cid):
    tokens, width = middle.shape
    half = proj_own.shape[0]
    tb = 256
    rows = grads[0].shape[0]
    block = pl.BlockSpec((tb, width), lambda i: (i, 0))
    return pl.pallas_call(
        functools.partial(middle_back_kernel, n, tokens // tb),
        grid=(tokens // tb,),
        in_specs=[
            pl.BlockSpec((tb, 128), lambda i: (i, 0)), *[whole((rows, width))] * 3, block, block,
            whole((1, width)), whole((half, width)), whole((half, width)), whole((tokens, width)), ANY,
        ],
        out_specs=[block, block, whole((half, width)), whole((half, width)), whole((8, width)), ANY],
        out_shape=[
            jax.ShapeDtypeStruct((tokens, width), F32),
            jax.ShapeDtypeStruct((tokens, width), BF),
            jax.ShapeDtypeStruct((half, width), F32),
            jax.ShapeDtypeStruct((half, width), BF),
            jax.ShapeDtypeStruct((8, width), F32),
            jax.ShapeDtypeStruct(y.shape, BF),
        ],
        scratch_shapes=[pltpu.VMEM((tokens, width), BF), *route_sems(n, 1)],
        compiler_params=params(collective_id=cid, has_side_effects=True),
        cost_estimate=cost(1.2e10, 3e7),
        name="middle_back",
    )(tcol, *grads, middle, cot, gain, proj_own, proj_oth, att, y)


def attend_back_kernel(
    n, pairs, q_ref, k_ref, v_ref, prob_ref, do_ref, o_ref, y_src, dq_ref, dk_ref, dv_ref, y_dst,
    dk_s, dv_s, send, recv, local,
):
    route = SideRoute(n, [(lambda e: y_src.at[e], lambda e: y_dst.at[e])], (send, recv, local))
    step = pl.program_id(0)
    scale = HEAD_DIM ** -0.5

    @pl.when(step == 0)
    def _():
        route.start()

    dk_s[...] = jnp.zeros_like(dk_s)
    dv_s[...] = jnp.zeros_like(dv_s)
    for i in range(BLOCKS):
        w, s = WIDTH[i], START[i]
        at = slice(i * QB, (i + 1) * QB)
        keys, values = k_ref[0, s:s + w, :], v_ref[0, s:s + w, :]
        go = do_ref[at, :]
        prod = go.astype(F32) * o_ref[at, :].astype(F32)
        query = q_ref[0, at, :]
        parts = []
        for j in range(2):
            pick = lane_pick(128, j == 0)
            go_j = jnp.where(pick, go, BF(0))
            q_j = jnp.where(pick, query, BF(0))
            inner = jnp.sum(jnp.where(pick, prod, 0.0), axis=-1, keepdims=True)
            probs = prob_ref[j, :, OFFSET[i]:OFFSET[i] + w]
            gp = dot_nt(go_j, values)
            gs = (probs.astype(F32) * (gp - inner)).astype(BF)
            parts.append(dot(gs, keys))
            dk_s[s:s + w, :] += dot_tn(gs, q_j)
            dv_s[s:s + w, :] += dot_tn(probs, go_j)
        dq_ref[0, at, :] = (jnp.where(lane_pick(128, True), parts[0], parts[1]) * scale).astype(BF)
    dk_ref[0] = (dk_s[...] * scale).astype(BF)
    dv_ref[0] = dv_s[...].astype(BF)

    @pl.when(step == pairs - 1)
    def _():
        route.wait()


def attend_back_call(n, head_rows, probs, gatt, att, y, cid):
    tokens, width = gatt.shape
    half = head_rows.shape[2]
    pairs, per = width // 128, half // 128

    def head(c):
        return pl.BlockSpec((1, tokens, 128), lambda h: (3 * (h // per) + c, 0, h % per))

    cols = pl.BlockSpec((tokens, 128), lambda h: (0, h))
    out = pl.BlockSpec((1, tokens, 128), lambda h: (h // per, 0, h % per))
    shape = jax.ShapeDtypeStruct((2, tokens, half), BF)
    return pl.pallas_call(
        functools.partial(attend_back_kernel, n, pairs),
        grid=(pairs,),
        in_specs=[
            head(0), head(1), head(2), pl.BlockSpec((2, QB, BAND), lambda h: (h, 0, 0)), cols, cols, ANY,
        ],
        out_specs=[out, out, out, ANY],
        out_shape=[shape, shape, shape, jax.ShapeDtypeStruct(y.shape, BF)],
        scratch_shapes=[pltpu.VMEM((tokens, 128), F32), pltpu.VMEM((tokens, 128), F32), *route_sems(n, 1)],
        compiler_params=params(collective_id=cid, has_side_effects=True),
        cost_estimate=cost(4e10, 4e7),
        name="attend_back",
    )(head_rows, head_rows, head_rows, probs, gatt, att, y)


def heads_back_kernel(
    n, x_ref, norm_ref, gq, gk, gv, own_ref, oth_ref, gmid_ref, gain_ref, y_src,
    qg_own, qg_oth, xg_ref, small_ref, y_dst, acc_s, send, recv, local,
):
    route = SideRoute(n, [(lambda e: y_src.at[e], lambda e: y_dst.at[e])], (send, recv, local))
    step = pl.program_id(0)
    tokens, width = x_ref.shape

    @pl.when(step == 0)
    def _():
        route.start()
        acc_s[...] = jnp.zeros_like(acc_s)

    for c, g_ref in enumerate((gq, gk, gv)):
        @pl.when(step == c)
        def _():
            qg_own[0] = dot_tn(norm_ref[...], g_ref[0])
            acc_s[...] += dot_nt(g_ref[0], own_ref[0])

        @pl.when(step == 3 + c)
        def _():
            qg_oth[0] = dot_tn(norm_ref[...], g_ref[0]).astype(BF)
            acc_s[...] += dot_nt(g_ref[0], oth_ref[0])

    @pl.when(step == 5)
    def _():
        small_ref[...] = jnp.zeros_like(small_ref)
        gain = gain_ref[...].astype(F32)

        def body(b, _):
            at = pl.ds(b * 128, 128)
            grad = acc_s[at, :]
            unit, inverse = unit_of(x_ref[at, :].astype(F32))
            scaled = grad * gain
            inner = jnp.mean(scaled, axis=-1, keepdims=True)
            along = jnp.mean(scaled * unit, axis=-1, keepdims=True)
            xg_ref[at, :] = gmid_ref[at, :] + inverse * (scaled - inner - unit * along)
            small_ref[0:1, :] += jnp.sum(grad * unit, axis=0, keepdims=True)
            small_ref[1:2, :] += jnp.sum(grad, axis=0, keepdims=True)
            return 0

        lax.fori_loop(0, tokens // 128, body, 0)
        route.wait()


def heads_back_call(n, x, norm, grads, own, oth, gmid, gain, y, cid):
    tokens, width = x.shape
    half = own.shape[2]
    g_spec = pl.BlockSpec((1, tokens, half), lambda i: (i // 3, 0, 0))
    first = pl.BlockSpec((1, width, half), lambda i: (jnp.minimum(i, 2), 0, 0))
    second = pl.BlockSpec((1, width, half), lambda i: (jnp.maximum(i - 3, 0), 0, 0))
    return pl.pallas_call(
        functools.partial(heads_back_kernel, n),
        grid=(6,),
        in_specs=[
            whole((tokens, width)), whole((tokens, width)), g_spec, g_spec, g_spec, first, second,
            whole((tokens, width)), whole((1, width)), ANY,
        ],
        out_specs=[first, second, whole((tokens, width)), whole((8, width)), ANY],
        out_shape=[
            jax.ShapeDtypeStruct((3, width, half), F32),
            jax.ShapeDtypeStruct((3, width, half), BF),
            jax.ShapeDtypeStruct((tokens, width), F32),
            jax.ShapeDtypeStruct((8, width), F32),
            jax.ShapeDtypeStruct(y.shape, BF),
        ],
        scratch_shapes=[pltpu.VMEM((tokens, width), F32), *route_sems(n, 1)],
        compiler_params=params(collective_id=cid, has_side_effects=True),
        cost_estimate=cost(1.3e10, 5e7),
        name="heads_back",
    )(x, norm, *grads, own, oth, gmid, gain, y)


def total_kernel(
    n, q_own, p_own, small_ref, q_oth, p_oth, q_out, p_out, small_out,
    acc, snd, rcv, res, q_got, p_got, small_got, dp_send, dp_recv, rs_send, rs_recv, ag_send, ag_recv, sm_send, sm_recv,
):
    me, core = lax.axis_index("expert"), lax.axis_index("dp")
    width, half = q_own.shape[1], q_own.shape[2]
    rows = acc.shape[0]
    bits = [1 << i for i in range(n.bit_length() - 1)]
    peers = [{"dp": 1 - core}] + [
        {"expert": me + b - 2 * b * lax.rem(lax.div(me, b), 2)} for b in bits
    ]
    barrier = pltpu.get_barrier_semaphore()
    for peer in peers:
        pl.semaphore_signal(barrier, inc=1, device_id=peer, device_id_type=MESH)
    pl.semaphore_wait(barrier, len(peers))

    def send(src, dst, s, r, peer):
        c = pltpu.make_async_remote_copy(src, dst, s, r, device_id=peer, device_id_type=MESH)
        c.start()
        return c

    first = [
        send(p_oth, p_got, dp_send.at[0], dp_recv.at[0], peers[0]),
        *[send(q_oth.at[c], q_got.at[c], dp_send.at[1 + c], dp_recv.at[1 + c], peers[0]) for c in range(3)],
    ]
    small_out[...] = small_ref[...]
    small_copy = send(small_out, small_got.at[0], sm_send.at[0], sm_recv.at[0], peers[0])

    first[0].wait()
    for b in range(width // half):
        acc[3 * width + b * half:3 * width + (b + 1) * half, :] = (
            p_own[:, b * half:(b + 1) * half] + p_got[:, b * half:(b + 1) * half].astype(F32)
        )
    for c in range(3):
        first[1 + c].wait()

        def add(b, _):
            acc[pl.ds(c * width + b * 128, 128), :] = (
                q_own[c, pl.ds(b * 128, 128), :] + q_got[c, pl.ds(b * 128, 128), :].astype(F32)
            )
            return 0

        lax.fori_loop(0, width // 128, add, 0)
    small_copy.wait()
    small_out[...] += small_got[0]

    units = rows // (16 * n)
    shares = [units // 3, units // 3, units - 2 * (units // 3)]
    order = [[(p + s) % 3 if s < 3 else s for s in range(len(bits))] if len(bits) > 3 else
             [(p + s) % len(bits) for s in range(len(bits))] for p in range(3)]
    base = [0, shares[0] * 16 * n, (shares[0] + shares[1]) * 16 * n]
    length = [share * 16 * n for share in shares]
    start = [jnp.int32(b) for b in base]
    used = list(base)

    def aligned(v):
        return pl.multiple_of(v, 16)

    for s in range(len(bits)):
        copies = []
        for p in range(3):
            if shares[p] == 0:
                continue
            k = order[p][s]
            up = lax.rem(lax.div(me, bits[k]), 2)
            hl = length[p] // 2
            step = shares[p] * 16
            away = start[p] + (1 - up) * hl
            keep = start[p] + up * hl
            slot = used[p]

            def pack(b, _):
                snd[pl.ds(aligned(slot + b * step), step), :] = acc[pl.ds(aligned(away + b * step), step), :].astype(BF)
                return 0

            lax.fori_loop(0, hl // step, pack, 0)
            copies.append((p, keep, hl, step, slot, send(
                snd.at[pl.ds(slot, hl)], rcv.at[pl.ds(slot, hl)], rs_send.at[s, p], rs_recv.at[s, p], peers[1 + k])))
        small_copy = send(small_out, small_got.at[1 + s], sm_send.at[1 + s], sm_recv.at[1 + s], peers[1 + s])
        for p, keep, hl, step, slot, copy in copies:
            copy.wait()

            def add(b, _):
                at = pl.ds(aligned(keep + b * step), step)
                acc[at, :] = acc[at, :] + rcv[pl.ds(aligned(slot + b * step), step), :].astype(F32)
                return 0

            lax.fori_loop(0, hl // step, add, 0)
            start[p], length[p], used[p] = keep, hl, slot + hl
        small_copy.wait()
        small_out[...] += small_got[1 + s]

    for p in range(3):
        if shares[p]:
            at = pl.ds(aligned(start[p]), length[p])
            res[at, :] = acc[at, :].astype(BF)
    for s in reversed(range(len(bits))):
        copies = []
        for p in range(3):
            if shares[p] == 0:
                continue
            k = order[p][s]
            at = pl.ds(aligned(start[p]), length[p])
            copies.append(send(res.at[at], res.at[at], ag_send.at[s, p], ag_recv.at[s, p], peers[1 + k]))
            start[p] = start[p] - lax.rem(lax.div(me, bits[k]), 2) * length[p]
            length[p] = 2 * length[p]
        for copy in copies:
            copy.wait()

    for c in range(3):
        def give(b, _):
            q_out[c, pl.ds(b * 128, 128), :] = res[pl.ds(c * width + b * 128, 128), :].astype(F32)
            return 0

        lax.fori_loop(0, width // 128, give, 0)
    for b in range(width // half):
        p_out[:, b * half:(b + 1) * half] = res[3 * width + b * half:3 * width + (b + 1) * half, :].astype(F32)


def total_call(n, q_own, p_own, small, q_oth, p_oth, cid):
    _, width, half = q_own.shape
    rows = 3 * width + (width // half) * half
    stages = n.bit_length() - 1
    vm = pl.BlockSpec(memory_space=pltpu.VMEM)
    dma = pltpu.SemaphoreType.DMA
    return pl.pallas_call(
        functools.partial(total_kernel, n),
        in_specs=[vm, vm, vm, ANY, ANY],
        out_specs=[vm, vm, vm],
        out_shape=[
            jax.ShapeDtypeStruct(q_own.shape, F32),
            jax.ShapeDtypeStruct(p_own.shape, F32),
            jax.ShapeDtypeStruct(small.shape, F32),
        ],
        scratch_shapes=[
            pltpu.VMEM((rows, half), F32), pltpu.VMEM((rows, half), BF), pltpu.VMEM((rows, half), BF),
            pltpu.VMEM((rows, half), BF), pltpu.VMEM(q_oth.shape, BF), pltpu.VMEM(p_oth.shape, BF),
            pltpu.VMEM((1 + stages, *small.shape), F32), dma((4,)), dma((4,)), dma((stages, 3)), dma((stages, 3)),
            dma((stages, 3)), dma((stages, 3)), dma((1 + stages,)), dma((1 + stages,)),
        ],
        compiler_params=params(collective_id=cid, has_side_effects=True),
        cost_estimate=cost(1e7, 5e7),
        name="totals",
    )(q_own, p_own, small, q_oth, p_oth)


def output_kernel(tcol_ref, y0, y1, y2, mid_ref, out_ref):
    rows = gather_rows(tcol_ref[...], (y0, y1, y2))
    out_ref[...] = (mid_ref[...] + rows.astype(BF).astype(F32)).astype(BF)


def output_call(tcol, ys, middle):
    tokens, width = middle.shape
    tb = 256
    rows = ys[0].shape[0]
    block = pl.BlockSpec((tb, width), lambda i: (i, 0))
    return pl.pallas_call(
        output_kernel,
        grid=(tokens // tb,),
        in_specs=[pl.BlockSpec((tb, 128), lambda i: (i, 0)), *[whole((rows, width))] * 3, block],
        out_specs=block,
        out_shape=jax.ShapeDtypeStruct((tokens, width), BF),
        compiler_params=params(),
        cost_estimate=cost(6 * tokens * rows * width, 1e7),
        name="output",
    )(tcol, *ys, middle)


def on_device(
    tokens, cotangent, segment_ids, expert_ids, qkv_weight, proj_weight, proj_bias, pre_gain, pre_shift,
    mid_gain, mid_shift, up_weight, up_bias, down_weight, down_bias,
):
    n = lax.axis_size("expert")
    count, width = tokens.shape
    cc = 3 * count // (2 * n) // CHUNKS
    rows = n * cc
    row = lambda v: v.reshape(1, -1)

    def swap(v):
        return lax.ppermute(v, "dp", [(0, 1), (1, 0)])

    qkv_oth = swap(qkv_weight)
    proj_oth = swap(proj_weight)
    down_own, up_own, bias_own = down_weight[0], up_weight[0], up_bias
    down_oth, up_oth, bias_oth = swap(down_own), swap(up_own), swap(bias_own)

    tcol, trow, cot_slots = slots_call(expert_ids, cotangent, cc, rows)
    norm, head_rows = heads_call(tokens, qkv_weight, qkv_oth, row(pre_gain), row(pre_shift))
    att, probs, middle, mid_slots, cot_arr = attend_call(
        n, tokens, segment_ids, head_rows, proj_weight, proj_oth, row(proj_bias), row(mid_gain), row(mid_shift),
        trow, cot_slots.reshape(CHUNKS, n, cc, width),
    )
    cot_rows = cot_arr.reshape(CHUNKS, rows, width)
    mid_slots = mid_slots.reshape(CHUNKS, n, cc, width)

    def flat(v):
        return v.reshape(rows, width)

    def routed(v):
        return v.reshape(n, cc, width)

    up, down, bias = (up_own, up_oth), (down_own, down_oth), (bias_own, bias_oth)
    arr0 = flat(route_call(n, mid_slots, 0, 2))
    act0, gh0, ub0, y0, dx0, arr1 = expert_call(
        n, 0, arr0, cot_rows, up, down, bias, down_bias, mid=mid_slots, mid_chunk=1, cid=3)
    arr1 = flat(arr1)
    act1, gh1, ub1, y1, dx1, arr2, gm0 = expert_call(
        n, 1, arr1, cot_rows, up, down, bias, down_bias, mid=mid_slots, mid_chunk=2, back=routed(dx0), cid=4)
    arr2 = flat(arr2)
    act2, gh2, ub2, y2, dx2, gm1 = expert_call(
        n, 2, arr2, cot_rows, up, down, bias, down_bias, back=routed(dx1), cid=5)
    acts, ghs, arrs = (act0, act1, act2), (gh0, gh1, gh2), (arr0, arr1, arr2)
    dw_oth, uw_oth, cot_sum, gm2 = wgrad_oth_call(n, acts, ghs, cot_rows, arrs, routed(dx2), 6)
    hid = down_own.shape[0]
    bias_sum = ub0[0] + ub1[0] + ub2[0]
    got_down, got_up = swap(dw_oth), swap(uw_oth)
    small_oth = swap(jnp.concatenate([bias_sum[hid:], cot_sum[0]]))
    upbias_grad = row(bias_sum[:hid] + small_oth[:hid])
    downbias_grad = row(cot_sum[0] + small_oth[hid:])

    gmid, gatt, pg_own, pg_oth, small_mid, z0 = middle_back_call(
        n, tcol, (flat(gm0), flat(gm1), flat(gm2)), middle, cotangent, row(mid_gain), proj_weight, proj_oth, att,
        routed(y0), 7)
    dq, dk, dv, z1 = attend_back_call(n, head_rows, probs, gatt, att, routed(y1), 8)
    qg_own, qg_oth, input_grad, small_pre, z2 = heads_back_call(
        n, tokens, norm, (dq, dk, dv), qkv_weight, qkv_oth, gmid, row(pre_gain), routed(y2), 9)
    small = jnp.concatenate([small_pre[0:2], small_mid[0:3], jnp.zeros((3, width), F32)], axis=0)
    qkv_grad, proj_grad, small = total_call(n, qg_own, pg_own, small, qg_oth, pg_oth, 10)
    down_grad, up_grad = wgrad_own_call(acts, ghs, cot_rows, arrs, got_down, got_up)
    output = output_call(tcol, (flat(z0), flat(z1), flat(z2)), middle)
    return (
        output, input_grad, qkv_grad, proj_grad, small[4], small[0], small[1], small[2], small[3],
        up_grad[None], upbias_grad, down_grad[None], downbias_grad,
    )


def solution(mesh):
    token = P(("dp", "expert"), None)
    in_specs = (
        token, token, token, token, P(None, None, "dp"), P("dp", None), P(), P(), P(), P(), P(),
        P("expert", "dp", None), P("expert", "dp"), P("expert", "dp", None), P("expert", None),
    )
    out_specs = (
        token, token, P(None, None, "dp"), P("dp", None), P(), P(), P(), P(), P(),
        P("expert", "dp", None), P("expert", "dp"), P("expert", "dp", None), P("expert", None),
    )
    return jax.shard_map(on_device, mesh=mesh, in_specs=in_specs, out_specs=out_specs, check_vma=False)
```

```python
import functools

import jax
import jax.numpy as jnp
from jax import lax
from jax.experimental import pallas as pl
from jax.experimental.pallas import tpu as pltpu
from jax.sharding import PartitionSpec as P

HEAD_DIM = 64
SEQ = 1024
DOC_MAX = 512
EPS = 1e-05
QB = 256
CHUNKS = 3
BF = jnp.bfloat16
F32 = jnp.float32
MESH = pl.DeviceIdType.MESH
VMEM_LIMIT = 60 * 1024 * 1024

BLOCKS = SEQ // QB
START = [max(0, i * QB - DOC_MAX) for i in range(BLOCKS)]
WIDTH = [(i + 1) * QB - START[i] for i in range(BLOCKS)]
OFFSET = [sum(WIDTH[:i]) for i in range(BLOCKS)]
BAND = sum(WIDTH)


def dot(a, b):
    return jnp.dot(a, b, preferred_element_type=F32)


def dot_nt(a, b):
    return lax.dot_general(a, b, (((1,), (1,)), ((), ())), preferred_element_type=F32)


def dot_tn(a, b):
    return lax.dot_general(a, b, (((0,), (0,)), ((), ())), preferred_element_type=F32)


def params(**kw):
    return pltpu.CompilerParams(vmem_limit_bytes=VMEM_LIMIT, **kw)


def cost(flops, nbytes, trans=0):
    return pl.CostEstimate(flops=int(flops), bytes_accessed=int(nbytes), transcendentals=int(trans))


ANY = pl.BlockSpec(memory_space=pl.ANY)


def whole(shape):
    return pl.BlockSpec(shape, lambda *_: (0,) * len(shape))


def block_of(index, size):
    return pl.ds(pl.multiple_of(index * size, size), size)


class Route:
    def __init__(self, n, src, dst, send, recv, local):
        self.n, self.src, self.dst = n, src, dst
        self.send, self.recv, self.local = send, recv, local

    def remote(self):
        me = lax.axis_index("expert")
        for d in range(1, self.n):
            there = lax.rem(me + d, self.n)
            yield pltpu.make_async_remote_copy(
                self.src(there), self.dst(me), self.send.at[d], self.recv.at[d],
                device_id={"expert": there}, device_id_type=MESH,
            )

    def own(self):
        me = lax.axis_index("expert")
        return pltpu.make_async_copy(self.src(me), self.dst(me), self.local)

    def start(self):
        for c in self.remote():
            c.start()
        self.own().start()

    def wait(self):
        self.own().wait()
        for c in self.remote():
            c.wait()


def route_sems(n, count):
    return [
        pltpu.SemaphoreType.DMA((count, n)),
        pltpu.SemaphoreType.DMA((count, n)),
        pltpu.SemaphoreType.DMA((count,)),
    ]


def greet(n, partner):
    me = lax.axis_index("expert")
    barrier = pltpu.get_barrier_semaphore()
    for d in range(1, n):
        pl.semaphore_signal(
            barrier, inc=1, device_id={"expert": lax.rem(me + d, n)}, device_id_type=MESH
        )
    if partner:
        pl.semaphore_signal(barrier, inc=1, device_id={"dp": 1 - lax.axis_index("dp")}, device_id_type=MESH)
    pl.semaphore_wait(barrier, n if partner else n - 1)


def to_partner(src, dst, send, recv):
    return pltpu.make_async_remote_copy(
        src, dst, send, recv, device_id={"dp": 1 - lax.axis_index("dp")}, device_id_type=MESH
    )


def unit_of(values):
    centre = values - jnp.mean(values, axis=-1, keepdims=True)
    inverse = lax.rsqrt(jnp.mean(centre * centre, axis=-1, keepdims=True) + EPS)
    return centre * inverse, inverse


def lane_pick(width, first):
    lanes = lax.broadcasted_iota(jnp.int32, (1, width), 1)
    return (lanes < HEAD_DIM) if first else (lanes >= HEAD_DIM)


PRE_GAIN, PRE_SHIFT, PROJ_BIAS, MID_GAIN, MID_SHIFT = range(5)


def front_kernel(
    n, cc, pairs, ids_ref, cot_ref, x_ref, seg_ref, vec_ref, w_ref, w_any, p_ref, p_any,
    tcol_ref, norm_ref, hr_ref, att_ref, prob_ref, mid_ref, slot_ref, arr_ref, wo_out, po_out,
    row_s, cs_s, norm_s, hr_s, wo_s, po_s, bias_s, low_s, send, recv, local, dsend, drecv, dlocal,
):
    step = pl.program_id(0)
    tokens, width = x_ref.shape
    half = p_ref.shape[0]
    rows = n * cc
    first_pair = 7
    routes = [
        Route(
            n, lambda e, c=c: cs_s.at[block_of(c * n + e, cc)], lambda d, c=c: arr_ref.at[c, block_of(d, cc)],
            send.at[c], recv.at[c], local.at[c],
        )
        for c in range(CHUNKS)
    ]

    def swaps():
        return [
            to_partner(w_any, wo_s, dsend.at[0], drecv.at[0]),
            to_partner(p_any, po_s, dsend.at[1], drecv.at[1]),
        ]

    def keeps():
        return [
            pltpu.make_async_copy(wo_s, wo_out, dlocal.at[0]),
            pltpu.make_async_copy(po_s, po_out, dlocal.at[1]),
        ]

    @pl.when(step == 0)
    def _():
        greet(n, True)
        for c in swaps():
            c.start()
        ids = jnp.transpose(jnp.broadcast_to(ids_ref[...].astype(F32), (128, tokens)))
        hot = (ids == lax.broadcasted_iota(jnp.int32, (tokens, 128), 1).astype(F32)).astype(F32)
        low_hot = hot.astype(BF)
        place = []
        for b in range(tokens // 256):
            span = (b + 1) * 256
            lower = (
                lax.broadcasted_iota(jnp.int32, (256, span), 0) + b * 256
                >= lax.broadcasted_iota(jnp.int32, (256, span), 1)
            ).astype(F32).astype(BF)
            counts = dot(lower, low_hot[0:span])
            rank = jnp.sum(counts * hot[b * 256:span], axis=1, keepdims=True) - 1.0
            chunk = jnp.floor((rank + 0.5) * (1.0 / cc))
            place.append(chunk * rows + ids[b * 256:span] * cc + (rank - chunk * cc))
        place = jnp.concatenate(place, axis=0)
        tcol_ref[...] = place.astype(jnp.int32)
        row_s[...] = jnp.transpose(place)[0:8, :].astype(jnp.int32)

        def fill(b, _):
            hot = (
                lax.broadcasted_iota(jnp.int32, (256, tokens), 0) + b * 256 == row_s[0:1, :]
            ).astype(F32).astype(BF)
            cs_s[block_of(b, 256), :] = dot(hot, cot_ref[...]).astype(BF)
            return 0

        lax.fori_loop(0, CHUNKS * rows // 256, fill, 0)
        for r in routes:
            r.start()

        gain, shift = vec_ref[PRE_GAIN:PRE_GAIN + 1, :], vec_ref[PRE_SHIFT:PRE_SHIFT + 1, :]

        def body(b, _):
            at = block_of(b, 128)
            unit, _ = unit_of(x_ref[at, :].astype(F32))
            low = (unit * gain + shift).astype(BF)
            norm_s[at, :] = low
            norm_ref[at, :] = low
            return 0

        lax.fori_loop(0, tokens // 128, body, 0)

    @pl.when((step >= 1) & (step <= 3))
    def _():
        out = dot(norm_s[...], w_ref[0]).astype(BF)
        hr_ref[0] = out
        hr_s[step - 1] = out

    @pl.when(step == 4)
    def _():
        for c in swaps():
            c.wait()
        for c in keeps():
            c.start()

    @pl.when((step >= 4) & (step <= 6))
    def _():
        out = dot(norm_s[...], wo_s[step - 4]).astype(BF)
        hr_ref[0] = out
        hr_s[step - 1] = out

    @pl.when(step == first_pair)
    def _():
        seg = seg_ref[...].astype(F32)
        seg_col = jnp.transpose(jnp.broadcast_to(seg, (128, tokens)))
        for i in range(BLOCKS):
            w, s = WIDTH[i], START[i]
            at_row = lax.broadcasted_iota(jnp.int32, (QB, w), 0) + i * QB
            at_key = lax.broadcasted_iota(jnp.int32, (QB, w), 1) + s
            same = seg_col[i * QB:(i + 1) * QB, 0:1] == seg[:, s:s + w]
            bias_s[:, OFFSET[i]:OFFSET[i] + w] = jnp.where(same & (at_key <= at_row), 0.0, -1e30)

    @pl.when((step >= first_pair) & (step < first_pair + pairs))
    def _():
        pair = step - first_pair
        per = half // 128
        side, lanes = lax.div(pair, per), block_of(lax.rem(pair, per), 128)
        query = hr_s[3 * side, :, lanes] * BF(HEAD_DIM ** -0.5)
        for i in range(BLOCKS):
            w, s = WIDTH[i], START[i]
            keys, values = hr_s[3 * side + 1, s:s + w, lanes], hr_s[3 * side + 2, s:s + w, lanes]
            bias = bias_s[:, OFFSET[i]:OFFSET[i] + w]
            parts = []
            for j in range(2):
                q = jnp.where(lane_pick(128, j == 0), query[i * QB:(i + 1) * QB], BF(0))
                scores = dot_nt(q, keys) + bias
                top = jnp.max(scores, axis=-1, keepdims=True)
                weights = jnp.exp(scores - top)
                probs = (weights * (1.0 / jnp.sum(weights, axis=-1, keepdims=True))).astype(BF)
                prob_ref[j, :, OFFSET[i]:OFFSET[i] + w] = probs
                parts.append(dot(probs, values))
            both = jnp.where(lane_pick(128, True), parts[0], parts[1])
            att_ref[i * QB:(i + 1) * QB, block_of(pair, 128)] = both.astype(BF)

    @pl.when(step == first_pair + pairs)
    def _():
        pbias = vec_ref[PROJ_BIAS:PROJ_BIAS + 1, :]
        gain, shift = vec_ref[MID_GAIN:MID_GAIN + 1, :], vec_ref[MID_SHIFT:MID_SHIFT + 1, :]

        def body(b, _):
            at = block_of(b, 128)
            branch = dot(att_ref[at, 0:half], p_ref[...]) + dot(att_ref[at, half:2 * half], po_s[...])
            middle = x_ref[at, :].astype(F32) + branch + pbias
            mid_ref[at, :] = middle
            unit, _ = unit_of(middle)
            low_s[at, :] = (unit * gain + shift).astype(BF)
            return 0

        lax.fori_loop(0, tokens // 128, body, 0)

        def fill(b, _):
            hot = (
                lax.broadcasted_iota(jnp.int32, (256, tokens), 0) + b * 256 == row_s[0:1, :]
            ).astype(F32).astype(BF)
            slot_ref[block_of(b, 256), :] = dot(hot, low_s[...]).astype(BF)
            return 0

        lax.fori_loop(0, CHUNKS * rows // 256, fill, 0)
        for c in keeps():
            c.wait()
        for r in routes:
            r.wait()


def front_call(n, cc, ids, cot, x, seg, vec, qkv, proj):
    tokens, width = x.shape
    half = proj.shape[0]
    pairs = width // 128
    rows = n * cc
    dma = pltpu.SemaphoreType.DMA
    sds = jax.ShapeDtypeStruct

    def pair_of(i):
        return jnp.clip(i - 7, 0, pairs - 1)

    return pl.pallas_call(
        functools.partial(front_kernel, n, cc, pairs),
        grid=(8 + pairs,),
        in_specs=[
            whole((1, tokens)), whole((tokens, width)), whole((tokens, width)), whole((1, tokens)),
            whole(vec.shape),
            pl.BlockSpec((1, width, half), lambda i: (jnp.clip(i - 1, 0, 2), 0, 0)), ANY,
            whole((half, width)), ANY,
        ],
        out_specs=[
            whole((tokens, 128)), whole((tokens, width)),
            pl.BlockSpec((1, tokens, half), lambda i: (jnp.clip(i - 1, 0, 5), 0, 0)),
            whole((tokens, width)), pl.BlockSpec((2, QB, BAND), lambda i: (pair_of(i), 0, 0)),
            whole((tokens, width)), whole((CHUNKS * rows, width)), ANY, ANY, ANY,
        ],
        out_shape=[
            sds((tokens, 128), jnp.int32), sds((tokens, width), BF), sds((6, tokens, half), BF),
            sds((tokens, width), BF), sds((2 * pairs, QB, BAND), BF), sds((tokens, width), F32),
            sds((CHUNKS * rows, width), BF), sds((CHUNKS, rows, width), BF), sds(qkv.shape, BF), sds(proj.shape, BF),
        ],
        scratch_shapes=[
            pltpu.VMEM((8, tokens), jnp.int32), pltpu.VMEM((CHUNKS * rows, width), BF),
            pltpu.VMEM((tokens, width), BF), pltpu.VMEM((6, tokens, half), BF), pltpu.VMEM(qkv.shape, BF),
            pltpu.VMEM(proj.shape, BF), pltpu.VMEM((QB, BAND), F32), pltpu.VMEM((tokens, width), BF),
            *route_sems(n, CHUNKS), dma((2,)), dma((2,)), dma((2,)),
        ],
        compiler_params=params(collective_id=1, has_side_effects=True),
        cost_estimate=cost(3e10, 6e7),
        name="front",
    )(ids, cot, x, seg, vec, qkv, qkv, proj, proj)


GELU_C = 0.7978845608028654
GELU_A = 0.044715
TILE = 512


def expert_kernel(
    n, cc, own_tiles, mid_ref, c_ref, uo_ref, ut_ref, do_ref, dt_ref, bo_ref, bt_ref, db_ref,
    act_ref, gh_ref, ub_ref, y_ref, dx_ref, x_out, back_out,
    x_s, g_s, y_s, dx_s, dxb_s, send, recv, local, xsem,
):
    step = pl.program_id(0)
    tiles = 2 * own_tiles
    phase, tile = lax.div(step, tiles), lax.rem(step, tiles)
    rows = n * cc
    ins = [
        Route(
            n, lambda e, c=c: mid_ref.at[block_of(c * n + e, cc)], lambda d, c=c: x_s.at[c, block_of(d, cc)],
            send.at[c], recv.at[c], local.at[c],
        )
        for c in range(CHUNKS)
    ]
    back = Route(
        n, lambda e: dxb_s.at[block_of(e, cc)], lambda d: back_out.at[block_of(d, cc)],
        send.at[CHUNKS], recv.at[CHUNKS], local.at[CHUNKS],
    )

    def keep(c):
        return pltpu.make_async_copy(x_s.at[c], x_out.at[c], xsem.at[c])

    @pl.when(step == 0)
    def _():
        greet(n, False)
        ins[0].start()
        ub_ref[...] = jnp.zeros_like(ub_ref)

    for c in range(CHUNKS):
        @pl.when(step == (c + 1) * tiles)
        def _():
            ins[c].wait()
            if c + 1 < CHUNKS:
                ins[c + 1].start()
            else:
                back.start()
            keep(c).start()

    lanes = block_of(tile, TILE)

    def early(down_ref):
        for c in range(CHUNKS):
            g_s[c, :, lanes] = dot_nt(c_ref[c], down_ref[...]).astype(BF)

    def late(c, up_ref, down_ref, b_ref):
        up, down = up_ref[...], down_ref[...]
        h = dot_nt(x_s[c], up) + b_ref[...].astype(F32)
        sq = h * h
        t = jnp.tanh(GELU_C * (h + GELU_A * (sq * h)))
        act = ((0.5 * h) * (1.0 + t)).astype(BF)
        act_ref[0] = act
        slope = 0.5 * (1.0 + t) + (0.5 * h) * ((1.0 - t * t) * (GELU_C * (1.0 + (3.0 * GELU_A) * sq)))
        gh = (g_s[c, :, lanes].astype(F32) * slope).astype(BF)
        gh_ref[0] = gh
        ub_ref[0:1, lanes] += jnp.sum(gh.astype(F32), axis=0, keepdims=True)
        y_s[...] += dot(act, down)
        dx_s[...] += dot(gh, up)

    @pl.when((phase >= 1) & (tile == 0))
    def _():
        y_s[...] = jnp.broadcast_to(db_ref[...].astype(F32), y_s.shape)
        dx_s[...] = jnp.zeros_like(dx_s)

    @pl.when((phase == 0) & (tile < own_tiles))
    def _():
        early(do_ref)

    @pl.when((phase == 0) & (tile >= own_tiles))
    def _():
        early(dt_ref)

    @pl.when((phase >= 1) & (tile < own_tiles))
    def _():
        late(phase - 1, uo_ref, do_ref, bo_ref)

    @pl.when((phase >= 1) & (tile >= own_tiles))
    def _():
        late(phase - 1, ut_ref, dt_ref, bt_ref)

    @pl.when((phase >= 1) & (tile == tiles - 1))
    def _():
        y_ref[0] = y_s[...].astype(BF)
        dx_ref[0] = dx_s[...].astype(BF)

    @pl.when((phase == 1) & (tile == tiles - 1))
    def _():
        dxb_s[...] = dx_s[...].astype(BF)

    @pl.when(step == (CHUNKS + 1) * tiles - 1)
    def _():
        for c in range(CHUNKS):
            keep(c).wait()
        back.wait()


def expert_call(n, cc, mid_slots, cot, up, down, bias, down_bias):
    up_own, up_oth = up
    down_own, down_oth = down
    b_own, b_oth = bias
    rows = n * cc
    hid, width = up_own.shape
    own_tiles = hid // TILE
    tiles = 2 * own_tiles
    sds = jax.ShapeDtypeStruct

    def first(i):
        return jnp.minimum(i % tiles, own_tiles - 1)

    def second(i):
        return jnp.maximum(i % tiles - own_tiles, 0)

    def up_first(i):
        return jnp.where(i < tiles, 0, first(i))

    def up_second(i):
        return jnp.where(i < tiles, 0, second(i))

    def chunk(i):
        return jnp.maximum(i // tiles - 1, 0)

    def column(i):
        return jnp.where(i < tiles, 0, i % tiles)

    col = pl.BlockSpec((1, rows, TILE), lambda i: (chunk(i), 0, column(i)))
    per_chunk = pl.BlockSpec((1, rows, width), lambda i: (chunk(i), 0, 0))
    return pl.pallas_call(
        functools.partial(expert_kernel, n, cc, own_tiles),
        grid=((CHUNKS + 1) * tiles,),
        in_specs=[
            ANY, whole(cot.shape),
            pl.BlockSpec((TILE, width), lambda i: (up_first(i), 0)),
            pl.BlockSpec((TILE, width), lambda i: (up_second(i), 0)),
            pl.BlockSpec((TILE, width), lambda i: (first(i), 0)),
            pl.BlockSpec((TILE, width), lambda i: (second(i), 0)),
            pl.BlockSpec((1, TILE), lambda i: (0, first(i))),
            pl.BlockSpec((1, TILE), lambda i: (0, second(i))),
            whole((1, width)),
        ],
        out_specs=[col, col, whole((8, 2 * hid)), per_chunk, per_chunk, ANY, ANY],
        out_shape=[
            sds((CHUNKS, rows, 2 * hid), BF), sds((CHUNKS, rows, 2 * hid), BF), sds((8, 2 * hid), F32),
            sds((CHUNKS, rows, width), BF), sds((CHUNKS, rows, width), BF), sds((CHUNKS, rows, width), BF),
            sds((rows, width), BF),
        ],
        scratch_shapes=[
            pltpu.VMEM((CHUNKS, rows, width), BF), pltpu.VMEM((CHUNKS, rows, 2 * hid), BF),
            pltpu.VMEM((rows, width), F32), pltpu.VMEM((rows, width), F32), pltpu.VMEM((rows, width), BF),
            *route_sems(n, CHUNKS + 1), pltpu.SemaphoreType.DMA((CHUNKS,)),
        ],
        compiler_params=params(collective_id=2, has_side_effects=True),
        cost_estimate=cost(5.2e10, 8e7),
        name="experts",
    )(mid_slots, cot, up_own, up_oth, down_own, down_oth, b_own, b_oth, down_bias)


def wgrad_kernel(
    n, cc, tiles, a_ref, g_ref, c_ref, x_ref, ub_ref, dx_ref,
    do_ref, up_ref, ubg_ref, cbg_ref, back1, back2,
    out_s, in_s, small_s, got_s, send, recv, local, dsend, drecv, ssend, srecv,
):
    step = pl.program_id(0)
    hid = ubg_ref.shape[1]
    routes = [
        Route(
            n, lambda e, c=c: dx_ref.at[c, block_of(e, cc)], lambda d, dst=dst: dst.at[block_of(d, cc)],
            send.at[k], recv.at[k], local.at[k],
        )
        for k, (c, dst) in enumerate(((1, back1), (2, back2)))
    ]

    def swap(k):
        return to_partner(out_s.at[k], in_s.at[k], dsend.at[k], drecv.at[k])

    small = to_partner(small_s, got_s, ssend, srecv)

    @pl.when(step == 0)
    def _():
        greet(n, True)
        routes[0].start()
        total = jnp.zeros((1, c_ref.shape[2]), F32)
        for c in range(CHUNKS):
            total = total + jnp.sum(c_ref[c].astype(F32), axis=0, keepdims=True)
        small_s[...] = jnp.zeros_like(small_s)
        small_s[0:1, 0:hid] = ub_ref[0:1, hid:2 * hid]
        small_s[0:1, hid:hid + total.shape[1]] = total
        small.start()

    @pl.when(step == 2 * tiles)
    def _():
        routes[0].wait()
        routes[1].start()
        small.wait()
        ubg_ref[...] = ub_ref[0:1, 0:hid] + got_s[0:1, 0:hid]
        cbg_ref[...] = small_s[0:1, hid:] + got_s[0:1, hid:]

    def product(left, right):
        total = dot_tn(left[0], right[0])
        for c in range(1, CHUNKS):
            total = total + dot_tn(left[c], right[c])
        return total

    for k in range(2 * tiles):
        @pl.when(step == k)
        def _():
            left, right = (a_ref, c_ref) if k < tiles else (g_ref, x_ref)
            out_s[k] = product(left, right).astype(BF)
            swap(k).start()

        @pl.when(step == 2 * tiles + k)
        def _():
            left, right, out = (a_ref, c_ref, do_ref) if k < tiles else (g_ref, x_ref, up_ref)
            total = product(left, right)
            swap(k).wait()
            out[...] = (total + in_s[k].astype(F32)).astype(BF)

    @pl.when(step == 4 * tiles - 1)
    def _():
        routes[1].wait()


def wgrad_call(n, cc, acts, ghs, cot, rows_in, ub, dx):
    _, rows, width = cot.shape
    hid = acts.shape[2] // 2
    tiles = hid // TILE
    dma = pltpu.SemaphoreType.DMA
    sds = jax.ShapeDtypeStruct

    def first(i):
        return jnp.minimum(i % (2 * tiles), tiles - 1)

    def second(i):
        return jnp.maximum(i % (2 * tiles) - tiles, 0)

    def other(i):
        return jnp.where(i < 2 * tiles, tiles, 0)

    a_spec = pl.BlockSpec((CHUNKS, rows, TILE), lambda i: (0, 0, other(i) + first(i)))
    g_spec = pl.BlockSpec((CHUNKS, rows, TILE), lambda i: (0, 0, other(i) + second(i)))

    def late(i):
        return jnp.where(i < 2 * tiles, 0, 1)

    d_spec = pl.BlockSpec((TILE, width), lambda i: (late(i) * first(i), 0))
    u_spec = pl.BlockSpec((TILE, width), lambda i: (late(i) * second(i), 0))
    return pl.pallas_call(
        functools.partial(wgrad_kernel, n, cc, tiles),
        grid=(4 * tiles,),
        in_specs=[a_spec, g_spec, whole(cot.shape), whole(rows_in.shape), whole(ub.shape), ANY],
        out_specs=[d_spec, u_spec, whole((1, hid)), whole((1, width)), ANY, ANY],
        out_shape=[
            sds((hid, width), BF), sds((hid, width), BF), sds((1, hid), F32), sds((1, width), F32),
            sds((rows, width), BF), sds((rows, width), BF),
        ],
        scratch_shapes=[
            pltpu.VMEM((2 * tiles, TILE, width), BF), pltpu.VMEM((2 * tiles, TILE, width), BF),
            pltpu.VMEM((8, hid + width), F32), pltpu.VMEM((8, hid + width), F32),
            *route_sems(n, 2), dma((2 * tiles,)), dma((2 * tiles,)), dma, dma,
        ],
        compiler_params=params(collective_id=3, has_side_effects=True),
        cost_estimate=cost(2.6e10, 8e7),
        name="weight_grads",
    )(acts, ghs, cot, rows_in, ub, dx)


def gather_rows(tcol, parts):
    total = None
    for c, part in enumerate(parts):
        rows = part.shape[0]
        hot = (
            lax.broadcasted_iota(jnp.int32, (tcol.shape[0], rows), 1) + c * rows == tcol[:, 0:1]
        ).astype(F32).astype(BF)
        term = dot(hot, part)
        total = term if total is None else total + term
    return total


def norm_back(grad, unit, inverse, gain):
    scaled = grad * gain
    inner = jnp.mean(scaled, axis=-1, keepdims=True)
    along = jnp.mean(scaled * unit, axis=-1, keepdims=True)
    return inverse * (scaled - inner - unit * along)


def middle_back_kernel(
    n, cc, blocks, tcol_ref, g0, g1, g2, mid_ref, cot_ref, vec_ref, own_ref, oth_ref, att_ref, y_src,
    gmid_ref, gatt_ref, pg_own, pg_oth, small_ref, y_dst, gb_s, send, recv, local,
):
    route = Route(
        n, lambda e: y_src.at[0, block_of(e, cc)], lambda d: y_dst.at[block_of(d, cc)],
        send.at[0], recv.at[0], local.at[0],
    )
    step = pl.program_id(0)
    half = own_ref.shape[0]
    tb = mid_ref.shape[0]

    @pl.when(step == 0)
    def _():
        greet(n, False)
        route.start()
        small_ref[...] = jnp.zeros_like(small_ref)

    grad = gather_rows(tcol_ref[...], (g0[...], g1[...], g2[...]))
    grad = grad.astype(BF).astype(F32)
    unit, inverse = unit_of(mid_ref[...])
    gmid = cot_ref[...].astype(F32) + norm_back(grad, unit, inverse, vec_ref[MID_GAIN:MID_GAIN + 1, :])
    gmid_ref[...] = gmid
    gb = gmid.astype(BF)
    gb_s[block_of(step, tb), :] = gb
    small_ref[2:3, :] += jnp.sum(grad * unit, axis=0, keepdims=True)
    small_ref[3:4, :] += jnp.sum(grad, axis=0, keepdims=True)
    small_ref[4:5, :] += jnp.sum(gb.astype(F32), axis=0, keepdims=True)
    gatt_ref[:, 0:half] = dot_nt(gb, own_ref[...]).astype(BF)
    gatt_ref[:, half:2 * half] = dot_nt(gb, oth_ref[...]).astype(BF)

    @pl.when(step == blocks - 1)
    def _():
        pg_own[...] = dot_tn(att_ref[:, 0:half], gb_s[...]).astype(BF)
        pg_oth[...] = dot_tn(att_ref[:, half:2 * half], gb_s[...]).astype(BF)
        route.wait()


def middle_back_call(n, cc, tcol, grads, middle, cot, vec, proj_own, proj_oth, att, y):
    tokens, width = middle.shape
    half = proj_own.shape[0]
    tb = 256
    rows = grads[0].shape[0]
    block = pl.BlockSpec((tb, width), lambda i: (i, 0))
    sds = jax.ShapeDtypeStruct
    return pl.pallas_call(
        functools.partial(middle_back_kernel, n, cc, tokens // tb),
        grid=(tokens // tb,),
        in_specs=[
            pl.BlockSpec((tb, 128), lambda i: (i, 0)), *[whole((rows, width))] * 3, block, block,
            whole(vec.shape), whole((half, width)), whole((half, width)), whole((tokens, width)), ANY,
        ],
        out_specs=[block, block, whole((half, width)), whole((half, width)), whole((8, width)), ANY],
        out_shape=[
            sds((tokens, width), F32), sds((tokens, width), BF), sds((half, width), BF), sds((half, width), BF),
            sds((8, width), F32), sds((rows, width), BF),
        ],
        scratch_shapes=[pltpu.VMEM((tokens, width), BF), *route_sems(n, 1)],
        compiler_params=params(collective_id=4, has_side_effects=True),
        cost_estimate=cost(1.2e10, 3e7),
        name="middle_back",
    )(tcol, *grads, middle, cot, vec, proj_own, proj_oth, att, y)


class Part:
    def __init__(self, index, base, length, order, me, refs):
        self.index, self.base, self.total, self.order, self.me = index, base, length, order, me
        self.acc, self.rcv, self.res, self.rs_send, self.rs_recv, self.ag_send, self.ag_recv = refs
        self.stages, self.stage = len(order), 0
        self.step = length >> len(order)

    def upper(self, s):
        return lax.rem(lax.div(self.me, 1 << self.order[s]), 2)

    def rows(self, start, length):
        return pl.ds(pl.multiple_of(start, 16), length)

    def start(self, s):
        at = self.base
        for k in range(s):
            at = at + self.upper(k) * (self.total >> (k + 1))
        return at

    def slot(self, s):
        return self.base + self.total - (self.total >> s)

    def copy(self):
        inward = self.stage < self.stages
        s = self.stage if inward else 2 * self.stages - 1 - self.stage
        bit = 1 << self.order[s]
        peer = {"expert": self.me + bit - 2 * bit * self.upper(s)}
        if inward:
            half = self.total >> (s + 1)
            away = self.start(s) + (1 - self.upper(s)) * half
            src, dst = self.acc.at[self.rows(away, half)], self.rcv.at[pl.ds(self.slot(s), half)]
            send, recv = self.rs_send, self.rs_recv
        else:
            src = dst = self.res.at[self.rows(self.start(s + 1), self.total >> (s + 1))]
            send, recv = self.ag_send, self.ag_recv
        return pltpu.make_async_remote_copy(
            src, dst, send.at[self.index, s], recv.at[self.index, s], device_id=peer, device_id_type=MESH
        )

    def begin(self):
        self.copy().start()

    def advance(self):
        self.copy().wait()
        s = self.stage
        if s < self.stages:
            keep, slot, step = self.start(s + 1), self.slot(s), self.step
            into = self.res if s == self.stages - 1 else self.acc

            def add(b, _):
                at = self.rows(keep + b * step, step)
                into[at, :] = (
                    self.acc[at, :].astype(F32) + self.rcv[self.rows(slot + b * step, step), :].astype(F32)
                ).astype(BF)
                return 0

            lax.fori_loop(0, (self.total >> (s + 1)) // step, add, 0)
        self.stage += 1
        if self.stage < 2 * self.stages:
            self.copy().start()


def back_kernel(
    n, cc, pairs, q_ref, k_ref, v_ref, prob_ref, do_ref, o_ref, x_ref, norm_ref, own_ref, oth_ref, gmid_ref,
    vec_ref, small_ref, pg_own, pg_oth, y_src,
    xg_ref, small_out, sum_out, z1, z2,
    dk_s, dv_s, gh_s, gnp_s, acc, rcv, res, got, pgot, snd, small_got,
    send, recv, local, dsend, drecv, rs_send, rs_recv, ag_send, ag_recv, sm_send, sm_recv, out_sem,
):
    step = pl.program_id(0)
    tokens, width = x_ref.shape
    half = own_ref.shape[2]
    scale = HEAD_DIM ** -0.5
    per = half // 128
    me = lax.axis_index("expert")
    stages = n.bit_length() - 1
    routes = [
        Route(
            n, lambda e, c=c: y_src.at[c, block_of(e, cc)], lambda d, z=z: z.at[block_of(d, cc)],
            send.at[c - 1], recv.at[c - 1], local.at[c - 1],
        )
        for c, z in ((1, z1), (2, z2))
    ]

    split = max(1, min(2, width // (32 * n)))
    size = width // split
    turn = max(1, stages - 1)
    refs = (acc, rcv, res, rs_send, rs_recv, ag_send, ag_recv)

    def part(i):
        order = [(i + s) % turn for s in range(turn)] + ([turn] if stages > turn else [])
        return Part(i, i * size, size, order, me, refs)

    proj_parts = [part(3 * split + i) for i in range(split)]
    head_parts = [[part(c * split + i) for i in range(split)] for c in range(3)]

    def dp_swap(c):
        src = snd.at[c] if c < 3 else pg_oth
        dst = got.at[c] if c < 3 else pgot
        return to_partner(src, dst, dsend.at[c], drecv.at[c])

    @pl.when(step == 0)
    def _():
        greet(n, True)
        dp_swap(3).start()
        routes[0].start()
        gnp_s[...] = jnp.zeros_like(gnp_s)

    @pl.when(step < pairs)
    def _():
        side, lanes = lax.div(step, per), block_of(lax.rem(step, per), 128)
        dk_s[...] = jnp.zeros_like(dk_s)
        dv_s[...] = jnp.zeros_like(dv_s)
        for i in range(BLOCKS):
            w, s = WIDTH[i], START[i]
            at = slice(i * QB, (i + 1) * QB)
            keys, values = k_ref[0, s:s + w, :], v_ref[0, s:s + w, :]
            go = do_ref[at, :]
            prod = go.astype(F32) * o_ref[at, :].astype(F32)
            query = q_ref[0, at, :]
            parts = []
            for j in range(2):
                pick = lane_pick(128, j == 0)
                go_j = jnp.where(pick, go, BF(0))
                q_j = jnp.where(pick, query, BF(0))
                inner = jnp.sum(jnp.where(pick, prod, 0.0), axis=-1, keepdims=True)
                probs = prob_ref[j, :, OFFSET[i]:OFFSET[i] + w]
                gp = dot_nt(go_j, values)
                gs = (probs.astype(F32) * (gp - inner)).astype(BF)
                parts.append(dot(gs, keys))
                dk_s[s:s + w, :] += dot_tn(gs, q_j)
                dv_s[s:s + w, :] += dot_tn(probs, go_j)
            gh_s[3 * side, at, lanes] = (jnp.where(lane_pick(128, True), parts[0], parts[1]) * scale).astype(BF)
        gh_s[3 * side + 1, :, lanes] = (dk_s[...] * scale).astype(BF)
        gh_s[3 * side + 2, :, lanes] = dv_s[...].astype(BF)

    def bring_to(parts, goal):
        while parts[0].stage < goal:
            for p in parts:
                p.advance()

    total_stages = 2 * stages

    @pl.when(step == 1)
    def _():
        dp_swap(3).wait()
        base = 3 * width
        for b in range(width // half):
            for p in range(half // 128):
                at = slice(p * 128, (p + 1) * 128)
                acc[base + b * half + p * 128:base + b * half + (p + 1) * 128, :] = (
                    pg_own[at, b * half:(b + 1) * half].astype(F32)
                    + pgot[at, b * half:(b + 1) * half].astype(F32)
                ).astype(BF)
        for p in proj_parts:
            p.begin()

    last = pairs + 6
    for t in range(2, last):
        goal = t - 1 if t < last - 1 else total_stages
        goal = min(goal, total_stages)
        prev = min(t - 2, total_stages)
        if goal > prev:
            @pl.when(step == t)
            def _():
                bring_to(proj_parts, goal)

    @pl.when(step == pairs - 1)
    def _():
        routes[0].wait()
        routes[1].start()

    for c in range(3):
        @pl.when(step == pairs + c)
        def _():
            g = gh_s[3 + c]
            snd[c] = dot_tn(norm_ref[...], g).astype(BF)
            dp_swap(c).start()
            gnp_s[...] += dot_nt(g, oth_ref[0])

        @pl.when(step == pairs + 3 + c)
        def _():
            g = gh_s[c]
            mine = dot_tn(norm_ref[...], g)
            dp_swap(c).wait()
            acc[c * width:(c + 1) * width, :] = (mine + got[c].astype(F32)).astype(BF)
            for p in head_parts[c]:
                p.begin()
            gnp_s[...] += dot_nt(g, own_ref[0])

    @pl.when(step == last)
    def _():
        small_out[...] = small_ref[...]

        def body(b, _):
            at = block_of(b, 128)
            grad = gnp_s[at, :]
            unit, inverse = unit_of(x_ref[at, :].astype(F32))
            xg_ref[at, :] = gmid_ref[at, :] + norm_back(grad, unit, inverse, vec_ref[PRE_GAIN:PRE_GAIN + 1, :])
            small_out[0:1, :] += jnp.sum(grad * unit, axis=0, keepdims=True)
            small_out[1:2, :] += jnp.sum(grad, axis=0, keepdims=True)
            return 0

        lax.fori_loop(0, tokens // 128, body, 0)

        def small_swap(k):
            if k == 0:
                peer = {"dp": 1 - lax.axis_index("dp")}
            else:
                bit = 1 << (k - 1)
                peer = {"expert": me + bit - 2 * bit * lax.rem(lax.div(me, bit), 2)}
            return pltpu.make_async_remote_copy(
                small_out, small_got.at[k], sm_send.at[k], sm_recv.at[k], device_id=peer, device_id_type=MESH
            )

        everything = [p for group in head_parts for p in group]
        small = small_swap(0)
        small.start()
        for s in range(total_stages):
            for p in everything:
                p.advance()
            if s <= stages:
                small.wait()
                small_out[...] += small_got[s]
                if s < stages:
                    small = small_swap(s + 1)
                    small.start()
        out = pltpu.make_async_copy(res, sum_out, out_sem)
        out.start()
        out.wait()
        routes[1].wait()


def back_call(n, cc, head_rows, probs, gatt, att, x, norm, own, oth, gmid, vec, small, pg_own, pg_oth, y):
    tokens, width = x.shape
    half = own.shape[2]
    pairs, per = width // 128, half // 128
    rows = n * cc
    stages = n.bit_length() - 1
    split = max(1, min(2, width // (32 * n)))
    parts = 4 * split
    sds, dma, once = jax.ShapeDtypeStruct, pltpu.SemaphoreType.DMA, pl.Buffered(1)
    total = 4 * width

    def pair_of(i):
        return jnp.minimum(i, pairs - 1)

    def head(c):
        return pl.BlockSpec((1, tokens, 128), lambda i: (3 * (pair_of(i) // per) + c, 0, pair_of(i) % per))

    def fixed(shape):
        return pl.BlockSpec(shape, lambda *_: (0,) * len(shape), pipeline_mode=once)

    cols = pl.BlockSpec((tokens, 128), lambda i: (0, pair_of(i)))
    return pl.pallas_call(
        functools.partial(back_kernel, n, cc, pairs),
        grid=(pairs + 7,),
        in_specs=[
            head(0), head(1), head(2), pl.BlockSpec((2, QB, BAND), lambda i: (pair_of(i), 0, 0)), cols, cols,
            fixed((tokens, width)), fixed((tokens, width)),
            pl.BlockSpec((1, width, half), lambda i: (jnp.clip(i - pairs - 3, 0, 2), 0, 0)),
            pl.BlockSpec((1, width, half), lambda i: (jnp.clip(i - pairs, 0, 2), 0, 0)),
            fixed((tokens, width)), fixed(vec.shape), fixed(small.shape), fixed((half, width)), ANY, ANY,
        ],
        out_specs=[fixed((tokens, width)), fixed(small.shape), ANY, ANY, ANY],
        out_shape=[
            sds((tokens, width), F32), sds(small.shape, F32), sds((total, half), BF),
            sds((rows, width), BF), sds((rows, width), BF),
        ],
        scratch_shapes=[
            pltpu.VMEM((tokens, 128), F32), pltpu.VMEM((tokens, 128), F32), pltpu.VMEM((6, tokens, half), BF),
            pltpu.VMEM((tokens, width), F32), pltpu.VMEM((total, half), BF), pltpu.VMEM((total, half), BF),
            pltpu.VMEM((total, half), BF), pltpu.VMEM((3, width, half), BF), pltpu.VMEM((half, width), BF),
            pltpu.VMEM((3, width, half), BF),
            pltpu.VMEM((1 + stages, *small.shape), F32),
            *route_sems(n, 2), dma((4,)), dma((4,)), dma((parts, stages)), dma((parts, stages)),
            dma((parts, stages)), dma((parts, stages)), dma((1 + stages,)), dma((1 + stages,)), dma,
        ],
        compiler_params=params(collective_id=5, has_side_effects=True),
        cost_estimate=cost(5.3e10, 9e7),
        name="back",
    )(head_rows, head_rows, head_rows, probs, gatt, att, x, norm, own, oth, gmid, vec, small, pg_own, pg_oth, y)


def result_kernel(tcol_ref, z0, z1, z2, mid_ref, sum_q, sum_p, xg_ref, wd_ref, wu_ref, out_ref, q_ref, p_ref, xo_ref, do_ref, uo_ref):
    rows = gather_rows(tcol_ref[...], (z0[...], z1[...], z2[...]))
    out_ref[...] = (mid_ref[...] + rows.astype(BF).astype(F32)).astype(BF)
    q_ref[...] = sum_q[...].astype(F32)
    p_ref[...] = sum_p[...].astype(F32)
    xo_ref[...] = xg_ref[...]
    do_ref[...] = wd_ref[...].astype(F32)
    uo_ref[...] = wu_ref[...].astype(F32)


def result_call(tcol, zs, middle, sums, xg, wd, wu):
    tokens, width = middle.shape
    half = sums.shape[1]
    hid = wd.shape[0]
    rows = zs[0].shape[0]
    steps = 8
    tb, qb, pb, wb = tokens // steps, 3 * width // steps, width // steps, hid // steps
    sds = jax.ShapeDtypeStruct
    side = half // pb

    def rows_of(size, cols):
        return pl.BlockSpec((size, cols), lambda i: (i, 0))

    p_out = pl.BlockSpec((pb, half), lambda i: (i % side, i // side))
    return pl.pallas_call(
        result_kernel,
        grid=(steps,),
        in_specs=[
            rows_of(tb, 128), *[whole((rows, width))] * 3, rows_of(tb, width), rows_of(qb, half),
            pl.BlockSpec((pb, half), lambda i: (3 * steps + i, 0)), rows_of(tb, width), rows_of(wb, width),
            rows_of(wb, width),
        ],
        out_specs=[rows_of(tb, width), rows_of(qb, half), p_out, rows_of(tb, width), rows_of(wb, width), rows_of(wb, width)],
        out_shape=[
            sds((tokens, width), BF), sds((3 * width, half), F32), sds((half, width), F32), sds((tokens, width), F32),
            sds((hid, width), F32), sds((hid, width), F32),
        ],
        compiler_params=params(),
        cost_estimate=cost(6 * tokens * rows * width, 6e7),
        name="results",
    )(tcol, *zs, middle, sums, sums, xg, wd, wu)


def on_device(
    tokens, cotangent, segment_ids, expert_ids, qkv_weight, proj_weight, proj_bias, pre_gain, pre_shift,
    mid_gain, mid_shift, up_weight, up_bias, down_weight, down_bias,
):
    n = lax.axis_size("expert")
    count, width = tokens.shape
    cc = 3 * count // (2 * n) // CHUNKS

    def swap(v):
        return lax.ppermute(v, "dp", [(0, 1), (1, 0)])

    down_own, up_own = down_weight[0], up_weight[0]
    up, down = (up_own, swap(up_own)), (down_own, swap(down_own))
    bias = (up_bias, swap(up_bias))
    vec = jnp.stack([pre_gain, pre_shift, proj_bias, mid_gain, mid_shift]).astype(F32)

    tcol, norm, head_rows, att, probs, middle, mid_slots, cot_rows, qkv_oth, proj_oth = front_call(
        n, cc, expert_ids.reshape(1, count), cotangent, tokens, segment_ids, vec, qkv_weight, proj_weight)
    acts, ghs, ub, y, dx, arrived, gm0 = expert_call(n, cc, mid_slots, cot_rows, up, down, bias, down_bias)
    down_grad, up_grad, upbias_grad, downbias_grad, gm1, gm2 = wgrad_call(n, cc, acts, ghs, cot_rows, arrived, ub, dx)

    gmid, gatt, pg_own, pg_oth, small, z0 = middle_back_call(
        n, cc, tcol, (gm0, gm1, gm2), middle, cotangent, vec, proj_weight, proj_oth, att, y)
    input_grad, small, sums, z1, z2 = back_call(
        n, cc, head_rows, probs, gatt, att, tokens, norm, qkv_weight, qkv_oth, gmid, vec, small, pg_own, pg_oth, y)
    output, qkv_grad, proj_grad, input_grad, down_grad, up_grad = result_call(
        tcol, (z0, z1, z2), middle, sums, input_grad, down_grad, up_grad)
    return (
        output, input_grad, qkv_grad.reshape(qkv_weight.shape), proj_grad, small[4], small[0], small[1], small[2], small[3],
        up_grad[None], upbias_grad, down_grad[None], downbias_grad,
    )


def solution(mesh):
    token = P(("dp", "expert"), None)
    in_specs = (
        token, token, token, token, P(None, None, "dp"), P("dp", None), P(), P(), P(), P(), P(),
        P("expert", "dp", None), P("expert", "dp"), P("expert", "dp", None), P("expert", None),
    )
    out_specs = (
        token, token, P(None, None, "dp"), P("dp", None), P(), P(), P(), P(), P(),
        P("expert", "dp", None), P("expert", "dp"), P("expert", "dp", None), P("expert", None),
    )
    return jax.shard_map(on_device, mesh=mesh, in_specs=in_specs, out_specs=out_specs, check_vma=False)
```

```python
import functools

import jax
import jax.numpy as jnp
from jax import lax
from jax.experimental import pallas as pl
from jax.experimental.pallas import tpu as pltpu
from jax.sharding import PartitionSpec as P

HEAD_DIM = 64
SEQ = 1024
DOC_MAX = 512
EPS = 1e-05
QB = 256
CHUNKS = 3
BF = jnp.bfloat16
F32 = jnp.float32
MESH = pl.DeviceIdType.MESH
VMEM_LIMIT = 60 * 1024 * 1024

BLOCKS = SEQ // QB
START = [max(0, i * QB - DOC_MAX) for i in range(BLOCKS)]
WIDTH = [(i + 1) * QB - START[i] for i in range(BLOCKS)]
OFFSET = [sum(WIDTH[:i]) for i in range(BLOCKS)]
BAND = sum(WIDTH)


def dot(a, b):
    return jnp.dot(a, b, preferred_element_type=F32)


def dot_nt(a, b):
    return lax.dot_general(a, b, (((1,), (1,)), ((), ())), preferred_element_type=F32)


def dot_tn(a, b):
    return lax.dot_general(a, b, (((0,), (0,)), ((), ())), preferred_element_type=F32)


def params(**kw):
    return pltpu.CompilerParams(vmem_limit_bytes=VMEM_LIMIT, **kw)


def cost(flops, nbytes, trans=0):
    return pl.CostEstimate(flops=int(flops), bytes_accessed=int(nbytes), transcendentals=int(trans))


ANY = pl.BlockSpec(memory_space=pl.ANY)


def whole(shape):
    return pl.BlockSpec(shape, lambda *_: (0,) * len(shape))


def block_of(index, size):
    return pl.ds(pl.multiple_of(index * size, size), size)


class Route:
    def __init__(self, n, src, dst, send, recv, local):
        self.n, self.src, self.dst = n, src, dst
        self.send, self.recv, self.local = send, recv, local

    def remote(self):
        me = lax.axis_index("expert")
        for d in range(1, self.n):
            there = lax.rem(me + d, self.n)
            yield pltpu.make_async_remote_copy(
                self.src(there), self.dst(me), self.send.at[d], self.recv.at[d],
                device_id={"expert": there}, device_id_type=MESH,
            )

    def own(self):
        me = lax.axis_index("expert")
        return pltpu.make_async_copy(self.src(me), self.dst(me), self.local)

    def start(self):
        for c in self.remote():
            c.start()
        self.own().start()

    def wait(self):
        self.own().wait()
        for c in self.remote():
            c.wait()


def route_sems(n, count):
    return [
        pltpu.SemaphoreType.DMA((count, n)),
        pltpu.SemaphoreType.DMA((count, n)),
        pltpu.SemaphoreType.DMA((count,)),
    ]


def greet(n, partner):
    me = lax.axis_index("expert")
    barrier = pltpu.get_barrier_semaphore()
    for d in range(1, n):
        pl.semaphore_signal(
            barrier, inc=1, device_id={"expert": lax.rem(me + d, n)}, device_id_type=MESH
        )
    if partner:
        pl.semaphore_signal(barrier, inc=1, device_id={"dp": 1 - lax.axis_index("dp")}, device_id_type=MESH)
    pl.semaphore_wait(barrier, n if partner else n - 1)


def to_partner(src, dst, send, recv):
    return pltpu.make_async_remote_copy(
        src, dst, send, recv, device_id={"dp": 1 - lax.axis_index("dp")}, device_id_type=MESH
    )


def unit_of(values):
    centre = values - jnp.mean(values, axis=-1, keepdims=True)
    inverse = lax.rsqrt(jnp.mean(centre * centre, axis=-1, keepdims=True) + EPS)
    return centre * inverse, inverse


def lane_pick(width, first):
    lanes = lax.broadcasted_iota(jnp.int32, (1, width), 1)
    return (lanes < HEAD_DIM) if first else (lanes >= HEAD_DIM)


PRE_GAIN, PRE_SHIFT, PROJ_BIAS, MID_GAIN, MID_SHIFT = range(5)


def front_kernel(
    n, cc, pairs, ids_ref, cot_ref, x_ref, seg_ref, vec_ref, w_ref, w_any, p_ref, p_any,
    tcol_ref, norm_t, hr_ref, att_ref, att_t, prob_ref, mid_ref, slot_ref, arr_ref, wo_out, po_out,
    row_s, cs_s, norm_s, hr_s, wo_s, po_s, bias_s, low_s, send, recv, local, dsend, drecv, dlocal,
):
    step = pl.program_id(0)
    tokens, width = x_ref.shape
    half = p_ref.shape[0]
    rows = n * cc
    first_pair = 7
    routes = [
        Route(
            n, lambda e, c=c: cs_s.at[block_of(c * n + e, cc)], lambda d, c=c: arr_ref.at[c, block_of(d, cc)],
            send.at[c], recv.at[c], local.at[c],
        )
        for c in range(CHUNKS)
    ]

    def swaps():
        return [
            to_partner(w_any, wo_s, dsend.at[0], drecv.at[0]),
            to_partner(p_any, po_s, dsend.at[1], drecv.at[1]),
        ]

    def keeps():
        return [
            pltpu.make_async_copy(wo_s, wo_out, dlocal.at[0]),
            pltpu.make_async_copy(po_s, po_out, dlocal.at[1]),
        ]

    @pl.when(step == 0)
    def _():
        greet(n, True)
        for c in swaps():
            c.start()
        ids = jnp.transpose(jnp.broadcast_to(ids_ref[...].astype(F32), (128, tokens)))
        hot = (ids == lax.broadcasted_iota(jnp.int32, (tokens, 128), 1).astype(F32)).astype(F32)
        low_hot = hot.astype(BF)
        place = []
        for b in range(tokens // 256):
            span = (b + 1) * 256
            lower = (
                lax.broadcasted_iota(jnp.int32, (256, span), 0) + b * 256
                >= lax.broadcasted_iota(jnp.int32, (256, span), 1)
            ).astype(F32).astype(BF)
            counts = dot(lower, low_hot[0:span])
            rank = jnp.sum(counts * hot[b * 256:span], axis=1, keepdims=True) - 1.0
            chunk = jnp.floor((rank + 0.5) * (1.0 / cc))
            place.append(chunk * rows + ids[b * 256:span] * cc + (rank - chunk * cc))
        place = jnp.concatenate(place, axis=0)
        tcol_ref[...] = place.astype(jnp.int32)
        row_s[...] = jnp.transpose(place)[0:8, :].astype(jnp.int32)

        def fill(b, _):
            hot = (
                lax.broadcasted_iota(jnp.int32, (256, tokens), 0) + b * 256 == row_s[0:1, :]
            ).astype(F32).astype(BF)
            cs_s[block_of(b, 256), :] = dot(hot, cot_ref[...]).astype(BF)
            return 0

        lax.fori_loop(0, CHUNKS * rows // 256, fill, 0)
        for r in routes:
            r.start()

        gain, shift = vec_ref[PRE_GAIN:PRE_GAIN + 1, :], vec_ref[PRE_SHIFT:PRE_SHIFT + 1, :]

        def body(b, _):
            at = block_of(b, 128)
            unit, _ = unit_of(x_ref[at, :].astype(F32))
            low = (unit * gain + shift).astype(BF)
            norm_s[at, :] = low
            norm_t[:, at] = jnp.transpose(low)
            return 0

        lax.fori_loop(0, tokens // 128, body, 0)

    @pl.when((step >= 1) & (step <= 3))
    def _():
        out = dot(norm_s[...], w_ref[0]).astype(BF)
        hr_ref[0] = out
        hr_s[step - 1] = out

    @pl.when(step == 4)
    def _():
        for c in swaps():
            c.wait()
        for c in keeps():
            c.start()

    @pl.when((step >= 4) & (step <= 6))
    def _():
        out = dot(norm_s[...], wo_s[step - 4]).astype(BF)
        hr_ref[0] = out
        hr_s[step - 1] = out

    @pl.when(step == first_pair)
    def _():
        seg = seg_ref[...].astype(F32)
        seg_col = jnp.transpose(jnp.broadcast_to(seg, (128, tokens)))
        for i in range(BLOCKS):
            w, s = WIDTH[i], START[i]
            at_row = lax.broadcasted_iota(jnp.int32, (QB, w), 0) + i * QB
            at_key = lax.broadcasted_iota(jnp.int32, (QB, w), 1) + s
            same = seg_col[i * QB:(i + 1) * QB, 0:1] == seg[:, s:s + w]
            bias_s[:, OFFSET[i]:OFFSET[i] + w] = jnp.where(same & (at_key <= at_row), 0.0, -1e30)

    @pl.when((step >= first_pair) & (step < first_pair + pairs))
    def _():
        pair = step - first_pair
        per = half // 128
        side, lanes = lax.div(pair, per), block_of(lax.rem(pair, per), 128)
        query = hr_s[3 * side, :, lanes] * BF(HEAD_DIM ** -0.5)
        for i in range(BLOCKS):
            w, s = WIDTH[i], START[i]
            keys, values = hr_s[3 * side + 1, s:s + w, lanes], hr_s[3 * side + 2, s:s + w, lanes]
            bias = bias_s[:, OFFSET[i]:OFFSET[i] + w]
            parts = []
            for j in range(2):
                q = jnp.where(lane_pick(128, j == 0), query[i * QB:(i + 1) * QB], BF(0))
                scores = dot_nt(q, keys) + bias
                top = jnp.max(scores, axis=-1, keepdims=True)
                weights = jnp.exp(scores - top)
                probs = (weights * (1.0 / jnp.sum(weights, axis=-1, keepdims=True))).astype(BF)
                prob_ref[j, :, OFFSET[i]:OFFSET[i] + w] = probs
                parts.append(dot(probs, values))
            both = jnp.where(lane_pick(128, True), parts[0], parts[1])
            both = both.astype(BF)
            att_ref[i * QB:(i + 1) * QB, block_of(pair, 128)] = both
            att_t[block_of(pair, 128), i * QB:(i + 1) * QB] = jnp.transpose(both)

    @pl.when(step == first_pair + pairs)
    def _():
        pbias = vec_ref[PROJ_BIAS:PROJ_BIAS + 1, :]
        gain, shift = vec_ref[MID_GAIN:MID_GAIN + 1, :], vec_ref[MID_SHIFT:MID_SHIFT + 1, :]

        def body(b, _):
            at = block_of(b, 128)
            branch = dot(att_ref[at, 0:half], p_ref[...]) + dot(att_ref[at, half:2 * half], po_s[...])
            middle = x_ref[at, :].astype(F32) + branch + pbias
            mid_ref[at, :] = middle
            unit, _ = unit_of(middle)
            low_s[at, :] = (unit * gain + shift).astype(BF)
            return 0

        lax.fori_loop(0, tokens // 128, body, 0)

        def fill(b, _):
            hot = (
                lax.broadcasted_iota(jnp.int32, (256, tokens), 0) + b * 256 == row_s[0:1, :]
            ).astype(F32).astype(BF)
            slot_ref[block_of(b, 256), :] = dot(hot, low_s[...]).astype(BF)
            return 0

        lax.fori_loop(0, CHUNKS * rows // 256, fill, 0)
        for c in keeps():
            c.wait()
        for r in routes:
            r.wait()


def front_call(n, cc, ids, cot, x, seg, vec, qkv, proj):
    tokens, width = x.shape
    half = proj.shape[0]
    pairs = width // 128
    rows = n * cc
    dma = pltpu.SemaphoreType.DMA
    sds = jax.ShapeDtypeStruct

    def pair_of(i):
        return jnp.clip(i - 7, 0, pairs - 1)

    return pl.pallas_call(
        functools.partial(front_kernel, n, cc, pairs),
        grid=(8 + pairs,),
        in_specs=[
            whole((1, tokens)), whole((tokens, width)), whole((tokens, width)), whole((1, tokens)),
            whole(vec.shape),
            pl.BlockSpec((1, width, half), lambda i: (jnp.clip(i - 1, 0, 2), 0, 0)), ANY,
            whole((half, width)), ANY,
        ],
        out_specs=[
            whole((tokens, 128)), whole((width, tokens)),
            pl.BlockSpec((1, tokens, half), lambda i: (jnp.clip(i - 1, 0, 5), 0, 0)),
            whole((tokens, width)), whole((width, tokens)), pl.BlockSpec((2, QB, BAND), lambda i: (pair_of(i), 0, 0)),
            whole((tokens, width)), whole((CHUNKS * rows, width)), ANY, ANY, ANY,
        ],
        out_shape=[
            sds((tokens, 128), jnp.int32), sds((width, tokens), BF), sds((6, tokens, half), BF),
            sds((tokens, width), BF), sds((width, tokens), BF), sds((2 * pairs, QB, BAND), BF), sds((tokens, width), F32),
            sds((CHUNKS * rows, width), BF), sds((CHUNKS, rows, width), BF), sds(qkv.shape, BF), sds(proj.shape, BF),
        ],
        scratch_shapes=[
            pltpu.VMEM((8, tokens), jnp.int32), pltpu.VMEM((CHUNKS * rows, width), BF),
            pltpu.VMEM((tokens, width), BF), pltpu.VMEM((6, tokens, half), BF), pltpu.VMEM(qkv.shape, BF),
            pltpu.VMEM(proj.shape, BF), pltpu.VMEM((QB, BAND), F32), pltpu.VMEM((tokens, width), BF),
            *route_sems(n, CHUNKS), dma((2,)), dma((2,)), dma((2,)),
        ],
        compiler_params=params(collective_id=1, has_side_effects=True),
        cost_estimate=cost(3e10, 6e7),
        name="front",
    )(ids, cot, x, seg, vec, qkv, qkv, proj, proj)


GELU_C = 0.7978845608028654
GELU_A = 0.044715
TILE = 512


def expert_kernel(
    n, cc, own_tiles, mid_ref, c_ref, uo_ref, ut_ref, do_ref, dt_ref, bo_ref, bt_ref, db_ref,
    act_ref, gh_ref, ub_ref, y_ref, dx_ref, x_out, back_out,
    x_s, g_s, y_s, dx_s, dxb_s, send, recv, local, xsem,
):
    step = pl.program_id(0)
    tiles = 2 * own_tiles
    phase, tile = lax.div(step, tiles), lax.rem(step, tiles)
    rows = n * cc
    ins = [
        Route(
            n, lambda e, c=c: mid_ref.at[block_of(c * n + e, cc)], lambda d, c=c: x_s.at[c, block_of(d, cc)],
            send.at[c], recv.at[c], local.at[c],
        )
        for c in range(CHUNKS)
    ]
    back = Route(
        n, lambda e: dxb_s.at[block_of(e, cc)], lambda d: back_out.at[block_of(d, cc)],
        send.at[CHUNKS], recv.at[CHUNKS], local.at[CHUNKS],
    )

    def keep(c):
        return pltpu.make_async_copy(x_s.at[c], x_out.at[c], xsem.at[c])

    @pl.when(step == 0)
    def _():
        greet(n, False)
        ins[0].start()
        ub_ref[...] = jnp.zeros_like(ub_ref)

    for c in range(CHUNKS):
        @pl.when(step == (c + 1) * tiles)
        def _():
            ins[c].wait()
            (ins[c + 1] if c + 1 < CHUNKS else back).start()
            keep(c).start()

    lanes = block_of(tile, TILE)

    def early(down_ref):
        for c in range(CHUNKS):
            g_s[c, :, lanes] = dot_nt(c_ref[c], down_ref[...]).astype(BF)

    def late(c, up_ref, down_ref, b_ref):
        up, down = up_ref[...], down_ref[...]
        h = dot_nt(x_s[c], up) + b_ref[...].astype(F32)
        sq = h * h
        t = jnp.tanh(GELU_C * (h + GELU_A * (sq * h)))
        act = ((0.5 * h) * (1.0 + t)).astype(BF)
        act_ref[0] = act
        slope = 0.5 * (1.0 + t) + (0.5 * h) * ((1.0 - t * t) * (GELU_C * (1.0 + (3.0 * GELU_A) * sq)))
        gh = (g_s[c, :, lanes].astype(F32) * slope).astype(BF)
        gh_ref[0] = gh
        ub_ref[0:1, lanes] += jnp.sum(gh.astype(F32), axis=0, keepdims=True)
        y_s[...] += dot(act, down)
        dx_s[...] += dot(gh, up)

    @pl.when((phase >= 1) & (tile == 0))
    def _():
        y_s[...] = jnp.broadcast_to(db_ref[...].astype(F32), y_s.shape)
        dx_s[...] = jnp.zeros_like(dx_s)

    @pl.when((phase == 0) & (tile < own_tiles))
    def _():
        early(do_ref)

    @pl.when((phase == 0) & (tile >= own_tiles))
    def _():
        early(dt_ref)

    @pl.when((phase >= 1) & (tile < own_tiles))
    def _():
        late(phase - 1, uo_ref, do_ref, bo_ref)

    @pl.when((phase >= 1) & (tile >= own_tiles))
    def _():
        late(phase - 1, ut_ref, dt_ref, bt_ref)

    @pl.when((phase >= 1) & (tile == tiles - 1))
    def _():
        y_ref[0] = y_s[...].astype(BF)
        dx_ref[0] = dx_s[...].astype(BF)

    @pl.when((phase == 1) & (tile == tiles - 1))
    def _():
        dxb_s[...] = dx_s[...].astype(BF)

    @pl.when(step == (CHUNKS + 1) * tiles - 1)
    def _():
        for c in range(CHUNKS):
            keep(c).wait()
        back.wait()


def expert_call(n, cc, mid_slots, cot, up, down, bias, down_bias):
    up_own, up_oth = up
    down_own, down_oth = down
    b_own, b_oth = bias
    rows = n * cc
    hid, width = up_own.shape
    own_tiles = hid // TILE
    tiles = 2 * own_tiles
    sds = jax.ShapeDtypeStruct

    def first(i):
        return jnp.minimum(i % tiles, own_tiles - 1)

    def second(i):
        return jnp.maximum(i % tiles - own_tiles, 0)

    def up_first(i):
        return jnp.where(i < tiles, 0, first(i))

    def up_second(i):
        return jnp.where(i < tiles, 0, second(i))

    def chunk(i):
        return jnp.maximum(i // tiles - 1, 0)

    def column(i):
        return jnp.where(i < tiles, 0, i % tiles)

    col = pl.BlockSpec((1, rows, TILE), lambda i: (chunk(i), 0, column(i)))
    per_chunk = pl.BlockSpec((1, rows, width), lambda i: (chunk(i), 0, 0))
    return pl.pallas_call(
        functools.partial(expert_kernel, n, cc, own_tiles),
        grid=((CHUNKS + 1) * tiles,),
        in_specs=[
            ANY, whole(cot.shape),
            pl.BlockSpec((TILE, width), lambda i: (up_first(i), 0)),
            pl.BlockSpec((TILE, width), lambda i: (up_second(i), 0)),
            pl.BlockSpec((TILE, width), lambda i: (first(i), 0)),
            pl.BlockSpec((TILE, width), lambda i: (second(i), 0)),
            pl.BlockSpec((1, TILE), lambda i: (0, first(i))),
            pl.BlockSpec((1, TILE), lambda i: (0, second(i))),
            whole((1, width)),
        ],
        out_specs=[col, col, whole((8, 2 * hid)), per_chunk, per_chunk, ANY, ANY],
        out_shape=[
            sds((CHUNKS, rows, 2 * hid), BF), sds((CHUNKS, rows, 2 * hid), BF), sds((8, 2 * hid), F32),
            sds((CHUNKS, rows, width), BF), sds((CHUNKS, rows, width), BF), sds((CHUNKS, rows, width), BF),
            sds((rows, width), BF),
        ],
        scratch_shapes=[
            pltpu.VMEM((CHUNKS, rows, width), BF), pltpu.VMEM((CHUNKS, rows, 2 * hid), BF),
            pltpu.VMEM((rows, width), F32), pltpu.VMEM((rows, width), F32), pltpu.VMEM((rows, width), BF),
            *route_sems(n, CHUNKS + 1), pltpu.SemaphoreType.DMA((CHUNKS,)),
        ],
        compiler_params=params(collective_id=2, has_side_effects=True),
        cost_estimate=cost(5.2e10, 8e7),
        name="experts",
    )(mid_slots, cot, up_own, up_oth, down_own, down_oth, b_own, b_oth, down_bias)


def wgrad_kernel(
    n, cc, tiles, a_ref, g_ref, c_ref, x_ref, ub_ref, dx_ref,
    do_ref, up_ref, ubg_ref, cbg_ref, back1, back2,
    out_s, in_s, small_s, got_s, send, recv, local, dsend, drecv, ssend, srecv,
):
    step = pl.program_id(0)
    hid = ubg_ref.shape[1]
    routes = [
        Route(
            n, lambda e, c=c: dx_ref.at[c, block_of(e, cc)], lambda d, dst=dst: dst.at[block_of(d, cc)],
            send.at[k], recv.at[k], local.at[k],
        )
        for k, (c, dst) in enumerate(((1, back1), (2, back2)))
    ]

    def swap(k):
        return to_partner(out_s.at[k], in_s.at[k], dsend.at[k], drecv.at[k])

    small = to_partner(small_s, got_s, ssend, srecv)

    @pl.when(step == 0)
    def _():
        greet(n, True)
        for r in routes:
            r.start()
        total = jnp.zeros((1, c_ref.shape[2]), F32)
        for c in range(CHUNKS):
            total = total + jnp.sum(c_ref[c].astype(F32), axis=0, keepdims=True)
        small_s[...] = jnp.zeros_like(small_s)
        small_s[0:1, 0:hid] = ub_ref[0:1, hid:2 * hid]
        small_s[0:1, hid:hid + total.shape[1]] = total
        small.start()

    @pl.when(step == 2 * tiles)
    def _():
        small.wait()
        ubg_ref[...] = ub_ref[0:1, 0:hid] + got_s[0:1, 0:hid]
        cbg_ref[...] = small_s[0:1, hid:] + got_s[0:1, hid:]

    def product(left, right):
        total = dot_tn(left[0], right[0])
        for c in range(1, CHUNKS):
            total = total + dot_tn(left[c], right[c])
        return total

    for k in range(2 * tiles):
        @pl.when(step == k)
        def _():
            left, right = (a_ref, c_ref) if k < tiles else (g_ref, x_ref)
            out_s[k] = product(left, right).astype(BF)
            swap(k).start()

        @pl.when(step == 2 * tiles + k)
        def _():
            left, right, out = (a_ref, c_ref, do_ref) if k < tiles else (g_ref, x_ref, up_ref)
            total = product(left, right)
            swap(k).wait()
            out[...] = (total + in_s[k].astype(F32)).astype(BF)

    @pl.when(step == 4 * tiles - 1)
    def _():
        for r in routes:
            r.wait()


def wgrad_call(n, cc, acts, ghs, cot, rows_in, ub, dx):
    _, rows, width = cot.shape
    hid = acts.shape[2] // 2
    tiles = hid // TILE
    dma = pltpu.SemaphoreType.DMA
    sds = jax.ShapeDtypeStruct

    def first(i):
        return jnp.minimum(i % (2 * tiles), tiles - 1)

    def second(i):
        return jnp.maximum(i % (2 * tiles) - tiles, 0)

    def other(i):
        return jnp.where(i < 2 * tiles, tiles, 0)

    a_spec = pl.BlockSpec((CHUNKS, rows, TILE), lambda i: (0, 0, other(i) + first(i)))
    g_spec = pl.BlockSpec((CHUNKS, rows, TILE), lambda i: (0, 0, other(i) + second(i)))

    def late(i):
        return jnp.where(i < 2 * tiles, 0, 1)

    d_spec = pl.BlockSpec((TILE, width), lambda i: (late(i) * first(i), 0))
    u_spec = pl.BlockSpec((TILE, width), lambda i: (late(i) * second(i), 0))
    return pl.pallas_call(
        functools.partial(wgrad_kernel, n, cc, tiles),
        grid=(4 * tiles,),
        in_specs=[a_spec, g_spec, whole(cot.shape), whole(rows_in.shape), whole(ub.shape), ANY],
        out_specs=[d_spec, u_spec, whole((1, hid)), whole((1, width)), ANY, ANY],
        out_shape=[
            sds((hid, width), BF), sds((hid, width), BF), sds((1, hid), F32), sds((1, width), F32),
            sds((rows, width), BF), sds((rows, width), BF),
        ],
        scratch_shapes=[
            pltpu.VMEM((2 * tiles, TILE, width), BF), pltpu.VMEM((2 * tiles, TILE, width), BF),
            pltpu.VMEM((8, hid + width), F32), pltpu.VMEM((8, hid + width), F32),
            *route_sems(n, 2), dma((2 * tiles,)), dma((2 * tiles,)), dma, dma,
        ],
        compiler_params=params(collective_id=3, has_side_effects=True),
        cost_estimate=cost(2.6e10, 8e7),
        name="weight_grads",
    )(acts, ghs, cot, rows_in, ub, dx)


def gather_rows(tcol, parts):
    total = None
    for c, part in enumerate(parts):
        rows = part.shape[0]
        hot = (
            lax.broadcasted_iota(jnp.int32, (tcol.shape[0], rows), 1) + c * rows == tcol[:, 0:1]
        ).astype(F32).astype(BF)
        term = dot(hot, part)
        total = term if total is None else total + term
    return total


def norm_back(grad, unit, inverse, gain):
    scaled = grad * gain
    inner = jnp.mean(scaled, axis=-1, keepdims=True)
    along = jnp.mean(scaled * unit, axis=-1, keepdims=True)
    return inverse * (scaled - inner - unit * along)


def middle_back_kernel(
    n, cc, blocks, tcol_ref, g0, g1, g2, mid_ref, cot_ref, vec_ref, own_ref, oth_ref, att_t, y_src,
    gmid_ref, gatt_ref, pg_own, pg_oth, small_ref, y_dst, gb_s, send, recv, local,
):
    route = Route(
        n, lambda e: y_src.at[0, block_of(e, cc)], lambda d: y_dst.at[block_of(d, cc)],
        send.at[0], recv.at[0], local.at[0],
    )
    step = pl.program_id(0)
    half = own_ref.shape[0]
    tb = mid_ref.shape[0]

    @pl.when(step == 0)
    def _():
        greet(n, False)
        route.start()
        small_ref[...] = jnp.zeros_like(small_ref)

    grad = gather_rows(tcol_ref[...], (g0[...], g1[...], g2[...]))
    grad = grad.astype(BF).astype(F32)
    unit, inverse = unit_of(mid_ref[...])
    gmid = cot_ref[...].astype(F32) + norm_back(grad, unit, inverse, vec_ref[MID_GAIN:MID_GAIN + 1, :])
    gmid_ref[...] = gmid
    gb = gmid.astype(BF)
    gb_s[block_of(step, tb), :] = gb
    small_ref[2:3, :] += jnp.sum(grad * unit, axis=0, keepdims=True)
    small_ref[3:4, :] += jnp.sum(grad, axis=0, keepdims=True)
    small_ref[4:5, :] += jnp.sum(gb.astype(F32), axis=0, keepdims=True)
    gatt_ref[:, 0:half] = dot_nt(gb, own_ref[...]).astype(BF)
    gatt_ref[:, half:2 * half] = dot_nt(gb, oth_ref[...]).astype(BF)

    @pl.when(step == blocks - 1)
    def _():
        pg_own[...] = dot(att_t[0:half, :], gb_s[...]).astype(BF)
        pg_oth[...] = dot(att_t[half:2 * half, :], gb_s[...]).astype(BF)
        route.wait()


def middle_back_call(n, cc, tcol, grads, middle, cot, vec, proj_own, proj_oth, att_t, y):
    tokens, width = middle.shape
    half = proj_own.shape[0]
    tb = 256
    rows = grads[0].shape[0]
    block = pl.BlockSpec((tb, width), lambda i: (i, 0))
    sds = jax.ShapeDtypeStruct
    return pl.pallas_call(
        functools.partial(middle_back_kernel, n, cc, tokens // tb),
        grid=(tokens // tb,),
        in_specs=[
            pl.BlockSpec((tb, 128), lambda i: (i, 0)), *[whole((rows, width))] * 3, block, block,
            whole(vec.shape), whole((half, width)), whole((half, width)), whole((tokens, width)), ANY,
        ],
        out_specs=[block, block, whole((half, width)), whole((half, width)), whole((8, width)), ANY],
        out_shape=[
            sds((tokens, width), F32), sds((tokens, width), BF), sds((half, width), BF), sds((half, width), BF),
            sds((8, width), F32), sds((rows, width), BF),
        ],
        scratch_shapes=[pltpu.VMEM((tokens, width), BF), *route_sems(n, 1)],
        compiler_params=params(collective_id=4, has_side_effects=True),
        cost_estimate=cost(1.2e10, 3e7),
        name="middle_back",
    )(tcol, *grads, middle, cot, vec, proj_own, proj_oth, att_t, y)


class Part:
    def __init__(self, index, base, length, order, me, refs, sems):
        self.index, self.base, self.total, self.order, self.me = index, base, length, order, me
        self.acc, self.rcv, self.res = refs
        self.rs_send, self.rs_recv, self.ag_send, self.ag_recv = sems
        self.stages, self.stage = len(order), 0
        self.step = length >> len(order)

    def upper(self, s):
        return lax.rem(lax.div(self.me, 1 << self.order[s]), 2)

    def rows(self, start, length):
        return pl.ds(pl.multiple_of(start, 16), length)

    def start(self, s):
        at = self.base
        for k in range(s):
            at = at + self.upper(k) * (self.total >> (k + 1))
        return at

    def slot(self, s):
        return self.base + self.total - (self.total >> s)

    def copy(self):
        inward = self.stage < self.stages
        s = self.stage if inward else 2 * self.stages - 1 - self.stage
        bit = 1 << self.order[s]
        peer = {"expert": self.me + bit - 2 * bit * self.upper(s)}
        if inward:
            half = self.total >> (s + 1)
            away = self.start(s) + (1 - self.upper(s)) * half
            src, dst = self.acc.at[self.rows(away, half)], self.rcv.at[pl.ds(self.slot(s), half)]
            send, recv = self.rs_send, self.rs_recv
        else:
            src = dst = self.res.at[self.rows(self.start(s + 1), self.total >> (s + 1))]
            send, recv = self.ag_send, self.ag_recv
        return pltpu.make_async_remote_copy(
            src, dst, send.at[self.index, s], recv.at[self.index, s], device_id=peer, device_id_type=MESH
        )

    def begin(self):
        self.copy().start()

    def advance(self):
        self.copy().wait()
        s = self.stage
        if s < self.stages:
            keep, slot, step = self.start(s + 1), self.slot(s), self.step
            into = self.res if s == self.stages - 1 else self.acc

            def add(b, _):
                at = self.rows(keep + b * step, step)
                into[at, :] = (
                    self.acc[at, :].astype(F32) + self.rcv[self.rows(slot + b * step, step), :].astype(F32)
                ).astype(BF)
                return 0

            lax.fori_loop(0, (self.total >> (s + 1)) // step, add, 0)
        self.stage += 1
        if self.stage < 2 * self.stages:
            self.copy().start()


def back_kernel(
    n, cc, groups, q_ref, k_ref, v_ref, prob_ref, do_ref, o_ref, x_ref, norm_t, own_ref, oth_ref,
    vec_ref, small_ref, pg_own, pg_oth, gmid_any, y_src,
    xg_ref, small_out, sum_q, sum_p, z1, z2,
    dk_s, dv_s, gh_s, gnp_s, acc, rcv, res, p_acc, p_rcv, p_res, got, pgot, snd, mine_s, small_got,
    send, recv, local, dsend, drecv, rs_send, rs_recv, ag_send, ag_recv, sm_send, sm_recv, out_sem,
):
    step = pl.program_id(0)
    tokens, width = x_ref.shape
    half = own_ref.shape[2]
    scale = HEAD_DIM ** -0.5
    last = 3 * groups
    kind, group = lax.rem(step, 3), lax.div(step, 3)
    me = lax.axis_index("expert")
    stages = n.bit_length() - 1
    routes = [
        Route(
            n, lambda e, c=c: y_src.at[c, block_of(e, cc)], lambda d, z=z: z.at[block_of(d, cc)],
            send.at[c - 1], recv.at[c - 1], local.at[c - 1],
        )
        for c, z in ((1, z1), (2, z2))
    ]

    split = 2 if width >= 32 * n else 1
    size = width // split
    sems = (rs_send, rs_recv, ag_send, ag_recv)
    order = list(range(stages))
    swapped = [1, 0, *order[2:]]

    def parts_of(first, at, refs):
        return [
            Part(first + i, at * width + i * size, size, order if i % 2 == 0 else swapped, me, refs, sems)
            for i in range(split)
        ]

    head_parts = [parts_of(k * split, k, (acc, rcv, res)) for k in range(groups)]
    proj_parts = parts_of(groups * split, 0, (p_acc, p_rcv, p_res))

    def dp_swap(k):
        src, dst = (snd.at[k], got.at[k]) if k < groups else (pg_oth, pgot)
        return to_partner(src, dst, dsend.at[k], drecv.at[k])

    def bring_to(parts, goal):
        while parts[0].stage < min(goal, 2 * stages):
            for p in parts:
                p.advance()

    def seed(k):
        return pltpu.make_async_copy(gmid_any, xg_ref, out_sem.at[2])

    @pl.when(step == 0)
    def _():
        greet(n, True)
        dp_swap(groups).start()
        for r in routes:
            r.start()
        seed(0).start()

    @pl.when((kind < 2) & (step < last))
    def _():
        side, lanes = 1 - kind, block_of(group, 128)
        dk_s[...] = jnp.zeros_like(dk_s)
        dv_s[...] = jnp.zeros_like(dv_s)
        for i in range(BLOCKS):
            w, s = WIDTH[i], START[i]
            at = slice(i * QB, (i + 1) * QB)
            keys, values = k_ref[0, s:s + w, :], v_ref[0, s:s + w, :]
            go = do_ref[at, :]
            prod = go.astype(F32) * o_ref[at, :].astype(F32)
            query = q_ref[0, at, :]
            parts = []
            for j in range(2):
                pick = lane_pick(128, j == 0)
                go_j = jnp.where(pick, go, BF(0))
                q_j = jnp.where(pick, query, BF(0))
                inner = jnp.sum(jnp.where(pick, prod, 0.0), axis=-1, keepdims=True)
                probs = prob_ref[j, :, OFFSET[i]:OFFSET[i] + w]
                gp = dot_nt(go_j, values)
                gs = (probs.astype(F32) * (gp - inner)).astype(BF)
                parts.append(dot(gs, keys))
                dk_s[s:s + w, :] += dot_tn(gs, q_j)
                dv_s[s:s + w, :] += dot_tn(probs, go_j)
            gh_s[3 * side, at, lanes] = (jnp.where(lane_pick(128, True), parts[0], parts[1]) * scale).astype(BF)
        gh_s[3 * side + 1, :, lanes] = (dk_s[...] * scale).astype(BF)
        gh_s[3 * side + 2, :, lanes] = dv_s[...].astype(BF)

    for k in range(groups):
        @pl.when(step == 3 * k + 2)
        def _():
            at = slice(k * 128, (k + 1) * 128)
            for c in range(3):
                both = dot(norm_t[...], jnp.concatenate([gh_s[3 + c, :, at], gh_s[c, :, at]], axis=1))
                snd[k, :, c * 128:(c + 1) * 128] = both[:, 0:128].astype(BF)
                mine_s[:, c * 128:(c + 1) * 128] = both[:, 128:256]
            dp_swap(k).start()

        @pl.when(step == 3 * k + 3)
        def _():
            dp_swap(k).wait()
            acc[k * width:(k + 1) * width, :] = (mine_s[...] + got[k].astype(F32)).astype(BF)
            for p in head_parts[k]:
                p.begin()

    @pl.when(step == 1)
    def _():
        dp_swap(groups).wait()
        rows = pgot.shape[0]
        for b in range(width // rows):
            at = slice(b * rows, (b + 1) * rows)
            p_acc[at, :] = (pg_own[:, at].astype(F32) + pgot[:, at].astype(F32)).astype(BF)
        for p in proj_parts:
            p.begin()

    for t in range(3, last):
        @pl.when(step == t)
        def _():
            bring_to(proj_parts, sum(t >= m for m in (5, 7, 9, 11)))
            for k in range(groups):
                bring_to(head_parts[k], sum(t >= 3 * k + m for m in (7, 9, 11)))

    @pl.when(step == last)
    def _():
        def small_swap(k):
            if k == 0:
                peer = {"dp": 1 - lax.axis_index("dp")}
            else:
                bit = 1 << (k - 1)
                peer = {"expert": me + bit - 2 * bit * lax.rem(lax.div(me, bit), 2)}
            return pltpu.make_async_remote_copy(
                small_out, small_got.at[k], sm_send.at[k], sm_recv.at[k], device_id=peer, device_id_type=MESH
            )

        def turn():
            for some in [proj_parts, *head_parts]:
                for p in some:
                    if p.stage < 2 * stages:
                        p.advance()

        for c in range(3):
            if c:
                turn()
            term = dot_nt(gh_s[c], own_ref[c]) + dot_nt(gh_s[3 + c], oth_ref[c])
            if c:
                gnp_s[...] += term
            else:
                gnp_s[...] = term
        turn()
        seed(0).wait()
        small_out[...] = small_ref[...]

        def body(b, _):
            at = block_of(b, 128)
            grad = gnp_s[at, :]
            unit, inverse = unit_of(x_ref[at, :].astype(F32))
            xg_ref[at, :] = xg_ref[at, :] + norm_back(grad, unit, inverse, vec_ref[PRE_GAIN:PRE_GAIN + 1, :])
            small_out[0:1, :] += jnp.sum(grad * unit, axis=0, keepdims=True)
            small_out[1:2, :] += jnp.sum(grad, axis=0, keepdims=True)
            return 0

        lax.fori_loop(0, tokens // 128, body, 0)
        small = small_swap(0)
        small.start()
        for s in range(2 * stages - 2):
            turn()
            if s <= stages:
                small.wait()
                small_out[...] += small_got[s]
                if s < stages:
                    small = small_swap(s + 1)
                    small.start()
        outs = [
            pltpu.make_async_copy(res, sum_q, out_sem.at[0]),
            pltpu.make_async_copy(p_res, sum_p, out_sem.at[1]),
        ]
        for out in outs:
            out.start()
        for out in outs:
            out.wait()
        for r in routes:
            r.wait()


def back_call(n, cc, head_rows, probs, gatt, att, x, norm_t, own, oth, gmid, vec, small, pg_own, pg_oth, y):
    tokens, width = x.shape
    half = own.shape[2]
    groups = half // 128
    last = 3 * groups
    rows = n * cc
    stages = n.bit_length() - 1
    parts = (groups + 1) * (2 if width >= 32 * n else 1)
    sds, dma, once = jax.ShapeDtypeStruct, pltpu.SemaphoreType.DMA, pl.Buffered(1)

    def place(i):
        i = jnp.minimum(i, last - 1)
        return jnp.maximum(1 - i % 3, 0), i // 3

    def head(c):
        def index(i):
            side, k = place(i)
            return (3 * side + c, 0, k)

        return pl.BlockSpec((1, tokens, 128), index)

    def pair(i):
        side, k = place(i)
        return side * groups + k

    def fixed(shape):
        return pl.BlockSpec(shape, lambda *_: (0,) * len(shape), pipeline_mode=once)

    cols = pl.BlockSpec((tokens, 128), lambda i: (0, pair(i)))
    sums = pltpu.VMEM((groups * width, 384), BF)
    p_sums = pltpu.VMEM((width, half), BF)
    return pl.pallas_call(
        functools.partial(back_kernel, n, cc, groups),
        grid=(last + 1,),
        in_specs=[
            head(0), head(1), head(2), pl.BlockSpec((2, QB, BAND), lambda i: (pair(i), 0, 0)), cols, cols,
            fixed((tokens, width)), fixed((width, tokens)), fixed(own.shape), fixed(oth.shape),
            fixed(vec.shape), fixed(small.shape), fixed((half, width)), ANY, ANY, ANY,
        ],
        out_specs=[fixed((tokens, width)), fixed(small.shape), ANY, ANY, ANY, ANY],
        out_shape=[
            sds((tokens, width), F32), sds(small.shape, F32), sds((groups * width, 384), BF), sds((width, half), BF),
            sds((rows, width), BF), sds((rows, width), BF),
        ],
        scratch_shapes=[
            pltpu.VMEM((tokens, 128), F32), pltpu.VMEM((tokens, 128), F32), pltpu.VMEM((6, tokens, half), BF),
            pltpu.VMEM((tokens, width), F32), sums, sums, sums, p_sums, p_sums, p_sums,
            pltpu.VMEM((groups, width, 384), BF), pltpu.VMEM((half, width), BF),
            pltpu.VMEM((groups, width, 384), BF), pltpu.VMEM((width, 384), F32),
            pltpu.VMEM((1 + stages, *small.shape), F32),
            *route_sems(n, 2), dma((groups + 1,)), dma((groups + 1,)), dma((parts, stages)), dma((parts, stages)),
            dma((parts, stages)), dma((parts, stages)), dma((1 + stages,)), dma((1 + stages,)), dma((3,)),
        ],
        compiler_params=params(collective_id=5, has_side_effects=True),
        cost_estimate=cost(5.3e10, 9e7),
        name="back",
    )(
        head_rows, head_rows, head_rows, probs, gatt, att, x, norm_t, own, oth, vec, small, pg_own, pg_oth, gmid, y
    )


def result_kernel(tcol_ref, z0, z1, z2, mid_ref, sum_q, sum_p, xg_ref, wd_ref, wu_ref, out_ref, q_ref, p_ref, xo_ref, do_ref, uo_ref):
    rows = gather_rows(tcol_ref[...], (z0[...], z1[...], z2[...]))
    out_ref[...] = (mid_ref[...] + rows.astype(BF).astype(F32)).astype(BF)
    for c in range(3):
        for k in range(sum_q.shape[0]):
            q_ref[c, :, k * 128:(k + 1) * 128] = sum_q[k, :, c * 128:(c + 1) * 128].astype(F32)
    half = sum_p.shape[2]
    for b in range(sum_p.shape[0]):
        p_ref[:, b * half:(b + 1) * half] = sum_p[b].astype(F32)
    xo_ref[...] = xg_ref[...]
    do_ref[...] = wd_ref[...].astype(F32)
    uo_ref[...] = wu_ref[...].astype(F32)


def result_call(tcol, zs, middle, sum_q, sum_p, xg, wd, wu):
    tokens, width = middle.shape
    half = sum_p.shape[1]
    groups = half // 128
    hid = wd.shape[0]
    rows = zs[0].shape[0]
    steps = 8
    tb, qb, pb, wb = tokens // steps, width // steps, half // steps, hid // steps
    sds = jax.ShapeDtypeStruct
    sum_q = sum_q.reshape(groups, width, 384)
    sum_p = sum_p.reshape(width // half, half, half)

    def rows_of(size, cols):
        return pl.BlockSpec((size, cols), lambda i: (i, 0))

    return pl.pallas_call(
        result_kernel,
        grid=(steps,),
        in_specs=[
            rows_of(tb, 128), *[whole((rows, width))] * 3, rows_of(tb, width),
            pl.BlockSpec((groups, qb, 384), lambda i: (0, i, 0)),
            pl.BlockSpec((width // half, pb, half), lambda i: (0, i, 0)), rows_of(tb, width), rows_of(wb, width),
            rows_of(wb, width),
        ],
        out_specs=[
            rows_of(tb, width), pl.BlockSpec((3, qb, half), lambda i: (0, i, 0)), rows_of(pb, width),
            rows_of(tb, width), rows_of(wb, width), rows_of(wb, width),
        ],
        out_shape=[
            sds((tokens, width), BF), sds((3, width, half), F32), sds((half, width), F32), sds((tokens, width), F32),
            sds((hid, width), F32), sds((hid, width), F32),
        ],
        compiler_params=params(),
        cost_estimate=cost(6 * tokens * rows * width, 6e7),
        name="results",
    )(tcol, *zs, middle, sum_q, sum_p, xg, wd, wu)


def on_device(
    tokens, cotangent, segment_ids, expert_ids, qkv_weight, proj_weight, proj_bias, pre_gain, pre_shift,
    mid_gain, mid_shift, up_weight, up_bias, down_weight, down_bias,
):
    n = lax.axis_size("expert")
    count, width = tokens.shape
    cc = 3 * count // (2 * n) // CHUNKS

    def swap(v):
        return lax.ppermute(v, "dp", [(0, 1), (1, 0)])

    down_own, up_own = down_weight[0], up_weight[0]
    up, down = (up_own, swap(up_own)), (down_own, swap(down_own))
    bias = (up_bias, swap(up_bias))
    vec = jnp.stack([pre_gain, pre_shift, proj_bias, mid_gain, mid_shift]).astype(F32)

    tcol, norm_t, head_rows, att, att_t, probs, middle, mid_slots, cot_rows, qkv_oth, proj_oth = front_call(
        n, cc, expert_ids.reshape(1, count), cotangent, tokens, segment_ids, vec, qkv_weight, proj_weight)
    acts, ghs, ub, y, dx, arrived, gm0 = expert_call(n, cc, mid_slots, cot_rows, up, down, bias, down_bias)
    down_grad, up_grad, upbias_grad, downbias_grad, gm1, gm2 = wgrad_call(n, cc, acts, ghs, cot_rows, arrived, ub, dx)

    gmid, gatt, pg_own, pg_oth, small, z0 = middle_back_call(
        n, cc, tcol, (gm0, gm1, gm2), middle, cotangent, vec, proj_weight, proj_oth, att_t, y)
    input_grad, small, sum_q, sum_p, z1, z2 = back_call(
        n, cc, head_rows, probs, gatt, att, tokens, norm_t, qkv_weight, qkv_oth, gmid, vec, small, pg_own, pg_oth, y)
    output, qkv_grad, proj_grad, input_grad, down_grad, up_grad = result_call(
        tcol, (z0, z1, z2), middle, sum_q, sum_p, input_grad, down_grad, up_grad)
    return (
        output, input_grad, qkv_grad, proj_grad, small[4], small[0], small[1], small[2], small[3],
        up_grad[None], upbias_grad, down_grad[None], downbias_grad,
    )


def solution(mesh):
    token = P(("dp", "expert"), None)
    in_specs = (
        token, token, token, token, P(None, None, "dp"), P("dp", None), P(), P(), P(), P(), P(),
        P("expert", "dp", None), P("expert", "dp"), P("expert", "dp", None), P("expert", None),
    )
    out_specs = (
        token, token, P(None, None, "dp"), P("dp", None), P(), P(), P(), P(), P(),
        P("expert", "dp", None), P("expert", "dp"), P("expert", "dp", None), P("expert", None),
    )
    return jax.shard_map(on_device, mesh=mesh, in_specs=in_specs, out_specs=out_specs, check_vma=False)
```

```python
import functools

import jax
import jax.numpy as jnp
from jax import lax
from jax.experimental import pallas as pl
from jax.experimental.pallas import tpu as pltpu
from jax.sharding import PartitionSpec as P

HEAD_DIM = 64
SEQ = 1024
DOC_MAX = 512
EPS = 1e-05
QB = 256
CHUNKS = 3
BF = jnp.bfloat16
F32 = jnp.float32
MESH = pl.DeviceIdType.MESH
VMEM_LIMIT = 60 * 1024 * 1024

BLOCKS = SEQ // QB
START = [max(0, i * QB - DOC_MAX) for i in range(BLOCKS)]
WIDTH = [(i + 1) * QB - START[i] for i in range(BLOCKS)]
OFFSET = [sum(WIDTH[:i]) for i in range(BLOCKS)]
BAND = sum(WIDTH)


def dot(a, b):
    return jnp.dot(a, b, preferred_element_type=F32)


def dot_nt(a, b):
    return lax.dot_general(a, b, (((1,), (1,)), ((), ())), preferred_element_type=F32)


def dot_tn(a, b):
    return lax.dot_general(a, b, (((0,), (0,)), ((), ())), preferred_element_type=F32)


def params(**kw):
    return pltpu.CompilerParams(vmem_limit_bytes=VMEM_LIMIT, **kw)


def cost(flops, nbytes, trans=0):
    return pl.CostEstimate(flops=int(flops), bytes_accessed=int(nbytes), transcendentals=int(trans))


ANY = pl.BlockSpec(memory_space=pl.ANY)


def whole(shape):
    return pl.BlockSpec(shape, lambda *_: (0,) * len(shape))


def block_of(index, size):
    return pl.ds(pl.multiple_of(index * size, size), size)


class Route:
    def __init__(self, n, src, dst, send, recv, local):
        self.n, self.src, self.dst = n, src, dst
        self.send, self.recv, self.local = send, recv, local

    def remote(self):
        me = lax.axis_index("expert")
        for d in range(1, self.n):
            there = lax.rem(me + d, self.n)
            yield pltpu.make_async_remote_copy(
                self.src(there), self.dst(me), self.send.at[d], self.recv.at[d],
                device_id={"expert": there}, device_id_type=MESH,
            )

    def own(self):
        me = lax.axis_index("expert")
        return pltpu.make_async_copy(self.src(me), self.dst(me), self.local)

    def start(self):
        for c in self.remote():
            c.start()
        self.own().start()

    def wait(self):
        self.own().wait()
        for c in self.remote():
            c.wait()


def route_sems(n, count):
    return [
        pltpu.SemaphoreType.DMA((count, n)),
        pltpu.SemaphoreType.DMA((count, n)),
        pltpu.SemaphoreType.DMA((count,)),
    ]


def greet(n, partner):
    me = lax.axis_index("expert")
    barrier = pltpu.get_barrier_semaphore()
    for d in range(1, n):
        pl.semaphore_signal(
            barrier, inc=1, device_id={"expert": lax.rem(me + d, n)}, device_id_type=MESH
        )
    if partner:
        pl.semaphore_signal(barrier, inc=1, device_id={"dp": 1 - lax.axis_index("dp")}, device_id_type=MESH)
    pl.semaphore_wait(barrier, n if partner else n - 1)


def to_partner(src, dst, send, recv):
    return pltpu.make_async_remote_copy(
        src, dst, send, recv, device_id={"dp": 1 - lax.axis_index("dp")}, device_id_type=MESH
    )


def unit_of(values):
    centre = values - jnp.mean(values, axis=-1, keepdims=True)
    inverse = lax.rsqrt(jnp.mean(centre * centre, axis=-1, keepdims=True) + EPS)
    return centre * inverse, inverse


def lane_pick(width, first):
    lanes = lax.broadcasted_iota(jnp.int32, (1, width), 1)
    return (lanes < HEAD_DIM) if first else (lanes >= HEAD_DIM)


def row_of(ref):
    return ref[...].astype(F32).reshape(1, ref.shape[0])


def front_kernel(
    n, cc, pairs, ids_ref, cot_ref, x_ref, seg_ref, pre_gain, pre_shift, proj_bias, mid_gain, mid_shift, w_ref, w_any, p_ref, p_any,
    tcol_ref, norm_t, hr_ref, att_ref, att_t, prob_ref, mid_ref, slot_ref, arr_ref, wo_out, po_out,
    row_s, cs_s, norm_s, hr_s, wo_s, po_s, bias_s, low_s, send, recv, local, dsend, drecv, dlocal,
):
    step = pl.program_id(0)
    tokens, width = x_ref.shape
    half = p_ref.shape[0]
    rows = n * cc
    first_pair = 7
    routes = [
        Route(
            n, lambda e, c=c: cs_s.at[block_of(c * n + e, cc)], lambda d, c=c: arr_ref.at[c, block_of(d, cc)],
            send.at[c], recv.at[c], local.at[c],
        )
        for c in range(CHUNKS)
    ]

    def swaps():
        return [
            to_partner(w_any, wo_s, dsend.at[0], drecv.at[0]),
            to_partner(p_any, po_s, dsend.at[1], drecv.at[1]),
        ]

    def keeps():
        return [
            pltpu.make_async_copy(wo_s, wo_out, dlocal.at[0]),
            pltpu.make_async_copy(po_s, po_out, dlocal.at[1]),
        ]

    @pl.when(step == 0)
    def _():
        greet(n, True)
        for c in swaps():
            c.start()
        ids = jnp.transpose(jnp.broadcast_to(ids_ref[...].astype(F32), (128, tokens)))
        hot = (ids == lax.broadcasted_iota(jnp.int32, (tokens, 128), 1).astype(F32)).astype(F32)
        low_hot = hot.astype(BF)
        place = []
        for b in range(tokens // 256):
            span = (b + 1) * 256
            lower = (
                lax.broadcasted_iota(jnp.int32, (256, span), 0) + b * 256
                >= lax.broadcasted_iota(jnp.int32, (256, span), 1)
            ).astype(F32).astype(BF)
            counts = dot(lower, low_hot[0:span])
            rank = jnp.sum(counts * hot[b * 256:span], axis=1, keepdims=True) - 1.0
            chunk = jnp.floor((rank + 0.5) * (1.0 / cc))
            place.append(chunk * rows + ids[b * 256:span] * cc + (rank - chunk * cc))
        place = jnp.concatenate(place, axis=0)
        tcol_ref[...] = place.astype(jnp.int32)
        row_s[...] = jnp.transpose(place)[0:8, :].astype(jnp.int32)

        def fill(b, _):
            hot = (
                lax.broadcasted_iota(jnp.int32, (256, tokens), 0) + b * 256 == row_s[0:1, :]
            ).astype(F32).astype(BF)
            cs_s[block_of(b, 256), :] = dot(hot, cot_ref[...]).astype(BF)
            return 0

        for c, r in enumerate(routes):
            lax.fori_loop(c * rows // 256, (c + 1) * rows // 256, fill, 0)
            r.start()

        gain, shift = row_of(pre_gain), row_of(pre_shift)

        def body(b, _):
            at = block_of(b, 128)
            unit, _ = unit_of(x_ref[at, :].astype(F32))
            low = (unit * gain + shift).astype(BF)
            norm_s[at, :] = low
            norm_t[:, at] = jnp.transpose(low)
            return 0

        lax.fori_loop(0, tokens // 128, body, 0)

    @pl.when((step >= 1) & (step <= 3))
    def _():
        out = dot(norm_s[...], w_ref[0]).astype(BF)
        hr_ref[0] = out
        hr_s[step - 1] = out

    @pl.when(step == 4)
    def _():
        for c in swaps():
            c.wait()
        for c in keeps():
            c.start()

    @pl.when((step >= 4) & (step <= 6))
    def _():
        out = dot(norm_s[...], wo_s[step - 4]).astype(BF)
        hr_ref[0] = out
        hr_s[step - 1] = out

    @pl.when(step == first_pair)
    def _():
        seg = seg_ref[...].astype(F32)
        seg_col = jnp.transpose(jnp.broadcast_to(seg, (128, tokens)))
        for i in range(BLOCKS):
            w, s = WIDTH[i], START[i]
            at_row = lax.broadcasted_iota(jnp.int32, (QB, w), 0) + i * QB
            at_key = lax.broadcasted_iota(jnp.int32, (QB, w), 1) + s
            same = seg_col[i * QB:(i + 1) * QB, 0:1] == seg[:, s:s + w]
            bias_s[:, OFFSET[i]:OFFSET[i] + w] = jnp.where(same & (at_key <= at_row), 0.0, -1e30)

    @pl.when((step >= first_pair) & (step < first_pair + pairs))
    def _():
        pair = step - first_pair
        per = half // 128
        side, lanes = lax.div(pair, per), block_of(lax.rem(pair, per), 128)
        query = hr_s[3 * side, :, lanes] * BF(HEAD_DIM ** -0.5)
        for i in range(BLOCKS):
            w, s = WIDTH[i], START[i]
            keys, values = hr_s[3 * side + 1, s:s + w, lanes], hr_s[3 * side + 2, s:s + w, lanes]
            bias = bias_s[:, OFFSET[i]:OFFSET[i] + w]
            parts = []
            for j in range(2):
                q = jnp.where(lane_pick(128, j == 0), query[i * QB:(i + 1) * QB], BF(0))
                scores = dot_nt(q, keys) + bias
                top = jnp.max(scores, axis=-1, keepdims=True)
                weights = jnp.exp(scores - top)
                probs = (weights * (1.0 / jnp.sum(weights, axis=-1, keepdims=True))).astype(BF)
                prob_ref[j, :, OFFSET[i]:OFFSET[i] + w] = probs
                parts.append(dot(probs, values))
            both = jnp.where(lane_pick(128, True), parts[0], parts[1])
            both = both.astype(BF)
            att_ref[i * QB:(i + 1) * QB, block_of(pair, 128)] = both
            att_t[block_of(pair, 128), i * QB:(i + 1) * QB] = jnp.transpose(both)

    @pl.when(step == first_pair + pairs)
    def _():
        pbias, gain, shift = row_of(proj_bias), row_of(mid_gain), row_of(mid_shift)

        def body(b, _):
            at = block_of(b, 128)
            branch = dot(att_ref[at, 0:half], p_ref[...]) + dot(att_ref[at, half:2 * half], po_s[...])
            middle = x_ref[at, :].astype(F32) + branch + pbias
            mid_ref[at, :] = middle
            unit, _ = unit_of(middle)
            low_s[at, :] = (unit * gain + shift).astype(BF)
            return 0

        lax.fori_loop(0, tokens // 128, body, 0)

        def fill(b, _):
            hot = (
                lax.broadcasted_iota(jnp.int32, (256, tokens), 0) + b * 256 == row_s[0:1, :]
            ).astype(F32).astype(BF)
            slot_ref[block_of(b, 256), :] = dot(hot, low_s[...]).astype(BF)
            return 0

        lax.fori_loop(0, CHUNKS * rows // 256, fill, 0)
        for c in keeps():
            c.wait()
        for r in routes:
            r.wait()


def front_call(n, cc, ids, cot, x, seg, vectors, qkv, proj):
    tokens, width = x.shape
    half = proj.shape[0]
    pairs = width // 128
    rows = n * cc
    dma = pltpu.SemaphoreType.DMA
    sds = jax.ShapeDtypeStruct

    def pair_of(i):
        return jnp.clip(i - 7, 0, pairs - 1)

    return pl.pallas_call(
        functools.partial(front_kernel, n, cc, pairs),
        grid=(8 + pairs,),
        in_specs=[
            whole((1, tokens)), whole((tokens, width)), whole((tokens, width)), whole((1, tokens)),
            *[whole((width,))] * 5,
            pl.BlockSpec((1, width, half), lambda i: (jnp.clip(i - 1, 0, 2), 0, 0)), ANY,
            whole((half, width)), ANY,
        ],
        out_specs=[
            whole((tokens, 128)), whole((width, tokens)),
            pl.BlockSpec((1, tokens, half), lambda i: (jnp.clip(i - 1, 0, 5), 0, 0)),
            whole((tokens, width)), whole((width, tokens)), pl.BlockSpec((2, QB, BAND), lambda i: (pair_of(i), 0, 0)),
            whole((tokens, width)), whole((CHUNKS * rows, width)), ANY, ANY, ANY,
        ],
        out_shape=[
            sds((tokens, 128), jnp.int32), sds((width, tokens), BF), sds((6, tokens, half), BF),
            sds((tokens, width), BF), sds((width, tokens), BF), sds((2 * pairs, QB, BAND), BF), sds((tokens, width), F32),
            sds((CHUNKS * rows, width), BF), sds((CHUNKS, rows, width), BF), sds(qkv.shape, BF), sds(proj.shape, BF),
        ],
        scratch_shapes=[
            pltpu.VMEM((8, tokens), jnp.int32), pltpu.VMEM((CHUNKS * rows, width), BF),
            pltpu.VMEM((tokens, width), BF), pltpu.VMEM((6, tokens, half), BF), pltpu.VMEM(qkv.shape, BF),
            pltpu.VMEM(proj.shape, BF), pltpu.VMEM((QB, BAND), F32), pltpu.VMEM((tokens, width), BF),
            *route_sems(n, CHUNKS), dma((2,)), dma((2,)), dma((2,)),
        ],
        compiler_params=params(collective_id=1, has_side_effects=True),
        cost_estimate=cost(3e10, 6e7),
        name="front",
    )(ids, cot, x, seg, *vectors, qkv, qkv, proj, proj)


GELU_C = 0.7978845608028654
GELU_A = 0.044715
TILE = 512


def expert_kernel(
    n, cc, own_tiles, mid_ref, c_ref, uo_ref, ut_ref, do_ref, dt_ref, bo_ref, bt_ref, db_ref,
    act_ref, gh_ref, ub_ref, y_ref, dx_ref, x_out, back_out,
    x_s, g_s, y_s, dx_s, dxb_s, send, recv, local, xsem,
):
    step = pl.program_id(0)
    tiles = 2 * own_tiles
    phase, tile = lax.div(step, tiles), lax.rem(step, tiles)
    rows = n * cc
    ins = [
        Route(
            n, lambda e, c=c: mid_ref.at[block_of(c * n + e, cc)], lambda d, c=c: x_s.at[c, block_of(d, cc)],
            send.at[c], recv.at[c], local.at[c],
        )
        for c in range(CHUNKS)
    ]
    back = Route(
        n, lambda e: dxb_s.at[block_of(e, cc)], lambda d: back_out.at[block_of(d, cc)],
        send.at[CHUNKS], recv.at[CHUNKS], local.at[CHUNKS],
    )

    def keep(c):
        return pltpu.make_async_copy(x_s.at[c], x_out.at[c], xsem.at[c])

    @pl.when(step == 0)
    def _():
        greet(n, False)
        ins[0].start()
        ub_ref[...] = jnp.zeros_like(ub_ref)

    for c in range(CHUNKS):
        @pl.when(step == (c + 1) * tiles)
        def _():
            ins[c].wait()
            (ins[c + 1] if c + 1 < CHUNKS else back).start()
            keep(c).start()

    lanes = block_of(tile, TILE)

    def early(down_ref):
        for c in range(CHUNKS):
            g_s[c, :, lanes] = dot_nt(c_ref[c], down_ref[...]).astype(BF)

    def late(c, up_ref, down_ref, b_ref):
        up, down = up_ref[...], down_ref[...]
        h = dot_nt(x_s[c], up) + b_ref[...].astype(F32)
        sq = h * h
        t = jnp.tanh(GELU_C * (h + GELU_A * (sq * h)))
        act = ((0.5 * h) * (1.0 + t)).astype(BF)
        act_ref[0] = act
        slope = 0.5 * (1.0 + t) + (0.5 * h) * ((1.0 - t * t) * (GELU_C * (1.0 + (3.0 * GELU_A) * sq)))
        gh = (g_s[c, :, lanes].astype(F32) * slope).astype(BF)
        gh_ref[0] = gh
        ub_ref[0:1, lanes] += jnp.sum(gh.astype(F32), axis=0, keepdims=True)
        y_s[...] += dot(act, down)
        dx_s[...] += dot(gh, up)

    @pl.when((phase >= 1) & (tile == 0))
    def _():
        y_s[...] = jnp.broadcast_to(db_ref[...].astype(F32), y_s.shape)
        dx_s[...] = jnp.zeros_like(dx_s)

    @pl.when((phase == 0) & (tile < own_tiles))
    def _():
        early(do_ref)

    @pl.when((phase == 0) & (tile >= own_tiles))
    def _():
        early(dt_ref)

    @pl.when((phase >= 1) & (tile < own_tiles))
    def _():
        late(phase - 1, uo_ref, do_ref, bo_ref)

    @pl.when((phase >= 1) & (tile >= own_tiles))
    def _():
        late(phase - 1, ut_ref, dt_ref, bt_ref)

    @pl.when((phase >= 1) & (tile == tiles - 1))
    def _():
        y_ref[0] = y_s[...].astype(BF)
        dx_ref[0] = dx_s[...].astype(BF)

    @pl.when((phase == 1) & (tile == tiles - 1))
    def _():
        dxb_s[...] = dx_s[...].astype(BF)

    @pl.when(step == (CHUNKS + 1) * tiles - 1)
    def _():
        for c in range(CHUNKS):
            keep(c).wait()
        back.wait()


def expert_call(n, cc, mid_slots, cot, up, down, bias, down_bias):
    up_own, up_oth = up
    down_own, down_oth = down
    b_own, b_oth = bias
    rows = n * cc
    hid, width = up_own.shape
    own_tiles = hid // TILE
    tiles = 2 * own_tiles
    sds = jax.ShapeDtypeStruct

    def first(i):
        return jnp.minimum(i % tiles, own_tiles - 1)

    def second(i):
        return jnp.maximum(i % tiles - own_tiles, 0)

    def up_first(i):
        return jnp.where(i < tiles, 0, first(i))

    def up_second(i):
        return jnp.where(i < tiles, 0, second(i))

    def chunk(i):
        return jnp.maximum(i // tiles - 1, 0)

    def column(i):
        return jnp.where(i < tiles, 0, i % tiles)

    col = pl.BlockSpec((1, rows, TILE), lambda i: (chunk(i), 0, column(i)))
    per_chunk = pl.BlockSpec((1, rows, width), lambda i: (chunk(i), 0, 0))
    return pl.pallas_call(
        functools.partial(expert_kernel, n, cc, own_tiles),
        grid=((CHUNKS + 1) * tiles,),
        in_specs=[
            ANY, whole(cot.shape),
            pl.BlockSpec((TILE, width), lambda i: (up_first(i), 0)),
            pl.BlockSpec((TILE, width), lambda i: (up_second(i), 0)),
            pl.BlockSpec((TILE, width), lambda i: (first(i), 0)),
            pl.BlockSpec((TILE, width), lambda i: (second(i), 0)),
            pl.BlockSpec((1, TILE), lambda i: (0, first(i))),
            pl.BlockSpec((1, TILE), lambda i: (0, second(i))),
            whole((1, width)),
        ],
        out_specs=[col, col, whole((8, 2 * hid)), per_chunk, per_chunk, ANY, ANY],
        out_shape=[
            sds((CHUNKS, rows, 2 * hid), BF), sds((CHUNKS, rows, 2 * hid), BF), sds((8, 2 * hid), F32),
            sds((CHUNKS, rows, width), BF), sds((CHUNKS, rows, width), BF), sds((CHUNKS, rows, width), BF),
            sds((rows, width), BF),
        ],
        scratch_shapes=[
            pltpu.VMEM((CHUNKS, rows, width), BF), pltpu.VMEM((CHUNKS, rows, 2 * hid), BF),
            pltpu.VMEM((rows, width), F32), pltpu.VMEM((rows, width), F32), pltpu.VMEM((rows, width), BF),
            *route_sems(n, CHUNKS + 1), pltpu.SemaphoreType.DMA((CHUNKS,)),
        ],
        compiler_params=params(collective_id=2, has_side_effects=True),
        cost_estimate=cost(5.2e10, 8e7),
        name="experts",
    )(mid_slots, cot, up_own, up_oth, down_own, down_oth, b_own, b_oth, down_bias)


def wgrad_kernel(
    n, cc, tiles, a_ref, g_ref, c_ref, x_ref, ub_ref, dx_ref,
    do_ref, up_ref, ubg_ref, cbg_ref, back1, back2,
    out_s, in_s, small_s, got_s, send, recv, local, dsend, drecv, ssend, srecv,
):
    step = pl.program_id(0)
    hid = ubg_ref.shape[1]
    routes = [
        Route(
            n, lambda e, c=c: dx_ref.at[c, block_of(e, cc)], lambda d, dst=dst: dst.at[block_of(d, cc)],
            send.at[k], recv.at[k], local.at[k],
        )
        for k, (c, dst) in enumerate(((1, back1), (2, back2)))
    ]

    def swap(k):
        return to_partner(out_s.at[k], in_s.at[k], dsend.at[k], drecv.at[k])

    small = to_partner(small_s, got_s, ssend, srecv)

    @pl.when(step == 0)
    def _():
        greet(n, True)
        for r in routes:
            r.start()
        total = jnp.zeros((1, c_ref.shape[2]), F32)
        for c in range(CHUNKS):
            total = total + jnp.sum(c_ref[c].astype(F32), axis=0, keepdims=True)
        small_s[...] = jnp.zeros_like(small_s)
        small_s[0:1, 0:hid] = ub_ref[0:1, hid:2 * hid]
        small_s[0:1, hid:hid + total.shape[1]] = total
        small.start()

    @pl.when(step == 2 * tiles)
    def _():
        small.wait()
        ubg_ref[...] = ub_ref[0:1, 0:hid] + got_s[0:1, 0:hid]
        cbg_ref[...] = small_s[0:1, hid:] + got_s[0:1, hid:]

    def product(left, right):
        total = dot_tn(left[0], right[0])
        for c in range(1, CHUNKS):
            total = total + dot_tn(left[c], right[c])
        return total

    for k in range(2 * tiles):
        @pl.when(step == k)
        def _():
            left, right = (a_ref, c_ref) if k < tiles else (g_ref, x_ref)
            out_s[k] = product(left, right).astype(BF)
            swap(k).start()

        @pl.when(step == 2 * tiles + k)
        def _():
            left, right, out = (a_ref, c_ref, do_ref) if k < tiles else (g_ref, x_ref, up_ref)
            total = product(left, right)
            swap(k).wait()
            out[...] = (total + in_s[k].astype(F32)).astype(BF)

    @pl.when(step == 4 * tiles - 1)
    def _():
        for r in routes:
            r.wait()


def wgrad_call(n, cc, acts, ghs, cot, rows_in, ub, dx):
    _, rows, width = cot.shape
    hid = acts.shape[2] // 2
    tiles = hid // TILE
    dma = pltpu.SemaphoreType.DMA
    sds = jax.ShapeDtypeStruct

    def first(i):
        return jnp.minimum(i % (2 * tiles), tiles - 1)

    def second(i):
        return jnp.maximum(i % (2 * tiles) - tiles, 0)

    def other(i):
        return jnp.where(i < 2 * tiles, tiles, 0)

    a_spec = pl.BlockSpec((CHUNKS, rows, TILE), lambda i: (0, 0, other(i) + first(i)))
    g_spec = pl.BlockSpec((CHUNKS, rows, TILE), lambda i: (0, 0, other(i) + second(i)))

    def late(i):
        return jnp.where(i < 2 * tiles, 0, 1)

    d_spec = pl.BlockSpec((TILE, width), lambda i: (late(i) * first(i), 0))
    u_spec = pl.BlockSpec((TILE, width), lambda i: (late(i) * second(i), 0))
    return pl.pallas_call(
        functools.partial(wgrad_kernel, n, cc, tiles),
        grid=(4 * tiles,),
        in_specs=[a_spec, g_spec, whole(cot.shape), whole(rows_in.shape), whole(ub.shape), ANY],
        out_specs=[d_spec, u_spec, whole((1, hid)), whole((1, width)), ANY, ANY],
        out_shape=[
            sds((hid, width), BF), sds((hid, width), BF), sds((1, hid), F32), sds((1, width), F32),
            sds((rows, width), BF), sds((rows, width), BF),
        ],
        scratch_shapes=[
            pltpu.VMEM((2 * tiles, TILE, width), BF), pltpu.VMEM((2 * tiles, TILE, width), BF),
            pltpu.VMEM((8, hid + width), F32), pltpu.VMEM((8, hid + width), F32),
            *route_sems(n, 2), dma((2 * tiles,)), dma((2 * tiles,)), dma, dma,
        ],
        compiler_params=params(collective_id=3, has_side_effects=True),
        cost_estimate=cost(2.6e10, 8e7),
        name="weight_grads",
    )(acts, ghs, cot, rows_in, ub, dx)


def gather_rows(tcol, parts):
    total = None
    for c, part in enumerate(parts):
        rows = part.shape[0]
        hot = (
            lax.broadcasted_iota(jnp.int32, (tcol.shape[0], rows), 1) + c * rows == tcol[:, 0:1]
        ).astype(F32).astype(BF)
        term = dot(hot, part)
        total = term if total is None else total + term
    return total


def norm_back(grad, unit, inverse, gain):
    scaled = grad * gain
    inner = jnp.mean(scaled, axis=-1, keepdims=True)
    along = jnp.mean(scaled * unit, axis=-1, keepdims=True)
    return inverse * (scaled - inner - unit * along)


def middle_back_kernel(
    n, cc, blocks, tcol_ref, g0, g1, g2, mid_ref, cot_ref, gain_ref, own_ref, oth_ref, att_t, y_src,
    gmid_ref, gatt_ref, pg_own, pg_oth, small_ref, y_dst, gb_s, send, recv, local,
):
    route = Route(
        n, lambda e: y_src.at[0, block_of(e, cc)], lambda d: y_dst.at[block_of(d, cc)],
        send.at[0], recv.at[0], local.at[0],
    )
    step = pl.program_id(0)
    half = own_ref.shape[0]
    tb = mid_ref.shape[0]

    @pl.when(step == 0)
    def _():
        greet(n, False)
        route.start()
        small_ref[...] = jnp.zeros_like(small_ref)

    grad = gather_rows(tcol_ref[...], (g0[...], g1[...], g2[...]))
    grad = grad.astype(BF).astype(F32)
    unit, inverse = unit_of(mid_ref[...])
    gmid = cot_ref[...].astype(F32) + norm_back(grad, unit, inverse, row_of(gain_ref))
    gmid_ref[...] = gmid
    gb = gmid.astype(BF)
    gb_s[block_of(step, tb), :] = gb
    small_ref[2:3, :] += jnp.sum(grad * unit, axis=0, keepdims=True)
    small_ref[3:4, :] += jnp.sum(grad, axis=0, keepdims=True)
    small_ref[4:5, :] += jnp.sum(gb.astype(F32), axis=0, keepdims=True)
    gatt_ref[:, 0:half] = dot_nt(gb, own_ref[...]).astype(BF)
    gatt_ref[:, half:2 * half] = dot_nt(gb, oth_ref[...]).astype(BF)

    @pl.when(step == blocks - 1)
    def _():
        pg_own[...] = dot(att_t[0:half, :], gb_s[...]).astype(BF)
        pg_oth[...] = dot(att_t[half:2 * half, :], gb_s[...]).astype(BF)
        route.wait()


def middle_back_call(n, cc, tcol, grads, middle, cot, gain, proj_own, proj_oth, att_t, y):
    tokens, width = middle.shape
    half = proj_own.shape[0]
    tb = 256
    rows = grads[0].shape[0]
    block = pl.BlockSpec((tb, width), lambda i: (i, 0))
    sds = jax.ShapeDtypeStruct
    return pl.pallas_call(
        functools.partial(middle_back_kernel, n, cc, tokens // tb),
        grid=(tokens // tb,),
        in_specs=[
            pl.BlockSpec((tb, 128), lambda i: (i, 0)), *[whole((rows, width))] * 3, block, block,
            whole((width,)), whole((half, width)), whole((half, width)), whole((tokens, width)), ANY,
        ],
        out_specs=[block, block, whole((half, width)), whole((half, width)), whole((8, width)), ANY],
        out_shape=[
            sds((tokens, width), F32), sds((tokens, width), BF), sds((half, width), BF), sds((half, width), BF),
            sds((8, width), F32), sds((rows, width), BF),
        ],
        scratch_shapes=[pltpu.VMEM((tokens, width), BF), *route_sems(n, 1)],
        compiler_params=params(collective_id=4, has_side_effects=True),
        cost_estimate=cost(1.2e10, 3e7),
        name="middle_back",
    )(tcol, *grads, middle, cot, gain, proj_own, proj_oth, att_t, y)


class Part:
    def __init__(self, index, base, length, order, me, refs, sems):
        self.index, self.base, self.total, self.order, self.me = index, base, length, order, me
        self.acc, self.rcv, self.res = refs
        self.rs_send, self.rs_recv, self.ag_send, self.ag_recv = sems
        self.stages, self.stage = len(order), 0
        self.step = length >> len(order)

    def upper(self, s):
        return lax.rem(lax.div(self.me, 1 << self.order[s]), 2)

    def rows(self, start, length):
        return pl.ds(pl.multiple_of(start, 16), length)

    def start(self, s):
        at = self.base
        for k in range(s):
            at = at + self.upper(k) * (self.total >> (k + 1))
        return at

    def slot(self, s):
        return self.base + self.total - (self.total >> s)

    def copy(self):
        inward = self.stage < self.stages
        s = self.stage if inward else 2 * self.stages - 1 - self.stage
        bit = 1 << self.order[s]
        peer = {"expert": self.me + bit - 2 * bit * self.upper(s)}
        if inward:
            half = self.total >> (s + 1)
            away = self.start(s) + (1 - self.upper(s)) * half
            src, dst = self.acc.at[self.rows(away, half)], self.rcv.at[pl.ds(self.slot(s), half)]
            send, recv = self.rs_send, self.rs_recv
        else:
            src = dst = self.res.at[self.rows(self.start(s + 1), self.total >> (s + 1))]
            send, recv = self.ag_send, self.ag_recv
        return pltpu.make_async_remote_copy(
            src, dst, send.at[self.index, s], recv.at[self.index, s], device_id=peer, device_id_type=MESH
        )

    def begin(self):
        self.copy().start()

    def advance(self):
        self.copy().wait()
        s = self.stage
        if s < self.stages:
            keep, slot, step = self.start(s + 1), self.slot(s), self.step
            into = self.res if s == self.stages - 1 else self.acc

            def add(b, _):
                at = self.rows(keep + b * step, step)
                into[at, :] = (
                    self.acc[at, :].astype(F32) + self.rcv[self.rows(slot + b * step, step), :].astype(F32)
                ).astype(BF)
                return 0

            lax.fori_loop(0, (self.total >> (s + 1)) // step, add, 0)
        self.stage += 1
        if self.stage < 2 * self.stages:
            self.copy().start()


def back_kernel(
    n, cc, groups, q_ref, k_ref, v_ref, prob_ref, do_ref, o_ref, x_ref, norm_t, own_ref, oth_ref,
    gain_ref, small_ref, pg_own, pg_oth, gmid_any, y_src,
    xg_ref, small_out, sum_q, sum_p, z1, z2,
    dk_s, dv_s, gh_s, gnp_s, acc, rcv, res, p_acc, p_rcv, p_res, got, pgot, snd, mine_s, small_got,
    send, recv, local, dsend, drecv, rs_send, rs_recv, ag_send, ag_recv, sm_send, sm_recv, out_sem,
):
    step = pl.program_id(0)
    tokens, width = x_ref.shape
    half = own_ref.shape[2]
    scale = HEAD_DIM ** -0.5
    last = 3 * groups
    kind, group = lax.rem(step, 3), lax.div(step, 3)
    me = lax.axis_index("expert")
    stages = n.bit_length() - 1
    routes = [
        Route(
            n, lambda e, c=c: y_src.at[c, block_of(e, cc)], lambda d, z=z: z.at[block_of(d, cc)],
            send.at[c - 1], recv.at[c - 1], local.at[c - 1],
        )
        for c, z in ((1, z1), (2, z2))
    ]

    split = 2 if width >= 32 * n else 1
    size = width // split
    sems = (rs_send, rs_recv, ag_send, ag_recv)
    order = list(range(stages))
    swapped = [1, 0, *order[2:]]

    def parts_of(first, at, refs):
        return [
            Part(first + i, at * width + i * size, size, order if i % 2 == 0 else swapped, me, refs, sems)
            for i in range(split)
        ]

    head_parts = [parts_of(k * split, k, (acc, rcv, res)) for k in range(groups)]
    proj_parts = parts_of(groups * split, 0, (p_acc, p_rcv, p_res))

    def dp_swap(k):
        src, dst = (snd.at[k], got.at[k]) if k < groups else (pg_oth, pgot)
        return to_partner(src, dst, dsend.at[k], drecv.at[k])

    def bring_to(parts, goal):
        while parts[0].stage < min(goal, 2 * stages):
            for p in parts:
                p.advance()

    def seed(k):
        return pltpu.make_async_copy(gmid_any, xg_ref, out_sem.at[2])

    @pl.when(step == 0)
    def _():
        greet(n, True)
        dp_swap(groups).start()
        for r in routes:
            r.start()
        seed(0).start()

    @pl.when((kind < 2) & (step < last))
    def _():
        side, lanes = 1 - kind, block_of(group, 128)
        dk_s[...] = jnp.zeros_like(dk_s)
        dv_s[...] = jnp.zeros_like(dv_s)
        for i in range(BLOCKS):
            w, s = WIDTH[i], START[i]
            at = slice(i * QB, (i + 1) * QB)
            keys, values = k_ref[0, s:s + w, :], v_ref[0, s:s + w, :]
            go = do_ref[at, :]
            prod = go.astype(F32) * o_ref[at, :].astype(F32)
            query = q_ref[0, at, :]
            parts = []
            for j in range(2):
                pick = lane_pick(128, j == 0)
                go_j = jnp.where(pick, go, BF(0))
                q_j = jnp.where(pick, query, BF(0))
                inner = jnp.sum(jnp.where(pick, prod, 0.0), axis=-1, keepdims=True)
                probs = prob_ref[j, :, OFFSET[i]:OFFSET[i] + w]
                gp = dot_nt(go_j, values)
                gs = (probs.astype(F32) * (gp - inner)).astype(BF)
                parts.append(dot(gs, keys))
                dk_s[s:s + w, :] += dot_tn(gs, q_j)
                dv_s[s:s + w, :] += dot_tn(probs, go_j)
            gh_s[3 * side, at, lanes] = (jnp.where(lane_pick(128, True), parts[0], parts[1]) * scale).astype(BF)
        gh_s[3 * side + 1, :, lanes] = (dk_s[...] * scale).astype(BF)
        gh_s[3 * side + 2, :, lanes] = dv_s[...].astype(BF)

    for k in range(groups):
        @pl.when(step == 3 * k + 2)
        def _():
            at = slice(k * 128, (k + 1) * 128)
            for c in range(3):
                both = dot(norm_t[...], jnp.concatenate([gh_s[3 + c, :, at], gh_s[c, :, at]], axis=1))
                snd[k, :, c * 128:(c + 1) * 128] = both[:, 0:128].astype(BF)
                mine_s[:, c * 128:(c + 1) * 128] = both[:, 128:256]
            dp_swap(k).start()

        @pl.when(step == 3 * k + 3)
        def _():
            dp_swap(k).wait()
            acc[k * width:(k + 1) * width, :] = (mine_s[...] + got[k].astype(F32)).astype(BF)
            for p in head_parts[k]:
                p.begin()

    @pl.when(step == 1)
    def _():
        dp_swap(groups).wait()
        rows = pgot.shape[0]
        for b in range(width // rows):
            at = slice(b * rows, (b + 1) * rows)
            p_acc[at, :] = (pg_own[:, at].astype(F32) + pgot[:, at].astype(F32)).astype(BF)
        for p in proj_parts:
            p.begin()

    for t in range(3, last):
        @pl.when(step == t)
        def _():
            bring_to(proj_parts, sum(t >= m for m in (5, 7, 9, 11)))
            for k in range(groups):
                bring_to(head_parts[k], sum(t >= 3 * k + m for m in (7, 9, 11)))

    @pl.when(step == last)
    def _():
        def small_swap(k):
            if k == 0:
                peer = {"dp": 1 - lax.axis_index("dp")}
            else:
                bit = 1 << (k - 1)
                peer = {"expert": me + bit - 2 * bit * lax.rem(lax.div(me, bit), 2)}
            return pltpu.make_async_remote_copy(
                small_out, small_got.at[k], sm_send.at[k], sm_recv.at[k], device_id=peer, device_id_type=MESH
            )

        def turn():
            for some in [proj_parts, *head_parts]:
                for p in some:
                    if p.stage < 2 * stages:
                        p.advance()

        for c in range(3):
            if c:
                turn()
            term = dot_nt(gh_s[c], own_ref[c]) + dot_nt(gh_s[3 + c], oth_ref[c])
            if c:
                gnp_s[...] += term
            else:
                gnp_s[...] = term
        turn()
        seed(0).wait()
        small_out[...] = small_ref[...]

        def body(b, _):
            at = block_of(b, 128)
            grad = gnp_s[at, :]
            unit, inverse = unit_of(x_ref[at, :].astype(F32))
            xg_ref[at, :] = xg_ref[at, :] + norm_back(grad, unit, inverse, row_of(gain_ref))
            small_out[0:1, :] += jnp.sum(grad * unit, axis=0, keepdims=True)
            small_out[1:2, :] += jnp.sum(grad, axis=0, keepdims=True)
            return 0

        lax.fori_loop(0, tokens // 128, body, 0)
        small = small_swap(0)
        small.start()
        for s in range(2 * stages - 2):
            turn()
            if s <= stages:
                small.wait()
                small_out[...] += small_got[s]
                if s < stages:
                    small = small_swap(s + 1)
                    small.start()
        outs = [
            pltpu.make_async_copy(res, sum_q, out_sem.at[0]),
            pltpu.make_async_copy(p_res, sum_p, out_sem.at[1]),
        ]
        for out in outs:
            out.start()
        for out in outs:
            out.wait()
        for r in routes:
            r.wait()


def back_call(n, cc, head_rows, probs, gatt, att, x, norm_t, own, oth, gmid, gain, small, pg_own, pg_oth, y):
    tokens, width = x.shape
    half = own.shape[2]
    groups = half // 128
    last = 3 * groups
    rows = n * cc
    stages = n.bit_length() - 1
    parts = (groups + 1) * (2 if width >= 32 * n else 1)
    sds, dma, once = jax.ShapeDtypeStruct, pltpu.SemaphoreType.DMA, pl.Buffered(1)

    def place(i):
        i = jnp.minimum(i, last - 1)
        return jnp.maximum(1 - i % 3, 0), i // 3

    def head(c):
        def index(i):
            side, k = place(i)
            return (3 * side + c, 0, k)

        return pl.BlockSpec((1, tokens, 128), index)

    def pair(i):
        side, k = place(i)
        return side * groups + k

    def fixed(shape):
        return pl.BlockSpec(shape, lambda *_: (0,) * len(shape), pipeline_mode=once)

    cols = pl.BlockSpec((tokens, 128), lambda i: (0, pair(i)))
    sums = pltpu.VMEM((groups * width, 384), BF)
    p_sums = pltpu.VMEM((width, half), BF)
    return pl.pallas_call(
        functools.partial(back_kernel, n, cc, groups),
        grid=(last + 1,),
        in_specs=[
            head(0), head(1), head(2), pl.BlockSpec((2, QB, BAND), lambda i: (pair(i), 0, 0)), cols, cols,
            fixed((tokens, width)), fixed((width, tokens)), fixed(own.shape), fixed(oth.shape),
            fixed((width,)), fixed(small.shape), fixed((half, width)), ANY, ANY, ANY,
        ],
        out_specs=[fixed((tokens, width)), fixed(small.shape), ANY, ANY, ANY, ANY],
        out_shape=[
            sds((tokens, width), F32), sds(small.shape, F32), sds((groups * width, 384), BF), sds((width, half), BF),
            sds((rows, width), BF), sds((rows, width), BF),
        ],
        scratch_shapes=[
            pltpu.VMEM((tokens, 128), F32), pltpu.VMEM((tokens, 128), F32), pltpu.VMEM((6, tokens, half), BF),
            pltpu.VMEM((tokens, width), F32), sums, sums, sums, p_sums, p_sums, p_sums,
            pltpu.VMEM((groups, width, 384), BF), pltpu.VMEM((half, width), BF),
            pltpu.VMEM((groups, width, 384), BF), pltpu.VMEM((width, 384), F32),
            pltpu.VMEM((1 + stages, *small.shape), F32),
            *route_sems(n, 2), dma((groups + 1,)), dma((groups + 1,)), dma((parts, stages)), dma((parts, stages)),
            dma((parts, stages)), dma((parts, stages)), dma((1 + stages,)), dma((1 + stages,)), dma((3,)),
        ],
        compiler_params=params(collective_id=5, has_side_effects=True),
        cost_estimate=cost(5.3e10, 9e7),
        name="back",
    )(
        head_rows, head_rows, head_rows, probs, gatt, att, x, norm_t, own, oth, gain, small, pg_own, pg_oth, gmid, y
    )


def result_kernel(tcol_ref, z0, z1, z2, mid_ref, sum_q, sum_p, xg_ref, wd_ref, wu_ref, small_ref, out_ref, q_ref, p_ref, xo_ref, do_ref, uo_ref, *smalls):
    rows = gather_rows(tcol_ref[...], (z0[...], z1[...], z2[...]))
    out_ref[...] = (mid_ref[...] + rows.astype(BF).astype(F32)).astype(BF)
    for c in range(3):
        for k in range(sum_q.shape[0]):
            q_ref[c, :, k * 128:(k + 1) * 128] = sum_q[k, :, c * 128:(c + 1) * 128].astype(F32)
    half = sum_p.shape[2]
    for b in range(sum_p.shape[0]):
        p_ref[:, b * half:(b + 1) * half] = sum_p[b].astype(F32)
    xo_ref[...] = xg_ref[...]
    do_ref[...] = wd_ref[...].astype(F32)
    uo_ref[...] = wu_ref[...].astype(F32)
    for k, small in enumerate(smalls):
        small[...] = small_ref[k:k + 1, :].reshape(small.shape)


def result_call(tcol, zs, middle, sum_q, sum_p, xg, wd, wu, small):
    tokens, width = middle.shape
    half = sum_p.shape[1]
    groups = half // 128
    hid = wd.shape[0]
    rows = zs[0].shape[0]
    steps = 8
    tb, qb, pb, wb = tokens // steps, width // steps, half // steps, hid // steps
    sds = jax.ShapeDtypeStruct
    sum_q = sum_q.reshape(groups, width, 384)
    sum_p = sum_p.reshape(width // half, half, half)

    def rows_of(size, cols):
        return pl.BlockSpec((size, cols), lambda i: (i, 0))

    return pl.pallas_call(
        result_kernel,
        grid=(steps,),
        in_specs=[
            rows_of(tb, 128), *[whole((rows, width))] * 3, rows_of(tb, width),
            pl.BlockSpec((groups, qb, 384), lambda i: (0, i, 0)),
            pl.BlockSpec((width // half, pb, half), lambda i: (0, i, 0)), rows_of(tb, width), rows_of(wb, width),
            rows_of(wb, width), whole(small.shape),
        ],
        out_specs=[
            rows_of(tb, width), pl.BlockSpec((3, qb, half), lambda i: (0, i, 0)), rows_of(pb, width),
            rows_of(tb, width), rows_of(wb, width), rows_of(wb, width), *[whole((width,))] * 5,
        ],
        out_shape=[
            sds((tokens, width), BF), sds((3, width, half), F32), sds((half, width), F32), sds((tokens, width), F32),
            sds((hid, width), F32), sds((hid, width), F32), *[sds((width,), F32)] * 5,
        ],
        compiler_params=params(),
        cost_estimate=cost(6 * tokens * rows * width, 6e7),
        name="results",
    )(tcol, *zs, middle, sum_q, sum_p, xg, wd, wu, small)


def on_device(
    tokens, cotangent, segment_ids, expert_ids, qkv_weight, proj_weight, proj_bias, pre_gain, pre_shift,
    mid_gain, mid_shift, up_weight, up_bias, down_weight, down_bias,
):
    n = lax.axis_size("expert")
    count, width = tokens.shape
    cc = 3 * count // (2 * n) // CHUNKS

    def swap(v):
        return lax.ppermute(v, "dp", [(0, 1), (1, 0)])

    down_own, up_own = down_weight[0], up_weight[0]
    up, down = (up_own, swap(up_own)), (down_own, swap(down_own))
    bias = (up_bias, swap(up_bias))
    vectors = (pre_gain, pre_shift, proj_bias, mid_gain, mid_shift)

    tcol, norm_t, head_rows, att, att_t, probs, middle, mid_slots, cot_rows, qkv_oth, proj_oth = front_call(
        n, cc, expert_ids.reshape(1, count), cotangent, tokens, segment_ids, vectors, qkv_weight, proj_weight)
    acts, ghs, ub, y, dx, arrived, gm0 = expert_call(n, cc, mid_slots, cot_rows, up, down, bias, down_bias)
    down_grad, up_grad, upbias_grad, downbias_grad, gm1, gm2 = wgrad_call(n, cc, acts, ghs, cot_rows, arrived, ub, dx)

    gmid, gatt, pg_own, pg_oth, small, z0 = middle_back_call(
        n, cc, tcol, (gm0, gm1, gm2), middle, cotangent, mid_gain, proj_weight, proj_oth, att_t, y)
    input_grad, small, sum_q, sum_p, z1, z2 = back_call(
        n, cc, head_rows, probs, gatt, att, tokens, norm_t, qkv_weight, qkv_oth, gmid, pre_gain, small, pg_own, pg_oth, y)
    output, qkv_grad, proj_grad, input_grad, down_grad, up_grad, pregain, preshift, midgain, midshift, projbias = result_call(
        tcol, (z0, z1, z2), middle, sum_q, sum_p, input_grad, down_grad, up_grad, small)
    return (
        output, input_grad, qkv_grad, proj_grad, projbias, pregain, preshift, midgain, midshift,
        up_grad[None], upbias_grad, down_grad[None], downbias_grad,
    )


def solution(mesh):
    token = P(("dp", "expert"), None)
    in_specs = (
        token, token, token, token, P(None, None, "dp"), P("dp", None), P(), P(), P(), P(), P(),
        P("expert", "dp", None), P("expert", "dp"), P("expert", "dp", None), P("expert", None),
    )
    out_specs = (
        token, token, P(None, None, "dp"), P("dp", None), P(), P(), P(), P(), P(),
        P("expert", "dp", None), P("expert", "dp"), P("expert", "dp", None), P("expert", None),
    )
    return jax.shard_map(on_device, mesh=mesh, in_specs=in_specs, out_specs=out_specs, check_vma=False)
```

```python
import functools

import jax
import jax.numpy as jnp
from jax import lax
from jax.experimental import pallas as pl
from jax.experimental.pallas import tpu as pltpu
from jax.sharding import PartitionSpec as P

HEAD_DIM = 64
SEQ = 1024
DOC_MAX = 512
EPS = 1e-05
QB = 256
CHUNKS = 3
BF = jnp.bfloat16
F32 = jnp.float32
MESH = pl.DeviceIdType.MESH
VMEM_LIMIT = 60 * 1024 * 1024

BLOCKS = SEQ // QB
START = [max(0, i * QB - DOC_MAX) for i in range(BLOCKS)]
WIDTH = [(i + 1) * QB - START[i] for i in range(BLOCKS)]
OFFSET = [sum(WIDTH[:i]) for i in range(BLOCKS)]
BAND = sum(WIDTH)


def dot(a, b):
    return jnp.dot(a, b, preferred_element_type=F32)


def dot_nt(a, b):
    return lax.dot_general(a, b, (((1,), (1,)), ((), ())), preferred_element_type=F32)


def dot_tn(a, b):
    return lax.dot_general(a, b, (((0,), (0,)), ((), ())), preferred_element_type=F32)


def params(**kw):
    return pltpu.CompilerParams(vmem_limit_bytes=VMEM_LIMIT, **kw)


def cost(flops, nbytes, trans=0):
    return pl.CostEstimate(flops=int(flops), bytes_accessed=int(nbytes), transcendentals=int(trans))


ANY = pl.BlockSpec(memory_space=pl.ANY)


def whole(shape):
    return pl.BlockSpec(shape, lambda *_: (0,) * len(shape))


def block_of(index, size):
    return pl.ds(pl.multiple_of(index * size, size), size)


class Route:
    def __init__(self, n, src, dst, send, recv, local):
        self.n, self.src, self.dst = n, src, dst
        self.send, self.recv, self.local = send, recv, local

    def remote(self):
        me = lax.axis_index("expert")
        for d in range(1, self.n):
            there = lax.rem(me + d, self.n)
            yield pltpu.make_async_remote_copy(
                self.src(there), self.dst(me), self.send.at[d], self.recv.at[d],
                device_id={"expert": there}, device_id_type=MESH,
            )

    def own(self):
        me = lax.axis_index("expert")
        return pltpu.make_async_copy(self.src(me), self.dst(me), self.local)

    def start(self):
        for c in self.remote():
            c.start()
        self.own().start()

    def wait(self):
        self.own().wait()
        for c in self.remote():
            c.wait()


def route_sems(n, count):
    return [
        pltpu.SemaphoreType.DMA((count, n)),
        pltpu.SemaphoreType.DMA((count, n)),
        pltpu.SemaphoreType.DMA((count,)),
    ]


def greet(n, partner):
    me = lax.axis_index("expert")
    barrier = pltpu.get_barrier_semaphore()
    for d in range(1, n):
        pl.semaphore_signal(
            barrier, inc=1, device_id={"expert": lax.rem(me + d, n)}, device_id_type=MESH
        )
    if partner:
        pl.semaphore_signal(barrier, inc=1, device_id={"dp": 1 - lax.axis_index("dp")}, device_id_type=MESH)
    pl.semaphore_wait(barrier, n if partner else n - 1)


def to_partner(src, dst, send, recv):
    return pltpu.make_async_remote_copy(
        src, dst, send, recv, device_id={"dp": 1 - lax.axis_index("dp")}, device_id_type=MESH
    )


def unit_of(values):
    centre = values - jnp.mean(values, axis=-1, keepdims=True)
    inverse = lax.rsqrt(jnp.mean(centre * centre, axis=-1, keepdims=True) + EPS)
    return centre * inverse, inverse


def lane_pick(width, first):
    lanes = lax.broadcasted_iota(jnp.int32, (1, width), 1)
    return (lanes < HEAD_DIM) if first else (lanes >= HEAD_DIM)


def two_heads(rows):
    return jnp.concatenate([jnp.where(lane_pick(128, j == 0), rows, BF(0)) for j in range(2)], axis=0)


def row_of(ref):
    return ref[...].astype(F32).reshape(1, ref.shape[0])


def front_kernel(
    n, cc, pairs, ids_ref, cot_ref, x_any, seg_ref, pre_gain, pre_shift, proj_bias, mid_gain, mid_shift, w_ref, w_any, p_any,
    tcol_ref, norm_t, hr_ref, att_ref, att_t, prob_ref, mid_ref, slot_ref, arr_ref, wo_out, po_out,
    x_ref, p_ref, row_s, cs_s, norm_s, hr_s, wo_s, po_s, bias_s, low_s, send, recv, local, dsend, drecv, dlocal,
):
    step = pl.program_id(0)
    tokens, width = x_ref.shape
    half = p_ref.shape[0]
    rows = n * cc
    first_pair = 7
    routes = [
        Route(
            n, lambda e, c=c: cs_s.at[block_of(c * n + e, cc)], lambda d, c=c: arr_ref.at[c, block_of(d, cc)],
            send.at[c], recv.at[c], local.at[c],
        )
        for c in range(CHUNKS)
    ]

    def swaps():
        return [
            to_partner(w_any, wo_s, dsend.at[0], drecv.at[0]),
            to_partner(p_any, po_s, dsend.at[1], drecv.at[1]),
        ]

    def keeps():
        return [
            pltpu.make_async_copy(wo_s, wo_out, dlocal.at[0]),
            pltpu.make_async_copy(po_s, po_out, dlocal.at[1]),
        ]

    def loads():
        return [
            pltpu.make_async_copy(x_any, x_ref, dlocal.at[2]),
            pltpu.make_async_copy(p_any, p_ref, dlocal.at[3]),
        ]

    @pl.when(step == 0)
    def _():
        for c in loads():
            c.start()
        greet(n, True)
        for c in swaps():
            c.start()
        ids = jnp.transpose(jnp.broadcast_to(ids_ref[...].astype(F32), (128, tokens)))
        hot = (ids == lax.broadcasted_iota(jnp.int32, (tokens, 128), 1).astype(F32)).astype(F32)
        low_hot = hot.astype(BF)
        place = []
        for b in range(tokens // 256):
            span = (b + 1) * 256
            lower = (
                lax.broadcasted_iota(jnp.int32, (256, span), 0) + b * 256
                >= lax.broadcasted_iota(jnp.int32, (256, span), 1)
            ).astype(F32).astype(BF)
            counts = dot(lower, low_hot[0:span])
            rank = jnp.sum(counts * hot[b * 256:span], axis=1, keepdims=True) - 1.0
            chunk = jnp.floor((rank + 0.5) * (1.0 / cc))
            place.append(chunk * rows + ids[b * 256:span] * cc + (rank - chunk * cc))
        place = jnp.concatenate(place, axis=0)
        tcol_ref[...] = place.astype(jnp.int32)
        row_s[...] = jnp.transpose(place)[0:8, :].astype(jnp.int32)

        def fill(b, _):
            hot = (
                lax.broadcasted_iota(jnp.int32, (256, tokens), 0) + b * 256 == row_s[0:1, :]
            ).astype(F32).astype(BF)
            cs_s[block_of(b, 256), :] = dot(hot, cot_ref[...]).astype(BF)
            return 0

        for c, r in enumerate(routes):
            lax.fori_loop(c * rows // 256, (c + 1) * rows // 256, fill, 0)
            r.start()

        for c in loads():
            c.wait()
        gain, shift = row_of(pre_gain), row_of(pre_shift)

        def body(b, _):
            at = block_of(b, 128)
            unit, _ = unit_of(x_ref[at, :].astype(F32))
            low = (unit * gain + shift).astype(BF)
            norm_s[at, :] = low
            norm_t[:, at] = jnp.transpose(low)
            return 0

        lax.fori_loop(0, tokens // 128, body, 0)

    @pl.when((step >= 1) & (step <= 3))
    def _():
        out = dot(norm_s[...], w_ref[0]).astype(BF)
        hr_ref[0] = out
        hr_s[step - 1] = out

    @pl.when(step == 4)
    def _():
        for c in swaps():
            c.wait()
        for c in keeps():
            c.start()

    @pl.when((step >= 4) & (step <= 6))
    def _():
        out = dot(norm_s[...], wo_s[step - 4]).astype(BF)
        hr_ref[0] = out
        hr_s[step - 1] = out

    @pl.when(step == first_pair)
    def _():
        seg = seg_ref[...].astype(F32)
        seg_col = jnp.transpose(jnp.broadcast_to(seg, (128, tokens)))
        for i in range(BLOCKS):
            w, s = WIDTH[i], START[i]
            at_row = lax.broadcasted_iota(jnp.int32, (QB, w), 0) + i * QB
            at_key = lax.broadcasted_iota(jnp.int32, (QB, w), 1) + s
            same = seg_col[i * QB:(i + 1) * QB, 0:1] == seg[:, s:s + w]
            bias_s[:, OFFSET[i]:OFFSET[i] + w] = jnp.where(same & (at_key <= at_row), 0.0, -1e30)

    @pl.when((step >= first_pair) & (step < first_pair + pairs))
    def _():
        pair = step - first_pair
        per = half // 128
        side, lanes = lax.div(pair, per), block_of(lax.rem(pair, per), 128)
        query = hr_s[3 * side, :, lanes] * BF(HEAD_DIM ** -0.5)
        for i in range(BLOCKS):
            w, s = WIDTH[i], START[i]
            keys, values = hr_s[3 * side + 1, s:s + w, lanes], hr_s[3 * side + 2, s:s + w, lanes]
            bias = bias_s[:, OFFSET[i]:OFFSET[i] + w]
            scores = dot_nt(two_heads(query[i * QB:(i + 1) * QB]), keys)
            parts = []
            for j in range(2):
                masked = scores[j * QB:(j + 1) * QB] + bias
                top = jnp.max(masked, axis=-1, keepdims=True)
                weights = jnp.exp(masked - top)
                probs = (weights * (1.0 / jnp.sum(weights, axis=-1, keepdims=True))).astype(BF)
                prob_ref[j, :, OFFSET[i]:OFFSET[i] + w] = probs
                parts.append(probs)
            out = dot(jnp.concatenate(parts, axis=0), values)
            both = jnp.where(lane_pick(128, True), out[0:QB], out[QB:2 * QB])
            both = both.astype(BF)
            att_ref[i * QB:(i + 1) * QB, block_of(pair, 128)] = both
            att_t[block_of(pair, 128), i * QB:(i + 1) * QB] = jnp.transpose(both)

    @pl.when(step == first_pair + pairs)
    def _():
        pbias, gain, shift = row_of(proj_bias), row_of(mid_gain), row_of(mid_shift)

        def body(b, _):
            at = block_of(b, 128)
            branch = dot(att_ref[at, 0:half], p_ref[...]) + dot(att_ref[at, half:2 * half], po_s[...])
            middle = x_ref[at, :].astype(F32) + branch + pbias
            mid_ref[at, :] = middle
            unit, _ = unit_of(middle)
            low_s[at, :] = (unit * gain + shift).astype(BF)
            return 0

        lax.fori_loop(0, tokens // 128, body, 0)

        def fill(b, _):
            hot = (
                lax.broadcasted_iota(jnp.int32, (256, tokens), 0) + b * 256 == row_s[0:1, :]
            ).astype(F32).astype(BF)
            slot_ref[block_of(b, 256), :] = dot(hot, low_s[...]).astype(BF)
            return 0

        lax.fori_loop(0, CHUNKS * rows // 256, fill, 0)
        for c in keeps():
            c.wait()
        for r in routes:
            r.wait()


def front_call(n, cc, ids, cot, x, seg, vectors, qkv, proj):
    tokens, width = x.shape
    half = proj.shape[0]
    pairs = width // 128
    rows = n * cc
    dma = pltpu.SemaphoreType.DMA
    sds = jax.ShapeDtypeStruct

    def pair_of(i):
        return jnp.clip(i - 7, 0, pairs - 1)

    return pl.pallas_call(
        functools.partial(front_kernel, n, cc, pairs),
        grid=(8 + pairs,),
        in_specs=[
            whole((1, tokens)), whole((tokens, width)), ANY, whole((1, tokens)),
            *[whole((width,))] * 5,
            pl.BlockSpec((1, width, half), lambda i: (jnp.clip(i - 1, 0, 2), 0, 0)), ANY,
            ANY,
        ],
        out_specs=[
            whole((tokens, 128)), whole((width, tokens)),
            pl.BlockSpec((1, tokens, half), lambda i: (jnp.clip(i - 1, 0, 5), 0, 0)),
            whole((tokens, width)), whole((width, tokens)), pl.BlockSpec((2, QB, BAND), lambda i: (pair_of(i), 0, 0)),
            whole((tokens, width)), whole((CHUNKS * rows, width)), ANY, ANY, ANY,
        ],
        out_shape=[
            sds((tokens, 128), jnp.int32), sds((width, tokens), BF), sds((6, tokens, half), BF),
            sds((tokens, width), BF), sds((width, tokens), BF), sds((2 * pairs, QB, BAND), BF), sds((tokens, width), F32),
            sds((CHUNKS * rows, width), BF), sds((CHUNKS, rows, width), BF), sds(qkv.shape, BF), sds(proj.shape, BF),
        ],
        scratch_shapes=[
            pltpu.VMEM((tokens, width), BF), pltpu.VMEM((half, width), BF),
            pltpu.VMEM((8, tokens), jnp.int32), pltpu.VMEM((CHUNKS * rows, width), BF),
            pltpu.VMEM((tokens, width), BF), pltpu.VMEM((6, tokens, half), BF), pltpu.VMEM(qkv.shape, BF),
            pltpu.VMEM(proj.shape, BF), pltpu.VMEM((QB, BAND), F32), pltpu.VMEM((tokens, width), BF),
            *route_sems(n, CHUNKS), dma((2,)), dma((2,)), dma((4,)),
        ],
        compiler_params=params(collective_id=1, has_side_effects=True),
        cost_estimate=cost(3e10, 6e7),
        name="front",
    )(ids, cot, x, seg, *vectors, qkv, qkv, proj)


GELU_C = 0.7978845608028654
GELU_A = 0.044715
TILE = 512


def expert_kernel(
    n, cc, own_tiles, mid_ref, c_ref, uo_ref, ut_ref, do_ref, dt_ref, bo_ref, bt_ref, db_ref,
    act_ref, gh_ref, ub_ref, y_ref, dx_ref, x_out, back_out,
    x_s, g_s, y_s, dx_s, dxb_s, send, recv, local, xsem,
):
    step = pl.program_id(0)
    tiles = 2 * own_tiles
    phase, tile = lax.div(step, tiles), lax.rem(step, tiles)
    rows = n * cc
    ins = [
        Route(
            n, lambda e, c=c: mid_ref.at[block_of(c * n + e, cc)], lambda d, c=c: x_s.at[c, block_of(d, cc)],
            send.at[c], recv.at[c], local.at[c],
        )
        for c in range(CHUNKS)
    ]
    back = Route(
        n, lambda e: dxb_s.at[block_of(e, cc)], lambda d: back_out.at[block_of(d, cc)],
        send.at[CHUNKS], recv.at[CHUNKS], local.at[CHUNKS],
    )

    def keep(c):
        return pltpu.make_async_copy(x_s.at[c], x_out.at[c], xsem.at[c])

    @pl.when(step == 0)
    def _():
        greet(n, False)
        ins[0].start()
        ub_ref[...] = jnp.zeros_like(ub_ref)

    for c in range(CHUNKS):
        @pl.when(step == (c + 1) * tiles)
        def _():
            ins[c].wait()
            (ins[c + 1] if c + 1 < CHUNKS else back).start()
            keep(c).start()

    lanes = block_of(tile, TILE)

    def early(down_ref):
        for c in range(CHUNKS):
            g_s[c, :, lanes] = dot_nt(c_ref[c], down_ref[...]).astype(BF)

    def late(c, up_ref, down_ref, b_ref):
        up, down = up_ref[...], down_ref[...]
        h = dot_nt(x_s[c], up) + b_ref[...].astype(F32)
        sq = h * h
        t = jnp.tanh(GELU_C * (h + GELU_A * (sq * h)))
        act = ((0.5 * h) * (1.0 + t)).astype(BF)
        act_ref[0] = act
        slope = 0.5 * (1.0 + t) + (0.5 * h) * ((1.0 - t * t) * (GELU_C * (1.0 + (3.0 * GELU_A) * sq)))
        gh = (g_s[c, :, lanes].astype(F32) * slope).astype(BF)
        gh_ref[0] = gh
        ub_ref[0:1, lanes] += jnp.sum(gh.astype(F32), axis=0, keepdims=True)
        y_s[...] += dot(act, down)
        dx_s[...] += dot(gh, up)

    @pl.when((phase >= 1) & (tile == 0))
    def _():
        y_s[...] = jnp.broadcast_to(db_ref[...].astype(F32), y_s.shape)
        dx_s[...] = jnp.zeros_like(dx_s)

    @pl.when((phase == 0) & (tile < own_tiles))
    def _():
        early(do_ref)

    @pl.when((phase == 0) & (tile >= own_tiles))
    def _():
        early(dt_ref)

    @pl.when((phase >= 1) & (tile < own_tiles))
    def _():
        late(phase - 1, uo_ref, do_ref, bo_ref)

    @pl.when((phase >= 1) & (tile >= own_tiles))
    def _():
        late(phase - 1, ut_ref, dt_ref, bt_ref)

    @pl.when((phase >= 1) & (tile == tiles - 1))
    def _():
        y_ref[0] = y_s[...].astype(BF)
        dx_ref[0] = dx_s[...].astype(BF)

    @pl.when((phase == 1) & (tile == tiles - 1))
    def _():
        dxb_s[...] = dx_s[...].astype(BF)

    @pl.when(step == (CHUNKS + 1) * tiles - 1)
    def _():
        for c in range(CHUNKS):
            keep(c).wait()
        back.wait()


def expert_call(n, cc, mid_slots, cot, up, down, bias, down_bias):
    up_own, up_oth = up
    down_own, down_oth = down
    b_own, b_oth = bias
    rows = n * cc
    hid, width = up_own.shape
    own_tiles = hid // TILE
    tiles = 2 * own_tiles
    sds = jax.ShapeDtypeStruct

    def first(i):
        return jnp.minimum(i % tiles, own_tiles - 1)

    def second(i):
        return jnp.maximum(i % tiles - own_tiles, 0)

    def up_first(i):
        return jnp.where(i < tiles, 0, first(i))

    def up_second(i):
        return jnp.where(i < tiles, 0, second(i))

    def chunk(i):
        return jnp.maximum(i // tiles - 1, 0)

    def column(i):
        return jnp.where(i < tiles, 0, i % tiles)

    col = pl.BlockSpec((1, rows, TILE), lambda i: (chunk(i), 0, column(i)))
    per_chunk = pl.BlockSpec((1, rows, width), lambda i: (chunk(i), 0, 0))
    return pl.pallas_call(
        functools.partial(expert_kernel, n, cc, own_tiles),
        grid=((CHUNKS + 1) * tiles,),
        in_specs=[
            ANY, whole(cot.shape),
            pl.BlockSpec((TILE, width), lambda i: (up_first(i), 0)),
            pl.BlockSpec((TILE, width), lambda i: (up_second(i), 0)),
            pl.BlockSpec((TILE, width), lambda i: (first(i), 0)),
            pl.BlockSpec((TILE, width), lambda i: (second(i), 0)),
            pl.BlockSpec((1, TILE), lambda i: (0, first(i))),
            pl.BlockSpec((1, TILE), lambda i: (0, second(i))),
            whole((1, width)),
        ],
        out_specs=[col, col, whole((8, 2 * hid)), per_chunk, per_chunk, ANY, ANY],
        out_shape=[
            sds((CHUNKS, rows, 2 * hid), BF), sds((CHUNKS, rows, 2 * hid), BF), sds((8, 2 * hid), F32),
            sds((CHUNKS, rows, width), BF), sds((CHUNKS, rows, width), BF), sds((CHUNKS, rows, width), BF),
            sds((rows, width), BF),
        ],
        scratch_shapes=[
            pltpu.VMEM((CHUNKS, rows, width), BF), pltpu.VMEM((CHUNKS, rows, 2 * hid), BF),
            pltpu.VMEM((rows, width), F32), pltpu.VMEM((rows, width), F32), pltpu.VMEM((rows, width), BF),
            *route_sems(n, CHUNKS + 1), pltpu.SemaphoreType.DMA((CHUNKS,)),
        ],
        compiler_params=params(collective_id=2, has_side_effects=True),
        cost_estimate=cost(5.2e10, 8e7),
        name="experts",
    )(mid_slots, cot, up_own, up_oth, down_own, down_oth, b_own, b_oth, down_bias)


def wgrad_kernel(
    n, cc, tiles, a_ref, g_ref, c_any, x_any, ub_ref, dx_ref,
    do_ref, up_ref, ubg_ref, cbg_ref, back1, back2,
    c_ref, x_ref, out_s, in_s, small_s, got_s, send, recv, local, dsend, drecv, ssend, srecv, lsem,
):
    step = pl.program_id(0)
    hid = ubg_ref.shape[1]
    routes = [
        Route(
            n, lambda e, c=c: dx_ref.at[c, block_of(e, cc)], lambda d, dst=dst: dst.at[block_of(d, cc)],
            send.at[k], recv.at[k], local.at[k],
        )
        for k, (c, dst) in enumerate(((1, back1), (2, back2)))
    ]

    def swap(k):
        return to_partner(out_s.at[k], in_s.at[k], dsend.at[k], drecv.at[k])

    small = to_partner(small_s, got_s, ssend, srecv)

    def loads():
        return [
            pltpu.make_async_copy(c_any, c_ref, lsem.at[0]),
            pltpu.make_async_copy(x_any, x_ref, lsem.at[1]),
        ]

    @pl.when(step == 0)
    def _():
        for c in loads():
            c.start()
        greet(n, True)
        for r in routes:
            r.start()
        loads()[0].wait()
        total = jnp.zeros((1, c_ref.shape[2]), F32)
        for c in range(CHUNKS):
            total = total + jnp.sum(c_ref[c].astype(F32), axis=0, keepdims=True)
        small_s[...] = jnp.zeros_like(small_s)
        small_s[0:1, 0:hid] = ub_ref[0:1, hid:2 * hid]
        small_s[0:1, hid:hid + total.shape[1]] = total
        small.start()

    @pl.when(step == 2 * tiles)
    def _():
        small.wait()
        ubg_ref[...] = ub_ref[0:1, 0:hid] + got_s[0:1, 0:hid]
        cbg_ref[...] = small_s[0:1, hid:] + got_s[0:1, hid:]

    def product(left, right):
        total = dot_tn(left[0], right[0])
        for c in range(1, CHUNKS):
            total = total + dot_tn(left[c], right[c])
        return total

    for k in range(2 * tiles):
        @pl.when(step == k)
        def _():
            left, right = (a_ref, c_ref) if k < tiles else (g_ref, x_ref)
            if k == tiles:
                loads()[1].wait()
            out_s[k] = product(left, right).astype(BF)
            swap(k).start()

        @pl.when(step == 2 * tiles + k)
        def _():
            left, right, out = (a_ref, c_ref, do_ref) if k < tiles else (g_ref, x_ref, up_ref)
            total = product(left, right)
            swap(k).wait()
            out[...] = (total + in_s[k].astype(F32)).astype(BF)

    @pl.when(step == 4 * tiles - 1)
    def _():
        for r in routes:
            r.wait()


def wgrad_call(n, cc, acts, ghs, cot, rows_in, ub, dx):
    _, rows, width = cot.shape
    hid = acts.shape[2] // 2
    tiles = hid // TILE
    dma = pltpu.SemaphoreType.DMA
    sds = jax.ShapeDtypeStruct

    def first(i):
        return jnp.minimum(i % (2 * tiles), tiles - 1)

    def second(i):
        return jnp.maximum(i % (2 * tiles) - tiles, 0)

    def other(i):
        return jnp.where(i < 2 * tiles, tiles, 0)

    a_spec = pl.BlockSpec((CHUNKS, rows, TILE), lambda i: (0, 0, other(i) + first(i)))
    g_spec = pl.BlockSpec((CHUNKS, rows, TILE), lambda i: (0, 0, other(i) + second(i)))

    def late(i):
        return jnp.where(i < 2 * tiles, 0, 1)

    d_spec = pl.BlockSpec((TILE, width), lambda i: (late(i) * first(i), 0))
    u_spec = pl.BlockSpec((TILE, width), lambda i: (late(i) * second(i), 0))
    return pl.pallas_call(
        functools.partial(wgrad_kernel, n, cc, tiles),
        grid=(4 * tiles,),
        in_specs=[a_spec, g_spec, ANY, ANY, whole(ub.shape), ANY],
        out_specs=[d_spec, u_spec, whole((1, hid)), whole((1, width)), ANY, ANY],
        out_shape=[
            sds((hid, width), BF), sds((hid, width), BF), sds((1, hid), F32), sds((1, width), F32),
            sds((rows, width), BF), sds((rows, width), BF),
        ],
        scratch_shapes=[
            pltpu.VMEM(cot.shape, BF), pltpu.VMEM(rows_in.shape, BF), pltpu.VMEM((2 * tiles, TILE, width), BF), pltpu.VMEM((2 * tiles, TILE, width), BF),
            pltpu.VMEM((8, hid + width), F32), pltpu.VMEM((8, hid + width), F32),
            *route_sems(n, 2), dma((2 * tiles,)), dma((2 * tiles,)), dma, dma, dma((2,)),
        ],
        compiler_params=params(collective_id=3, has_side_effects=True),
        cost_estimate=cost(2.6e10, 8e7),
        name="weight_grads",
    )(acts, ghs, cot, rows_in, ub, dx)


def gather_rows(tcol, parts):
    total = None
    for c, part in enumerate(parts):
        rows = part.shape[0]
        hot = (
            lax.broadcasted_iota(jnp.int32, (tcol.shape[0], rows), 1) + c * rows == tcol[:, 0:1]
        ).astype(F32).astype(BF)
        term = dot(hot, part)
        total = term if total is None else total + term
    return total


def norm_back(grad, unit, inverse, gain):
    scaled = grad * gain
    inner = jnp.mean(scaled, axis=-1, keepdims=True)
    along = jnp.mean(scaled * unit, axis=-1, keepdims=True)
    return inverse * (scaled - inner - unit * along)


def middle_back_kernel(
    n, cc, blocks, tcol_ref, g0_any, g1_any, g2_any, mid_ref, cot_ref, gain_ref, own_any, oth_any, att_any, y_src,
    gmid_ref, gatt_ref, pg_own, pg_oth, small_ref, y_dst,
    gb_s, g0, g1, g2, own_ref, oth_ref, att_t, send, recv, local, lsem,
):
    route = Route(
        n, lambda e: y_src.at[0, block_of(e, cc)], lambda d: y_dst.at[block_of(d, cc)],
        send.at[0], recv.at[0], local.at[0],
    )
    step = pl.program_id(0)
    half = own_ref.shape[0]
    tb = mid_ref.shape[0]

    def load(k):
        src = (g0_any, g1_any, g2_any, own_any, oth_any, att_any)[k]
        return pltpu.make_async_copy(src, (g0, g1, g2, own_ref, oth_ref, att_t)[k], lsem.at[k])

    @pl.when(step == 0)
    def _():
        for k in range(6):
            load(k).start()
        greet(n, False)
        route.start()
        small_ref[...] = jnp.zeros_like(small_ref)
        for k in range(5):
            load(k).wait()

    grad = gather_rows(tcol_ref[...], (g0[...], g1[...], g2[...]))
    grad = grad.astype(BF).astype(F32)
    unit, inverse = unit_of(mid_ref[...])
    gmid = cot_ref[...].astype(F32) + norm_back(grad, unit, inverse, row_of(gain_ref))
    gmid_ref[...] = gmid
    gb = gmid.astype(BF)
    gb_s[block_of(step, tb), :] = gb
    small_ref[2:3, :] += jnp.sum(grad * unit, axis=0, keepdims=True)
    small_ref[3:4, :] += jnp.sum(grad, axis=0, keepdims=True)
    small_ref[4:5, :] += jnp.sum(gb.astype(F32), axis=0, keepdims=True)
    gatt_ref[:, 0:half] = dot_nt(gb, own_ref[...]).astype(BF)
    gatt_ref[:, half:2 * half] = dot_nt(gb, oth_ref[...]).astype(BF)

    @pl.when(step == blocks - 1)
    def _():
        load(5).wait()
        pg_own[...] = dot(att_t[0:half, :], gb_s[...]).astype(BF)
        pg_oth[...] = dot(att_t[half:2 * half, :], gb_s[...]).astype(BF)
        route.wait()


def middle_back_call(n, cc, tcol, grads, middle, cot, gain, proj_own, proj_oth, att_t, y):
    tokens, width = middle.shape
    half = proj_own.shape[0]
    tb = 256
    rows = grads[0].shape[0]
    block = pl.BlockSpec((tb, width), lambda i: (i, 0))
    sds = jax.ShapeDtypeStruct
    return pl.pallas_call(
        functools.partial(middle_back_kernel, n, cc, tokens // tb),
        grid=(tokens // tb,),
        in_specs=[
            pl.BlockSpec((tb, 128), lambda i: (i, 0)), ANY, ANY, ANY, block, block,
            whole((width,)), ANY, ANY, ANY, ANY,
        ],
        out_specs=[block, block, whole((half, width)), whole((half, width)), whole((8, width)), ANY],
        out_shape=[
            sds((tokens, width), F32), sds((tokens, width), BF), sds((half, width), BF), sds((half, width), BF),
            sds((8, width), F32), sds((rows, width), BF),
        ],
        scratch_shapes=[
            pltpu.VMEM((tokens, width), BF), *[pltpu.VMEM((rows, width), BF)] * CHUNKS, pltpu.VMEM((half, width), BF),
            pltpu.VMEM((half, width), BF), pltpu.VMEM((width, tokens), BF), *route_sems(n, 1),
            pltpu.SemaphoreType.DMA((6,)),
        ],
        compiler_params=params(collective_id=4, has_side_effects=True),
        cost_estimate=cost(1.2e10, 3e7),
        name="middle_back",
    )(tcol, *grads, middle, cot, gain, proj_own, proj_oth, att_t, y)


class Part:
    def __init__(self, index, base, length, order, me, refs, sems):
        self.index, self.base, self.total, self.order, self.me = index, base, length, order, me
        self.acc, self.rcv, self.res = refs
        self.rs_send, self.rs_recv, self.ag_send, self.ag_recv = sems
        self.stages, self.stage = len(order), 0
        self.step = length >> len(order)

    def upper(self, s):
        return lax.rem(lax.div(self.me, 1 << self.order[s]), 2)

    def rows(self, start, length):
        return pl.ds(pl.multiple_of(start, 16), length)

    def start(self, s):
        at = self.base
        for k in range(s):
            at = at + self.upper(k) * (self.total >> (k + 1))
        return at

    def slot(self, s):
        return self.base + self.total - (self.total >> s)

    def copy(self):
        inward = self.stage < self.stages
        s = self.stage if inward else 2 * self.stages - 1 - self.stage
        bit = 1 << self.order[s]
        peer = {"expert": self.me + bit - 2 * bit * self.upper(s)}
        if inward:
            half = self.total >> (s + 1)
            away = self.start(s) + (1 - self.upper(s)) * half
            src, dst = self.acc.at[self.rows(away, half)], self.rcv.at[pl.ds(self.slot(s), half)]
            send, recv = self.rs_send, self.rs_recv
        else:
            src = dst = self.res.at[self.rows(self.start(s + 1), self.total >> (s + 1))]
            send, recv = self.ag_send, self.ag_recv
        return pltpu.make_async_remote_copy(
            src, dst, send.at[self.index, s], recv.at[self.index, s], device_id=peer, device_id_type=MESH
        )

    def begin(self):
        self.copy().start()

    def advance(self):
        self.copy().wait()
        s = self.stage
        if s < self.stages:
            keep, slot, step = self.start(s + 1), self.slot(s), self.step
            into = self.res if s == self.stages - 1 else self.acc

            def add(b, _):
                at = self.rows(keep + b * step, step)
                into[at, :] = (
                    self.acc[at, :].astype(F32) + self.rcv[self.rows(slot + b * step, step), :].astype(F32)
                ).astype(BF)
                return 0

            lax.fori_loop(0, (self.total >> (s + 1)) // step, add, 0)
        self.stage += 1
        if self.stage < 2 * self.stages:
            self.copy().start()


def back_kernel(
    n, cc, groups, q_ref, k_ref, v_ref, prob_ref, do_ref, o_ref, x_any, norm_any, own_any, oth_any,
    gain_ref, small_ref, pg_own, pg_oth, gmid_any, y_src,
    xg_ref, small_out, sum_q, sum_p, z1, z2,
    x_ref, norm_t, own_ref, oth_ref, dk_s, dv_s, gh_s, gnp_s, acc, rcv, res, p_acc, p_rcv, p_res, got, pgot, snd, mine_s, small_got,
    send, recv, local, dsend, drecv, rs_send, rs_recv, ag_send, ag_recv, sm_send, sm_recv, out_sem,
):
    step = pl.program_id(0)
    tokens, width = x_ref.shape
    half = own_ref.shape[2]
    scale = HEAD_DIM ** -0.5
    last = 3 * groups
    kind, group = lax.rem(step, 3), lax.div(step, 3)
    me = lax.axis_index("expert")
    stages = n.bit_length() - 1
    routes = [
        Route(
            n, lambda e, c=c: y_src.at[c, block_of(e, cc)], lambda d, z=z: z.at[block_of(d, cc)],
            send.at[c - 1], recv.at[c - 1], local.at[c - 1],
        )
        for c, z in ((1, z1), (2, z2))
    ]

    split = 2 if width >= 32 * n else 1
    size = width // split
    sems = (rs_send, rs_recv, ag_send, ag_recv)
    order = list(range(stages))
    swapped = [1, 0, *order[2:]]

    def parts_of(first, at, refs):
        return [
            Part(first + i, at * width + i * size, size, order if i % 2 == 0 else swapped, me, refs, sems)
            for i in range(split)
        ]

    head_parts = [parts_of(k * split, k, (acc, rcv, res)) for k in range(groups)]
    proj_parts = parts_of(groups * split, 0, (p_acc, p_rcv, p_res))

    def dp_swap(k):
        src, dst = (snd.at[k], got.at[k]) if k < groups else (pg_oth, pgot)
        return to_partner(src, dst, dsend.at[k], drecv.at[k])

    def bring_to(parts, goal):
        while parts[0].stage < min(goal, 2 * stages):
            for p in parts:
                p.advance()

    def fetch(k):
        src = (gmid_any, norm_any, own_any, oth_any, x_any)[k]
        dst = (xg_ref, norm_t, own_ref, oth_ref, x_ref)[k]
        return pltpu.make_async_copy(src, dst, out_sem.at[2 + k])

    @pl.when(step == 0)
    def _():
        greet(n, True)
        dp_swap(groups).start()
        for r in routes:
            r.start()
        for k in (1, 2, 3, 4, 0):
            fetch(k).start()

    @pl.when((kind < 2) & (step < last))
    def _():
        side, lanes = 1 - kind, block_of(group, 128)
        dk_s[...] = jnp.zeros_like(dk_s)
        dv_s[...] = jnp.zeros_like(dv_s)
        for i in range(BLOCKS):
            w, s = WIDTH[i], START[i]
            at = slice(i * QB, (i + 1) * QB)
            keys, values = k_ref[0, s:s + w, :], v_ref[0, s:s + w, :]
            go = do_ref[at, :]
            prod = go.astype(F32) * o_ref[at, :].astype(F32)
            query = q_ref[0, at, :]
            query, go_two = two_heads(query), two_heads(go)
            inner = jnp.concatenate(
                [jnp.sum(jnp.where(lane_pick(128, j == 0), prod, 0.0), axis=-1, keepdims=True) for j in range(2)], axis=0
            )
            probs = prob_ref[:, :, OFFSET[i]:OFFSET[i] + w].reshape(2 * QB, w)
            gp = dot_nt(go_two, values)
            gs = (probs.astype(F32) * (gp - inner)).astype(BF)
            gq = dot(gs, keys)
            dk_s[s:s + w, :] += dot_tn(gs, query)
            dv_s[s:s + w, :] += dot_tn(probs, go_two)
            gh_s[3 * side, at, lanes] = (jnp.where(lane_pick(128, True), gq[0:QB], gq[QB:2 * QB]) * scale).astype(BF)
        gh_s[3 * side + 1, :, lanes] = (dk_s[...] * scale).astype(BF)
        gh_s[3 * side + 2, :, lanes] = dv_s[...].astype(BF)

    for k in range(groups):
        @pl.when(step == 3 * k + 2)
        def _():
            if k == 0:
                fetch(1).wait()
            at = slice(k * 128, (k + 1) * 128)
            for c in range(3):
                both = dot(norm_t[...], jnp.concatenate([gh_s[3 + c, :, at], gh_s[c, :, at]], axis=1))
                snd[k, :, c * 128:(c + 1) * 128] = both[:, 0:128].astype(BF)
                mine_s[:, c * 128:(c + 1) * 128] = both[:, 128:256]
            dp_swap(k).start()

        @pl.when(step == 3 * k + 3)
        def _():
            dp_swap(k).wait()
            acc[k * width:(k + 1) * width, :] = (mine_s[...] + got[k].astype(F32)).astype(BF)
            for p in head_parts[k]:
                p.begin()

    @pl.when(step == 1)
    def _():
        dp_swap(groups).wait()
        rows = pgot.shape[0]
        for b in range(width // rows):
            at = slice(b * rows, (b + 1) * rows)
            p_acc[at, :] = (pg_own[:, at].astype(F32) + pgot[:, at].astype(F32)).astype(BF)
        for p in proj_parts:
            p.begin()

    for t in range(3, last):
        @pl.when(step == t)
        def _():
            bring_to(proj_parts, sum(t >= m for m in (5, 7, 9, 11)))
            for k in range(groups):
                bring_to(head_parts[k], sum(t >= 3 * k + m for m in (7, 9, 11)))

    @pl.when(step == last)
    def _():
        def small_swap(k):
            if k == 0:
                peer = {"dp": 1 - lax.axis_index("dp")}
            else:
                bit = 1 << (k - 1)
                peer = {"expert": me + bit - 2 * bit * lax.rem(lax.div(me, bit), 2)}
            return pltpu.make_async_remote_copy(
                small_out, small_got.at[k], sm_send.at[k], sm_recv.at[k], device_id=peer, device_id_type=MESH
            )

        def turn():
            for some in [proj_parts, *head_parts]:
                for p in some:
                    if p.stage < 2 * stages:
                        p.advance()

        fetch(2).wait()
        fetch(3).wait()
        for c in range(3):
            if c:
                turn()
            term = dot_nt(gh_s[c], own_ref[c]) + dot_nt(gh_s[3 + c], oth_ref[c])
            if c:
                gnp_s[...] += term
            else:
                gnp_s[...] = term
        turn()
        fetch(0).wait()
        fetch(4).wait()
        small_out[...] = small_ref[...]

        def body(b, _):
            at = block_of(b, 128)
            grad = gnp_s[at, :]
            unit, inverse = unit_of(x_ref[at, :].astype(F32))
            xg_ref[at, :] = xg_ref[at, :] + norm_back(grad, unit, inverse, row_of(gain_ref))
            small_out[0:1, :] += jnp.sum(grad * unit, axis=0, keepdims=True)
            small_out[1:2, :] += jnp.sum(grad, axis=0, keepdims=True)
            return 0

        lax.fori_loop(0, tokens // 128, body, 0)
        small = small_swap(0)
        small.start()
        for s in range(2 * stages - 2):
            turn()
            if s <= stages:
                small.wait()
                small_out[...] += small_got[s]
                if s < stages:
                    small = small_swap(s + 1)
                    small.start()
        outs = [
            pltpu.make_async_copy(res, sum_q, out_sem.at[0]),
            pltpu.make_async_copy(p_res, sum_p, out_sem.at[1]),
        ]
        for out in outs:
            out.start()
        for out in outs:
            out.wait()
        for r in routes:
            r.wait()


def back_call(n, cc, head_rows, probs, gatt, att, x, norm_t, own, oth, gmid, gain, small, pg_own, pg_oth, y):
    tokens, width = x.shape
    half = own.shape[2]
    groups = half // 128
    last = 3 * groups
    rows = n * cc
    stages = n.bit_length() - 1
    parts = (groups + 1) * (2 if width >= 32 * n else 1)
    sds, dma, once = jax.ShapeDtypeStruct, pltpu.SemaphoreType.DMA, pl.Buffered(1)

    def place(i):
        i = jnp.minimum(i, last - 1)
        return jnp.maximum(1 - i % 3, 0), i // 3

    def head(c):
        def index(i):
            side, k = place(i)
            return (3 * side + c, 0, k)

        return pl.BlockSpec((1, tokens, 128), index)

    def pair(i):
        side, k = place(i)
        return side * groups + k

    def fixed(shape):
        return pl.BlockSpec(shape, lambda *_: (0,) * len(shape), pipeline_mode=once)

    cols = pl.BlockSpec((tokens, 128), lambda i: (0, pair(i)))
    sums = pltpu.VMEM((groups * width, 384), BF)
    p_sums = pltpu.VMEM((width, half), BF)
    return pl.pallas_call(
        functools.partial(back_kernel, n, cc, groups),
        grid=(last + 1,),
        in_specs=[
            head(0), head(1), head(2), pl.BlockSpec((2, QB, BAND), lambda i: (pair(i), 0, 0)), cols, cols,
            ANY, ANY, ANY, ANY,
            fixed((width,)), fixed(small.shape), fixed((half, width)), ANY, ANY, ANY,
        ],
        out_specs=[fixed((tokens, width)), fixed(small.shape), ANY, ANY, ANY, ANY],
        out_shape=[
            sds((tokens, width), F32), sds(small.shape, F32), sds((groups * width, 384), BF), sds((width, half), BF),
            sds((rows, width), BF), sds((rows, width), BF),
        ],
        scratch_shapes=[
            pltpu.VMEM((tokens, width), BF), pltpu.VMEM((width, tokens), BF), pltpu.VMEM(own.shape, BF), pltpu.VMEM(oth.shape, BF),
            pltpu.VMEM((tokens, 128), F32), pltpu.VMEM((tokens, 128), F32), pltpu.VMEM((6, tokens, half), BF),
            pltpu.VMEM((tokens, width), F32), sums, sums, sums, p_sums, p_sums, p_sums,
            pltpu.VMEM((groups, width, 384), BF), pltpu.VMEM((half, width), BF),
            pltpu.VMEM((groups, width, 384), BF), pltpu.VMEM((width, 384), F32),
            pltpu.VMEM((1 + stages, *small.shape), F32),
            *route_sems(n, 2), dma((groups + 1,)), dma((groups + 1,)), dma((parts, stages)), dma((parts, stages)),
            dma((parts, stages)), dma((parts, stages)), dma((1 + stages,)), dma((1 + stages,)), dma((7,)),
        ],
        compiler_params=params(collective_id=5, has_side_effects=True),
        cost_estimate=cost(5.3e10, 9e7),
        name="back",
    )(
        head_rows, head_rows, head_rows, probs, gatt, att, x, norm_t, own, oth, gain, small, pg_own, pg_oth, gmid, y
    )


def result_kernel(tcol_ref, z0, z1, z2, mid_ref, sum_q, sum_p, xg_ref, wd_ref, wu_ref, small_ref, out_ref, q_ref, p_ref, xo_ref, do_ref, uo_ref, *smalls):
    rows = gather_rows(tcol_ref[...], (z0[...], z1[...], z2[...]))
    out_ref[...] = (mid_ref[...] + rows.astype(BF).astype(F32)).astype(BF)
    for c in range(3):
        for k in range(sum_q.shape[0]):
            q_ref[c, :, k * 128:(k + 1) * 128] = sum_q[k, :, c * 128:(c + 1) * 128].astype(F32)
    half = sum_p.shape[2]
    for b in range(sum_p.shape[0]):
        p_ref[:, b * half:(b + 1) * half] = sum_p[b].astype(F32)
    xo_ref[...] = xg_ref[...]
    do_ref[...] = wd_ref[...].astype(F32)
    uo_ref[...] = wu_ref[...].astype(F32)
    for k, small in enumerate(smalls):
        small[...] = small_ref[k:k + 1, :].reshape(small.shape)


def result_call(tcol, zs, middle, sum_q, sum_p, xg, wd, wu, small):
    tokens, width = middle.shape
    half = sum_p.shape[1]
    groups = half // 128
    hid = wd.shape[0]
    rows = zs[0].shape[0]
    steps = 8
    tb, qb, pb, wb = tokens // steps, width // steps, half // steps, hid // steps
    sds = jax.ShapeDtypeStruct
    sum_q = sum_q.reshape(groups, width, 384)
    sum_p = sum_p.reshape(width // half, half, half)

    def rows_of(size, cols):
        return pl.BlockSpec((size, cols), lambda i: (i, 0))

    return pl.pallas_call(
        result_kernel,
        grid=(steps,),
        in_specs=[
            rows_of(tb, 128), *[whole((rows, width))] * 3, rows_of(tb, width),
            pl.BlockSpec((groups, qb, 384), lambda i: (0, i, 0)),
            pl.BlockSpec((width // half, pb, half), lambda i: (0, i, 0)), rows_of(tb, width), rows_of(wb, width),
            rows_of(wb, width), whole(small.shape),
        ],
        out_specs=[
            rows_of(tb, width), pl.BlockSpec((3, qb, half), lambda i: (0, i, 0)), rows_of(pb, width),
            rows_of(tb, width), rows_of(wb, width), rows_of(wb, width), *[whole((width,))] * 5,
        ],
        out_shape=[
            sds((tokens, width), BF), sds((3, width, half), F32), sds((half, width), F32), sds((tokens, width), F32),
            sds((hid, width), F32), sds((hid, width), F32), *[sds((width,), F32)] * 5,
        ],
        compiler_params=params(),
        cost_estimate=cost(6 * tokens * rows * width, 6e7),
        name="results",
    )(tcol, *zs, middle, sum_q, sum_p, xg, wd, wu, small)


def on_device(
    tokens, cotangent, segment_ids, expert_ids, qkv_weight, proj_weight, proj_bias, pre_gain, pre_shift,
    mid_gain, mid_shift, up_weight, up_bias, down_weight, down_bias,
):
    n = lax.axis_size("expert")
    count, width = tokens.shape
    cc = 3 * count // (2 * n) // CHUNKS

    def swap(v):
        return lax.ppermute(v, "dp", [(0, 1), (1, 0)])

    down_own, up_own = down_weight[0], up_weight[0]
    up, down = (up_own, swap(up_own)), (down_own, swap(down_own))
    bias = (up_bias, swap(up_bias))
    vectors = (pre_gain, pre_shift, proj_bias, mid_gain, mid_shift)

    tcol, norm_t, head_rows, att, att_t, probs, middle, mid_slots, cot_rows, qkv_oth, proj_oth = front_call(
        n, cc, expert_ids.reshape(1, count), cotangent, tokens, segment_ids, vectors, qkv_weight, proj_weight)
    acts, ghs, ub, y, dx, arrived, gm0 = expert_call(n, cc, mid_slots, cot_rows, up, down, bias, down_bias)
    down_grad, up_grad, upbias_grad, downbias_grad, gm1, gm2 = wgrad_call(n, cc, acts, ghs, cot_rows, arrived, ub, dx)

    gmid, gatt, pg_own, pg_oth, small, z0 = middle_back_call(
        n, cc, tcol, (gm0, gm1, gm2), middle, cotangent, mid_gain, proj_weight, proj_oth, att_t, y)
    input_grad, small, sum_q, sum_p, z1, z2 = back_call(
        n, cc, head_rows, probs, gatt, att, tokens, norm_t, qkv_weight, qkv_oth, gmid, pre_gain, small, pg_own, pg_oth, y)
    output, qkv_grad, proj_grad, input_grad, down_grad, up_grad, pregain, preshift, midgain, midshift, projbias = result_call(
        tcol, (z0, z1, z2), middle, sum_q, sum_p, input_grad, down_grad, up_grad, small)
    return (
        output, input_grad, qkv_grad, proj_grad, projbias, pregain, preshift, midgain, midshift,
        up_grad[None], upbias_grad, down_grad[None], downbias_grad,
    )


def solution(mesh):
    token = P(("dp", "expert"), None)
    in_specs = (
        token, token, token, token, P(None, None, "dp"), P("dp", None), P(), P(), P(), P(), P(),
        P("expert", "dp", None), P("expert", "dp"), P("expert", "dp", None), P("expert", None),
    )
    out_specs = (
        token, token, P(None, None, "dp"), P("dp", None), P(), P(), P(), P(), P(),
        P("expert", "dp", None), P("expert", "dp"), P("expert", "dp", None), P("expert", None),
    )
    return jax.shard_map(on_device, mesh=mesh, in_specs=in_specs, out_specs=out_specs, check_vma=False)
```

```python
import functools

import jax
import jax.numpy as jnp
from jax import lax
from jax.experimental import pallas as pl
from jax.experimental.pallas import tpu as pltpu
from jax.sharding import PartitionSpec as P

HEAD_DIM = 64
SEQ = 1024
DOC_MAX = 512
EPS = 1e-05
QB = 256
CHUNKS = 3
BF = jnp.bfloat16
F32 = jnp.float32
MESH = pl.DeviceIdType.MESH
VMEM_LIMIT = 60 * 1024 * 1024

BLOCKS = SEQ // QB
START = [max(0, i * QB - DOC_MAX) for i in range(BLOCKS)]
WIDTH = [(i + 1) * QB - START[i] for i in range(BLOCKS)]
OFFSET = [sum(WIDTH[:i]) for i in range(BLOCKS)]
BAND = sum(WIDTH)


def dot(a, b):
    return jnp.dot(a, b, preferred_element_type=F32)


def dot_nt(a, b):
    return lax.dot_general(a, b, (((1,), (1,)), ((), ())), preferred_element_type=F32)


def dot_tn(a, b):
    return lax.dot_general(a, b, (((0,), (0,)), ((), ())), preferred_element_type=F32)


def params(**kw):
    return pltpu.CompilerParams(vmem_limit_bytes=VMEM_LIMIT, **kw)


def cost(flops, nbytes, trans=0):
    return pl.CostEstimate(flops=int(flops), bytes_accessed=int(nbytes), transcendentals=int(trans))


ANY = pl.BlockSpec(memory_space=pl.ANY)


def whole(shape):
    return pl.BlockSpec(shape, lambda *_: (0,) * len(shape))


def block_of(index, size):
    return pl.ds(pl.multiple_of(index * size, size), size)


class Route:
    def __init__(self, n, src, dst, send, recv, local):
        self.n, self.src, self.dst = n, src, dst
        self.send, self.recv, self.local = send, recv, local

    def remote(self):
        me = lax.axis_index("expert")
        for d in range(1, self.n):
            there = lax.rem(me + d, self.n)
            yield pltpu.make_async_remote_copy(
                self.src(there), self.dst(me), self.send.at[d], self.recv.at[d],
                device_id={"expert": there}, device_id_type=MESH,
            )

    def own(self):
        me = lax.axis_index("expert")
        return pltpu.make_async_copy(self.src(me), self.dst(me), self.local)

    def start(self):
        for c in self.remote():
            c.start()
        self.own().start()

    def wait(self):
        self.own().wait()
        for c in self.remote():
            c.wait()


def route_sems(n, count):
    return [
        pltpu.SemaphoreType.DMA((count, n)),
        pltpu.SemaphoreType.DMA((count, n)),
        pltpu.SemaphoreType.DMA((count,)),
    ]


def greet(n, partner):
    me = lax.axis_index("expert")
    barrier = pltpu.get_barrier_semaphore()
    for d in range(1, n):
        pl.semaphore_signal(
            barrier, inc=1, device_id={"expert": lax.rem(me + d, n)}, device_id_type=MESH
        )
    if partner:
        pl.semaphore_signal(barrier, inc=1, device_id={"dp": 1 - lax.axis_index("dp")}, device_id_type=MESH)
    pl.semaphore_wait(barrier, n if partner else n - 1)


def to_partner(src, dst, send, recv):
    return pltpu.make_async_remote_copy(
        src, dst, send, recv, device_id={"dp": 1 - lax.axis_index("dp")}, device_id_type=MESH
    )


def unit_of(values):
    centre = values - jnp.mean(values, axis=-1, keepdims=True)
    inverse = lax.rsqrt(jnp.mean(centre * centre, axis=-1, keepdims=True) + EPS)
    return centre * inverse, inverse


def lane_pick(width, first):
    lanes = lax.broadcasted_iota(jnp.int32, (1, width), 1)
    return (lanes < HEAD_DIM) if first else (lanes >= HEAD_DIM)


def two_heads(rows):
    return jnp.concatenate([jnp.where(lane_pick(128, j == 0), rows, BF(0)) for j in range(2)], axis=0)


def row_of(ref):
    return ref[...].astype(F32).reshape(1, ref.shape[0])


def front_kernel(
    n, cc, pairs, ids_ref, cot_ref, x_any, seg_ref, pre_gain, pre_shift, proj_bias, mid_gain, mid_shift, w_ref, w_any, p_any,
    tcol_ref, norm_t, hr_ref, att_ref, att_t, prob_ref, mid_ref, slot_ref, arr_ref, wo_out, po_out,
    x_ref, p_ref, row_s, cs_s, norm_s, hr_s, wo_s, po_s, bias_s, low_s, send, recv, local, dsend, drecv, dlocal,
):
    step = pl.program_id(0)
    tokens, width = x_ref.shape
    half = p_ref.shape[0]
    rows = n * cc
    first_pair = 7
    routes = [
        Route(
            n, lambda e, c=c: cs_s.at[block_of(c * n + e, cc)], lambda d, c=c: arr_ref.at[c, block_of(d, cc)],
            send.at[c], recv.at[c], local.at[c],
        )
        for c in range(CHUNKS)
    ]

    def swaps():
        return [
            to_partner(w_any, wo_s, dsend.at[0], drecv.at[0]),
            to_partner(p_any, po_s, dsend.at[1], drecv.at[1]),
        ]

    def keeps():
        return [
            pltpu.make_async_copy(wo_s, wo_out, dlocal.at[0]),
            pltpu.make_async_copy(po_s, po_out, dlocal.at[1]),
        ]

    def loads():
        return [
            pltpu.make_async_copy(x_any, x_ref, dlocal.at[2]),
            pltpu.make_async_copy(p_any, p_ref, dlocal.at[3]),
        ]

    @pl.when(step == 0)
    def _():
        for c in loads():
            c.start()
        greet(n, True)
        for c in swaps():
            c.start()
        ids = jnp.transpose(jnp.broadcast_to(ids_ref[...].astype(F32), (128, tokens)))
        hot = (ids == lax.broadcasted_iota(jnp.int32, (tokens, 128), 1).astype(F32)).astype(F32)
        low_hot = hot.astype(BF)
        place = []
        for b in range(tokens // 256):
            span = (b + 1) * 256
            lower = (
                lax.broadcasted_iota(jnp.int32, (256, span), 0) + b * 256
                >= lax.broadcasted_iota(jnp.int32, (256, span), 1)
            ).astype(F32).astype(BF)
            counts = dot(lower, low_hot[0:span])
            rank = jnp.sum(counts * hot[b * 256:span], axis=1, keepdims=True) - 1.0
            chunk = jnp.floor((rank + 0.5) * (1.0 / cc))
            place.append(chunk * rows + ids[b * 256:span] * cc + (rank - chunk * cc))
        place = jnp.concatenate(place, axis=0)
        tcol_ref[...] = place.astype(jnp.int32)
        row_s[...] = jnp.transpose(place)[0:8, :].astype(jnp.int32)

        def fill(b, _):
            hot = (
                lax.broadcasted_iota(jnp.int32, (256, tokens), 0) + b * 256 == row_s[0:1, :]
            ).astype(F32).astype(BF)
            cs_s[block_of(b, 256), :] = dot(hot, cot_ref[...]).astype(BF)
            return 0

        for c, r in enumerate(routes):
            lax.fori_loop(c * rows // 256, (c + 1) * rows // 256, fill, 0)
            r.start()

        for c in loads():
            c.wait()
        gain, shift = row_of(pre_gain), row_of(pre_shift)

        def body(b, _):
            at = block_of(b, 128)
            unit, _ = unit_of(x_ref[at, :].astype(F32))
            low = (unit * gain + shift).astype(BF)
            norm_s[at, :] = low
            norm_t[:, at] = jnp.transpose(low)
            return 0

        lax.fori_loop(0, tokens // 128, body, 0)

    @pl.when((step >= 1) & (step <= 3))
    def _():
        out = dot(norm_s[...], w_ref[0]).astype(BF)
        hr_ref[0] = out
        hr_s[step - 1] = out

    @pl.when(step == 4)
    def _():
        for c in swaps():
            c.wait()
        for c in keeps():
            c.start()

    @pl.when((step >= 4) & (step <= 6))
    def _():
        out = dot(norm_s[...], wo_s[step - 4]).astype(BF)
        hr_ref[0] = out
        hr_s[step - 1] = out

    @pl.when(step == first_pair)
    def _():
        seg = seg_ref[...].astype(F32)
        seg_col = jnp.transpose(jnp.broadcast_to(seg, (128, tokens)))
        for i in range(BLOCKS):
            w, s = WIDTH[i], START[i]
            at_row = lax.broadcasted_iota(jnp.int32, (QB, w), 0) + i * QB
            at_key = lax.broadcasted_iota(jnp.int32, (QB, w), 1) + s
            same = seg_col[i * QB:(i + 1) * QB, 0:1] == seg[:, s:s + w]
            bias_s[:, OFFSET[i]:OFFSET[i] + w] = jnp.where(same & (at_key <= at_row), 0.0, -1e30)

    @pl.when((step >= first_pair) & (step < first_pair + pairs))
    def _():
        pair = step - first_pair
        per = half // 128
        side, lanes = lax.div(pair, per), block_of(lax.rem(pair, per), 128)
        query = hr_s[3 * side, :, lanes] * BF(HEAD_DIM ** -0.5)
        for i in range(BLOCKS):
            w, s = WIDTH[i], START[i]
            keys, values = hr_s[3 * side + 1, s:s + w, lanes], hr_s[3 * side + 2, s:s + w, lanes]
            bias = bias_s[:, OFFSET[i]:OFFSET[i] + w]
            scores = dot_nt(two_heads(query[i * QB:(i + 1) * QB]), keys)
            parts = []
            for j in range(2):
                masked = scores[j * QB:(j + 1) * QB] + bias
                top = jnp.max(masked, axis=-1, keepdims=True)
                weights = jnp.exp(masked - top)
                probs = (weights * (1.0 / jnp.sum(weights, axis=-1, keepdims=True))).astype(BF)
                prob_ref[j, :, OFFSET[i]:OFFSET[i] + w] = probs
                parts.append(probs)
            out = dot(jnp.concatenate(parts, axis=0), values)
            both = jnp.where(lane_pick(128, True), out[0:QB], out[QB:2 * QB])
            both = both.astype(BF)
            att_ref[i * QB:(i + 1) * QB, block_of(pair, 128)] = both
            att_t[block_of(pair, 128), i * QB:(i + 1) * QB] = jnp.transpose(both)

    @pl.when(step == first_pair + pairs)
    def _():
        pbias, gain, shift = row_of(proj_bias), row_of(mid_gain), row_of(mid_shift)

        def body(b, _):
            at = block_of(b, 128)
            branch = dot(att_ref[at, 0:half], p_ref[...]) + dot(att_ref[at, half:2 * half], po_s[...])
            middle = x_ref[at, :].astype(F32) + branch + pbias
            mid_ref[at, :] = middle
            unit, _ = unit_of(middle)
            low_s[at, :] = (unit * gain + shift).astype(BF)
            return 0

        lax.fori_loop(0, tokens // 128, body, 0)

        def fill(b, _):
            hot = (
                lax.broadcasted_iota(jnp.int32, (256, tokens), 0) + b * 256 == row_s[0:1, :]
            ).astype(F32).astype(BF)
            slot_ref[block_of(b, 256), :] = dot(hot, low_s[...]).astype(BF)
            return 0

        lax.fori_loop(0, CHUNKS * rows // 256, fill, 0)
        for c in keeps():
            c.wait()
        for r in routes:
            r.wait()


def front_call(n, cc, ids, cot, x, seg, vectors, qkv, proj):
    tokens, width = x.shape
    half = proj.shape[0]
    pairs = width // 128
    rows = n * cc
    dma = pltpu.SemaphoreType.DMA
    sds = jax.ShapeDtypeStruct

    def pair_of(i):
        return jnp.clip(i - 7, 0, pairs - 1)

    return pl.pallas_call(
        functools.partial(front_kernel, n, cc, pairs),
        grid=(8 + pairs,),
        in_specs=[
            whole((1, tokens)), whole((tokens, width)), ANY, whole((1, tokens)),
            *[whole((width,))] * 5,
            pl.BlockSpec((1, width, half), lambda i: (jnp.clip(i - 1, 0, 2), 0, 0)), ANY,
            ANY,
        ],
        out_specs=[
            whole((tokens, 128)), whole((width, tokens)),
            pl.BlockSpec((1, tokens, half), lambda i: (jnp.clip(i - 1, 0, 5), 0, 0)),
            whole((tokens, width)), whole((width, tokens)), pl.BlockSpec((2, QB, BAND), lambda i: (pair_of(i), 0, 0)),
            whole((tokens, width)), whole((CHUNKS * rows, width)), ANY, ANY, ANY,
        ],
        out_shape=[
            sds((tokens, 128), jnp.int32), sds((width, tokens), BF), sds((6, tokens, half), BF),
            sds((tokens, width), BF), sds((width, tokens), BF), sds((2 * pairs, QB, BAND), BF), sds((tokens, width), F32),
            sds((CHUNKS * rows, width), BF), sds((CHUNKS, rows, width), BF), sds(qkv.shape, BF), sds(proj.shape, BF),
        ],
        scratch_shapes=[
            pltpu.VMEM((tokens, width), BF), pltpu.VMEM((half, width), BF),
            pltpu.VMEM((8, tokens), jnp.int32), pltpu.VMEM((CHUNKS * rows, width), BF),
            pltpu.VMEM((tokens, width), BF), pltpu.VMEM((6, tokens, half), BF), pltpu.VMEM(qkv.shape, BF),
            pltpu.VMEM(proj.shape, BF), pltpu.VMEM((QB, BAND), F32), pltpu.VMEM((tokens, width), BF),
            *route_sems(n, CHUNKS), dma((2,)), dma((2,)), dma((4,)),
        ],
        compiler_params=params(collective_id=1, has_side_effects=True),
        cost_estimate=cost(3e10, 6e7),
        name="front",
    )(ids, cot, x, seg, *vectors, qkv, qkv, proj)


GELU_C = 0.7978845608028654
GELU_A = 0.044715
TILE = 512


def expert_kernel(
    n, cc, own_tiles, mid_ref, c_any, uo_ref, ut_ref, do_ref, dt_ref, bo_ref, bt_ref, db_ref,
    act_ref, gh_ref, ub_ref, y_ref, dx_ref, x_out, back_out,
    c_ref, x_s, g_s, y_s, dx_s, dxb_s, send, recv, local, xsem,
):
    step = pl.program_id(0)
    tiles = 2 * own_tiles
    phase, tile = lax.div(step, tiles), lax.rem(step, tiles)
    rows = n * cc
    ins = [
        Route(
            n, lambda e, c=c: mid_ref.at[block_of(c * n + e, cc)], lambda d, c=c: x_s.at[c, block_of(d, cc)],
            send.at[c], recv.at[c], local.at[c],
        )
        for c in range(CHUNKS)
    ]
    back = Route(
        n, lambda e: dxb_s.at[block_of(e, cc)], lambda d: back_out.at[block_of(d, cc)],
        send.at[CHUNKS], recv.at[CHUNKS], local.at[CHUNKS],
    )

    def keep(c):
        return pltpu.make_async_copy(x_s.at[c], x_out.at[c], xsem.at[c])

    @pl.when(step == 0)
    def _():
        load = pltpu.make_async_copy(c_any, c_ref, xsem.at[CHUNKS])
        load.start()
        greet(n, False)
        ins[0].start()
        ub_ref[...] = jnp.zeros_like(ub_ref)
        load.wait()

    for c in range(CHUNKS):
        @pl.when(step == (c + 1) * tiles)
        def _():
            ins[c].wait()
            (ins[c + 1] if c + 1 < CHUNKS else back).start()
            keep(c).start()

    lanes = block_of(tile, TILE)

    def early(down_ref):
        for c in range(CHUNKS):
            g_s[c, :, lanes] = dot_nt(c_ref[c], down_ref[...]).astype(BF)

    def late(c, up_ref, down_ref, b_ref):
        up, down = up_ref[...], down_ref[...]
        h = dot_nt(x_s[c], up) + b_ref[...].astype(F32)
        sq = h * h
        t = jnp.tanh(GELU_C * (h + GELU_A * (sq * h)))
        act = ((0.5 * h) * (1.0 + t)).astype(BF)
        act_ref[0] = act
        slope = 0.5 * (1.0 + t) + (0.5 * h) * ((1.0 - t * t) * (GELU_C * (1.0 + (3.0 * GELU_A) * sq)))
        gh = (g_s[c, :, lanes].astype(F32) * slope).astype(BF)
        gh_ref[0] = gh
        ub_ref[0:1, lanes] += jnp.sum(gh.astype(F32), axis=0, keepdims=True)
        y_s[...] += dot(act, down)
        dx_s[...] += dot(gh, up)

    @pl.when((phase >= 1) & (tile == 0))
    def _():
        y_s[...] = jnp.broadcast_to(db_ref[...].astype(F32), y_s.shape)
        dx_s[...] = jnp.zeros_like(dx_s)

    @pl.when((phase == 0) & (tile < own_tiles))
    def _():
        early(do_ref)

    @pl.when((phase == 0) & (tile >= own_tiles))
    def _():
        early(dt_ref)

    @pl.when((phase >= 1) & (tile < own_tiles))
    def _():
        late(phase - 1, uo_ref, do_ref, bo_ref)

    @pl.when((phase >= 1) & (tile >= own_tiles))
    def _():
        late(phase - 1, ut_ref, dt_ref, bt_ref)

    @pl.when((phase >= 1) & (tile == tiles - 1))
    def _():
        y_ref[0] = y_s[...].astype(BF)
        dx_ref[0] = dx_s[...].astype(BF)

    @pl.when((phase == 1) & (tile == tiles - 1))
    def _():
        dxb_s[...] = dx_s[...].astype(BF)

    @pl.when(step == (CHUNKS + 1) * tiles - 1)
    def _():
        for c in range(CHUNKS):
            keep(c).wait()
        back.wait()


def expert_call(n, cc, mid_slots, cot, up, down, bias, down_bias):
    up_own, up_oth = up
    down_own, down_oth = down
    b_own, b_oth = bias
    rows = n * cc
    hid, width = up_own.shape
    own_tiles = hid // TILE
    tiles = 2 * own_tiles
    sds = jax.ShapeDtypeStruct

    def first(i):
        return jnp.minimum(i % tiles, own_tiles - 1)

    def second(i):
        return jnp.maximum(i % tiles - own_tiles, 0)

    def up_first(i):
        return jnp.where(i < tiles, 0, first(i))

    def up_second(i):
        return jnp.where(i < tiles, 0, second(i))

    def chunk(i):
        return jnp.maximum(i // tiles - 1, 0)

    def column(i):
        return jnp.where(i < tiles, 0, i % tiles)

    col = pl.BlockSpec((1, rows, TILE), lambda i: (chunk(i), 0, column(i)))
    per_chunk = pl.BlockSpec((1, rows, width), lambda i: (chunk(i), 0, 0))
    return pl.pallas_call(
        functools.partial(expert_kernel, n, cc, own_tiles),
        grid=((CHUNKS + 1) * tiles,),
        in_specs=[
            ANY, ANY,
            pl.BlockSpec((TILE, width), lambda i: (up_first(i), 0)),
            pl.BlockSpec((TILE, width), lambda i: (up_second(i), 0)),
            pl.BlockSpec((TILE, width), lambda i: (first(i), 0)),
            pl.BlockSpec((TILE, width), lambda i: (second(i), 0)),
            pl.BlockSpec((1, TILE), lambda i: (0, first(i))),
            pl.BlockSpec((1, TILE), lambda i: (0, second(i))),
            whole((1, width)),
        ],
        out_specs=[col, col, whole((8, 2 * hid)), per_chunk, per_chunk, ANY, ANY],
        out_shape=[
            sds((CHUNKS, rows, 2 * hid), BF), sds((CHUNKS, rows, 2 * hid), BF), sds((8, 2 * hid), F32),
            sds((CHUNKS, rows, width), BF), sds((CHUNKS, rows, width), BF), sds((CHUNKS, rows, width), BF),
            sds((rows, width), BF),
        ],
        scratch_shapes=[
            pltpu.VMEM(cot.shape, BF), pltpu.VMEM((CHUNKS, rows, width), BF), pltpu.VMEM((CHUNKS, rows, 2 * hid), BF),
            pltpu.VMEM((rows, width), F32), pltpu.VMEM((rows, width), F32), pltpu.VMEM((rows, width), BF),
            *route_sems(n, CHUNKS + 1), pltpu.SemaphoreType.DMA((CHUNKS + 1,)),
        ],
        compiler_params=params(collective_id=2, has_side_effects=True),
        cost_estimate=cost(5.2e10, 8e7),
        name="experts",
    )(mid_slots, cot, up_own, up_oth, down_own, down_oth, b_own, b_oth, down_bias)


def wgrad_kernel(
    n, cc, tiles, a_ref, g_ref, c_any, x_any, ub_ref, dx_ref,
    do_ref, up_ref, ubg_ref, cbg_ref, back1, back2,
    c_ref, x_ref, out_s, in_s, small_s, got_s, send, recv, local, dsend, drecv, ssend, srecv, lsem,
):
    step = pl.program_id(0)
    hid = ubg_ref.shape[1]
    routes = [
        Route(
            n, lambda e, c=c: dx_ref.at[c, block_of(e, cc)], lambda d, dst=dst: dst.at[block_of(d, cc)],
            send.at[k], recv.at[k], local.at[k],
        )
        for k, (c, dst) in enumerate(((1, back1), (2, back2)))
    ]

    def swap(k):
        return to_partner(out_s.at[k], in_s.at[k], dsend.at[k], drecv.at[k])

    small = to_partner(small_s, got_s, ssend, srecv)

    def loads():
        return [
            pltpu.make_async_copy(c_any, c_ref, lsem.at[0]),
            pltpu.make_async_copy(x_any, x_ref, lsem.at[1]),
        ]

    @pl.when(step == 0)
    def _():
        for c in loads():
            c.start()
        greet(n, True)
        for r in routes:
            r.start()
        loads()[0].wait()
        total = jnp.zeros((1, c_ref.shape[2]), F32)
        for c in range(CHUNKS):
            total = total + jnp.sum(c_ref[c].astype(F32), axis=0, keepdims=True)
        small_s[...] = jnp.zeros_like(small_s)
        small_s[0:1, 0:hid] = ub_ref[0:1, hid:2 * hid]
        small_s[0:1, hid:hid + total.shape[1]] = total
        small.start()

    @pl.when(step == 2 * tiles)
    def _():
        small.wait()
        ubg_ref[...] = ub_ref[0:1, 0:hid] + got_s[0:1, 0:hid]
        cbg_ref[...] = small_s[0:1, hid:] + got_s[0:1, hid:]

    def product(left, right):
        total = dot_tn(left[0], right[0])
        for c in range(1, CHUNKS):
            total = total + dot_tn(left[c], right[c])
        return total

    for k in range(2 * tiles):
        @pl.when(step == k)
        def _():
            left, right = (a_ref, c_ref) if k < tiles else (g_ref, x_ref)
            if k == tiles:
                loads()[1].wait()
            out_s[k] = product(left, right).astype(BF)
            swap(k).start()

        @pl.when(step == 2 * tiles + k)
        def _():
            left, right, out = (a_ref, c_ref, do_ref) if k < tiles else (g_ref, x_ref, up_ref)
            total = product(left, right)
            swap(k).wait()
            out[...] = (total + in_s[k].astype(F32)).astype(BF)

    @pl.when(step == 4 * tiles - 1)
    def _():
        for r in routes:
            r.wait()


def wgrad_call(n, cc, acts, ghs, cot, rows_in, ub, dx):
    _, rows, width = cot.shape
    hid = acts.shape[2] // 2
    tiles = hid // TILE
    dma = pltpu.SemaphoreType.DMA
    sds = jax.ShapeDtypeStruct

    def first(i):
        return jnp.minimum(i % (2 * tiles), tiles - 1)

    def second(i):
        return jnp.maximum(i % (2 * tiles) - tiles, 0)

    def other(i):
        return jnp.where(i < 2 * tiles, tiles, 0)

    a_spec = pl.BlockSpec((CHUNKS, rows, TILE), lambda i: (0, 0, other(i) + first(i)))
    g_spec = pl.BlockSpec((CHUNKS, rows, TILE), lambda i: (0, 0, other(i) + second(i)))

    def late(i):
        return jnp.where(i < 2 * tiles, 0, 1)

    d_spec = pl.BlockSpec((TILE, width), lambda i: (late(i) * first(i), 0))
    u_spec = pl.BlockSpec((TILE, width), lambda i: (late(i) * second(i), 0))
    return pl.pallas_call(
        functools.partial(wgrad_kernel, n, cc, tiles),
        grid=(4 * tiles,),
        in_specs=[a_spec, g_spec, ANY, ANY, whole(ub.shape), ANY],
        out_specs=[d_spec, u_spec, whole((1, hid)), whole((1, width)), ANY, ANY],
        out_shape=[
            sds((hid, width), BF), sds((hid, width), BF), sds((1, hid), F32), sds((1, width), F32),
            sds((rows, width), BF), sds((rows, width), BF),
        ],
        scratch_shapes=[
            pltpu.VMEM(cot.shape, BF), pltpu.VMEM(rows_in.shape, BF), pltpu.VMEM((2 * tiles, TILE, width), BF), pltpu.VMEM((2 * tiles, TILE, width), BF),
            pltpu.VMEM((8, hid + width), F32), pltpu.VMEM((8, hid + width), F32),
            *route_sems(n, 2), dma((2 * tiles,)), dma((2 * tiles,)), dma, dma, dma((2,)),
        ],
        compiler_params=params(collective_id=3, has_side_effects=True),
        cost_estimate=cost(2.6e10, 8e7),
        name="weight_grads",
    )(acts, ghs, cot, rows_in, ub, dx)


def gather_rows(tcol, parts):
    total = None
    for c, part in enumerate(parts):
        rows = part.shape[0]
        hot = (
            lax.broadcasted_iota(jnp.int32, (tcol.shape[0], rows), 1) + c * rows == tcol[:, 0:1]
        ).astype(F32).astype(BF)
        term = dot(hot, part)
        total = term if total is None else total + term
    return total


def norm_back(grad, unit, inverse, gain):
    scaled = grad * gain
    inner = jnp.mean(scaled, axis=-1, keepdims=True)
    along = jnp.mean(scaled * unit, axis=-1, keepdims=True)
    return inverse * (scaled - inner - unit * along)


def middle_back_kernel(
    n, cc, blocks, tcol_ref, g0_any, g1_any, g2_any, mid_ref, cot_ref, gain_ref, own_any, oth_any, att_any, y_src,
    gmid_ref, gatt_ref, pg_own, pg_oth, small_ref, y_dst,
    gb_s, g0, g1, g2, own_ref, oth_ref, att_t, send, recv, local, lsem,
):
    route = Route(
        n, lambda e: y_src.at[0, block_of(e, cc)], lambda d: y_dst.at[block_of(d, cc)],
        send.at[0], recv.at[0], local.at[0],
    )
    step = pl.program_id(0)
    half = own_ref.shape[0]
    tb = mid_ref.shape[0]

    def load(k):
        src = (g0_any, g1_any, g2_any, own_any, oth_any, att_any)[k]
        return pltpu.make_async_copy(src, (g0, g1, g2, own_ref, oth_ref, att_t)[k], lsem.at[k])

    @pl.when(step == 0)
    def _():
        for k in range(6):
            load(k).start()
        greet(n, False)
        route.start()
        small_ref[...] = jnp.zeros_like(small_ref)
        for k in range(5):
            load(k).wait()

    grad = gather_rows(tcol_ref[...], (g0[...], g1[...], g2[...]))
    grad = grad.astype(BF).astype(F32)
    unit, inverse = unit_of(mid_ref[...])
    gmid = cot_ref[...].astype(F32) + norm_back(grad, unit, inverse, row_of(gain_ref))
    gmid_ref[...] = gmid
    gb = gmid.astype(BF)
    gb_s[block_of(step, tb), :] = gb
    small_ref[2:3, :] += jnp.sum(grad * unit, axis=0, keepdims=True)
    small_ref[3:4, :] += jnp.sum(grad, axis=0, keepdims=True)
    small_ref[4:5, :] += jnp.sum(gb.astype(F32), axis=0, keepdims=True)
    gatt_ref[:, 0:half] = dot_nt(gb, own_ref[...]).astype(BF)
    gatt_ref[:, half:2 * half] = dot_nt(gb, oth_ref[...]).astype(BF)

    @pl.when(step == blocks - 1)
    def _():
        load(5).wait()
        pg_own[...] = dot(att_t[0:half, :], gb_s[...]).astype(BF)
        pg_oth[...] = dot(att_t[half:2 * half, :], gb_s[...]).astype(BF)
        route.wait()


def middle_back_call(n, cc, tcol, grads, middle, cot, gain, proj_own, proj_oth, att_t, y):
    tokens, width = middle.shape
    half = proj_own.shape[0]
    tb = 256
    rows = grads[0].shape[0]
    block = pl.BlockSpec((tb, width), lambda i: (i, 0))
    sds = jax.ShapeDtypeStruct
    return pl.pallas_call(
        functools.partial(middle_back_kernel, n, cc, tokens // tb),
        grid=(tokens // tb,),
        in_specs=[
            pl.BlockSpec((tb, 128), lambda i: (i, 0)), ANY, ANY, ANY, block, block,
            whole((width,)), ANY, ANY, ANY, ANY,
        ],
        out_specs=[block, block, whole((half, width)), whole((half, width)), whole((8, width)), ANY],
        out_shape=[
            sds((tokens, width), F32), sds((tokens, width), BF), sds((half, width), BF), sds((half, width), BF),
            sds((8, width), F32), sds((rows, width), BF),
        ],
        scratch_shapes=[
            pltpu.VMEM((tokens, width), BF), *[pltpu.VMEM((rows, width), BF)] * CHUNKS, pltpu.VMEM((half, width), BF),
            pltpu.VMEM((half, width), BF), pltpu.VMEM((width, tokens), BF), *route_sems(n, 1),
            pltpu.SemaphoreType.DMA((6,)),
        ],
        compiler_params=params(collective_id=4, has_side_effects=True),
        cost_estimate=cost(1.2e10, 3e7),
        name="middle_back",
    )(tcol, *grads, middle, cot, gain, proj_own, proj_oth, att_t, y)


class Part:
    def __init__(self, index, base, length, order, me, refs, sems):
        self.index, self.base, self.total, self.order, self.me = index, base, length, order, me
        self.acc, self.rcv, self.res = refs
        self.rs_send, self.rs_recv, self.ag_send, self.ag_recv = sems
        self.stages, self.stage = len(order), 0
        self.step = length >> len(order)

    def upper(self, s):
        return lax.rem(lax.div(self.me, 1 << self.order[s]), 2)

    def rows(self, start, length):
        return pl.ds(pl.multiple_of(start, 16), length)

    def start(self, s):
        at = self.base
        for k in range(s):
            at = at + self.upper(k) * (self.total >> (k + 1))
        return at

    def slot(self, s):
        return self.base + self.total - (self.total >> s)

    def copy(self):
        inward = self.stage < self.stages
        s = self.stage if inward else 2 * self.stages - 1 - self.stage
        bit = 1 << self.order[s]
        peer = {"expert": self.me + bit - 2 * bit * self.upper(s)}
        if inward:
            half = self.total >> (s + 1)
            away = self.start(s) + (1 - self.upper(s)) * half
            src, dst = self.acc.at[self.rows(away, half)], self.rcv.at[pl.ds(self.slot(s), half)]
            send, recv = self.rs_send, self.rs_recv
        else:
            src = dst = self.res.at[self.rows(self.start(s + 1), self.total >> (s + 1))]
            send, recv = self.ag_send, self.ag_recv
        return pltpu.make_async_remote_copy(
            src, dst, send.at[self.index, s], recv.at[self.index, s], device_id=peer, device_id_type=MESH
        )

    def begin(self):
        self.copy().start()

    def advance(self):
        self.copy().wait()
        s = self.stage
        if s < self.stages:
            keep, slot, step = self.start(s + 1), self.slot(s), self.step
            into = self.res if s == self.stages - 1 else self.acc

            def add(b, _):
                at = self.rows(keep + b * step, step)
                into[at, :] = (
                    self.acc[at, :].astype(F32) + self.rcv[self.rows(slot + b * step, step), :].astype(F32)
                ).astype(BF)
                return 0

            lax.fori_loop(0, (self.total >> (s + 1)) // step, add, 0)
        self.stage += 1
        if self.stage < 2 * self.stages:
            self.copy().start()


def back_kernel(
    n, cc, groups, q_ref, k_ref, v_ref, prob_ref, do_ref, o_ref, x_any, norm_any, own_any, oth_any,
    gain_ref, small_ref, pg_own, pg_oth, gmid_any, y_src,
    xg_out, small_out, sum_q, sum_p, z1, z2,
    xg_ref, x_ref, norm_t, own_ref, oth_ref, dk_s, dv_s, gh_s, gnp_s, acc, rcv, res, p_acc, p_rcv, p_res, got, pgot, snd, mine_s, small_got,
    send, recv, local, dsend, drecv, rs_send, rs_recv, ag_send, ag_recv, sm_send, sm_recv, out_sem,
):
    step = pl.program_id(0)
    tokens, width = x_ref.shape
    half = own_ref.shape[2]
    scale = HEAD_DIM ** -0.5
    last = 3 * groups
    kind, group = lax.rem(step, 3), lax.div(step, 3)
    me = lax.axis_index("expert")
    stages = n.bit_length() - 1
    routes = [
        Route(
            n, lambda e, c=c: y_src.at[c, block_of(e, cc)], lambda d, z=z: z.at[block_of(d, cc)],
            send.at[c - 1], recv.at[c - 1], local.at[c - 1],
        )
        for c, z in ((1, z1), (2, z2))
    ]

    split = 2 if width >= 32 * n else 1
    size = width // split
    sems = (rs_send, rs_recv, ag_send, ag_recv)
    order = list(range(stages))
    swapped = [1, 0, *order[2:]]

    def parts_of(first, at, refs):
        return [
            Part(first + i, at * width + i * size, size, order if i % 2 == 0 else swapped, me, refs, sems)
            for i in range(split)
        ]

    head_parts = [parts_of(k * split, k, (acc, rcv, res)) for k in range(groups)]
    proj_parts = parts_of(groups * split, 0, (p_acc, p_rcv, p_res))

    def dp_swap(k):
        src, dst = (snd.at[k], got.at[k]) if k < groups else (pg_oth, pgot)
        return to_partner(src, dst, dsend.at[k], drecv.at[k])

    def bring_to(parts, goal):
        while parts[0].stage < min(goal, 2 * stages):
            for p in parts:
                p.advance()

    def fetch(k):
        src = (gmid_any, norm_any, own_any, oth_any, x_any)[k]
        dst = (xg_ref, norm_t, own_ref, oth_ref, x_ref)[k]
        return pltpu.make_async_copy(src, dst, out_sem.at[2 + k])

    @pl.when(step == 0)
    def _():
        greet(n, True)
        dp_swap(groups).start()
        for r in routes:
            r.start()
        for k in (1, 2, 3, 4, 0):
            fetch(k).start()

    @pl.when((kind < 2) & (step < last))
    def _():
        side, lanes = 1 - kind, block_of(group, 128)
        dk_s[...] = jnp.zeros_like(dk_s)
        dv_s[...] = jnp.zeros_like(dv_s)
        for i in range(BLOCKS):
            w, s = WIDTH[i], START[i]
            at = slice(i * QB, (i + 1) * QB)
            keys, values = k_ref[0, s:s + w, :], v_ref[0, s:s + w, :]
            go = do_ref[at, :]
            prod = go.astype(F32) * o_ref[at, :].astype(F32)
            query = q_ref[0, at, :]
            query, go_two = two_heads(query), two_heads(go)
            inner = jnp.concatenate(
                [jnp.sum(jnp.where(lane_pick(128, j == 0), prod, 0.0), axis=-1, keepdims=True) for j in range(2)], axis=0
            )
            probs = prob_ref[:, :, OFFSET[i]:OFFSET[i] + w].reshape(2 * QB, w)
            gp = dot_nt(go_two, values)
            gs = (probs.astype(F32) * (gp - inner)).astype(BF)
            gq = dot(gs, keys)
            dk_s[s:s + w, :] += dot_tn(gs, query)
            dv_s[s:s + w, :] += dot_tn(probs, go_two)
            gh_s[3 * side, at, lanes] = (jnp.where(lane_pick(128, True), gq[0:QB], gq[QB:2 * QB]) * scale).astype(BF)
        gh_s[3 * side + 1, :, lanes] = (dk_s[...] * scale).astype(BF)
        gh_s[3 * side + 2, :, lanes] = dv_s[...].astype(BF)

    for k in range(groups):
        @pl.when(step == 3 * k + 2)
        def _():
            if k == 0:
                fetch(1).wait()
            at = slice(k * 128, (k + 1) * 128)
            for c in range(3):
                both = dot(norm_t[...], jnp.concatenate([gh_s[3 + c, :, at], gh_s[c, :, at]], axis=1))
                snd[k, :, c * 128:(c + 1) * 128] = both[:, 0:128].astype(BF)
                mine_s[:, c * 128:(c + 1) * 128] = both[:, 128:256]
            dp_swap(k).start()

        @pl.when(step == 3 * k + 3)
        def _():
            dp_swap(k).wait()
            acc[k * width:(k + 1) * width, :] = (mine_s[...] + got[k].astype(F32)).astype(BF)
            for p in head_parts[k]:
                p.begin()

    @pl.when(step == 1)
    def _():
        dp_swap(groups).wait()
        rows = pgot.shape[0]
        for b in range(width // rows):
            at = slice(b * rows, (b + 1) * rows)
            p_acc[at, :] = (pg_own[:, at].astype(F32) + pgot[:, at].astype(F32)).astype(BF)
        for p in proj_parts:
            p.begin()

    for t in range(3, last):
        @pl.when(step == t)
        def _():
            bring_to(proj_parts, sum(t >= m for m in (5, 7, 9, 11)))
            for k in range(groups):
                bring_to(head_parts[k], sum(t >= 3 * k + m for m in (7, 9, 11)))

    @pl.when(step == last)
    def _():
        def small_swap(k):
            if k == 0:
                peer = {"dp": 1 - lax.axis_index("dp")}
            else:
                bit = 1 << (k - 1)
                peer = {"expert": me + bit - 2 * bit * lax.rem(lax.div(me, bit), 2)}
            return pltpu.make_async_remote_copy(
                small_out, small_got.at[k], sm_send.at[k], sm_recv.at[k], device_id=peer, device_id_type=MESH
            )

        def turn():
            for some in [proj_parts, *head_parts]:
                for p in some:
                    if p.stage < 2 * stages:
                        p.advance()

        fetch(2).wait()
        fetch(3).wait()
        for c in range(3):
            if c:
                turn()
            term = dot_nt(gh_s[c], own_ref[c]) + dot_nt(gh_s[3 + c], oth_ref[c])
            if c:
                gnp_s[...] += term
            else:
                gnp_s[...] = term
        turn()
        fetch(0).wait()
        fetch(4).wait()
        small_out[...] = small_ref[...]

        def body(b, _):
            at = block_of(b, 128)
            grad = gnp_s[at, :]
            unit, inverse = unit_of(x_ref[at, :].astype(F32))
            xg_ref[at, :] = xg_ref[at, :] + norm_back(grad, unit, inverse, row_of(gain_ref))
            small_out[0:1, :] += jnp.sum(grad * unit, axis=0, keepdims=True)
            small_out[1:2, :] += jnp.sum(grad, axis=0, keepdims=True)
            return 0

        lax.fori_loop(0, tokens // 128, body, 0)
        done = pltpu.make_async_copy(xg_ref, xg_out, out_sem.at[7])
        done.start()
        small = small_swap(0)
        small.start()
        for s in range(2 * stages - 2):
            turn()
            if s <= stages:
                small.wait()
                small_out[...] += small_got[s]
                if s < stages:
                    small = small_swap(s + 1)
                    small.start()
        outs = [
            pltpu.make_async_copy(res, sum_q, out_sem.at[0]),
            pltpu.make_async_copy(p_res, sum_p, out_sem.at[1]),
        ]
        for out in outs:
            out.start()
        for out in outs:
            out.wait()
        done.wait()
        for r in routes:
            r.wait()


def back_call(n, cc, head_rows, probs, gatt, att, x, norm_t, own, oth, gmid, gain, small, pg_own, pg_oth, y):
    tokens, width = x.shape
    half = own.shape[2]
    groups = half // 128
    last = 3 * groups
    rows = n * cc
    stages = n.bit_length() - 1
    parts = (groups + 1) * (2 if width >= 32 * n else 1)
    sds, dma, once = jax.ShapeDtypeStruct, pltpu.SemaphoreType.DMA, pl.Buffered(1)

    def place(i):
        i = jnp.minimum(i, last - 1)
        return jnp.maximum(1 - i % 3, 0), i // 3

    def head(c):
        def index(i):
            side, k = place(i)
            return (3 * side + c, 0, k)

        return pl.BlockSpec((1, tokens, 128), index)

    def pair(i):
        side, k = place(i)
        return side * groups + k

    def fixed(shape):
        return pl.BlockSpec(shape, lambda *_: (0,) * len(shape), pipeline_mode=once)

    cols = pl.BlockSpec((tokens, 128), lambda i: (0, pair(i)))
    sums = pltpu.VMEM((groups * width, 384), BF)
    p_sums = pltpu.VMEM((width, half), BF)
    return pl.pallas_call(
        functools.partial(back_kernel, n, cc, groups),
        grid=(last + 1,),
        in_specs=[
            head(0), head(1), head(2), pl.BlockSpec((2, QB, BAND), lambda i: (pair(i), 0, 0)), cols, cols,
            ANY, ANY, ANY, ANY,
            fixed((width,)), fixed(small.shape), fixed((half, width)), ANY, ANY, ANY,
        ],
        out_specs=[ANY, fixed(small.shape), ANY, ANY, ANY, ANY],
        out_shape=[
            sds((tokens, width), F32), sds(small.shape, F32), sds((groups * width, 384), BF), sds((width, half), BF),
            sds((rows, width), BF), sds((rows, width), BF),
        ],
        scratch_shapes=[
            pltpu.VMEM((tokens, width), F32),
            pltpu.VMEM((tokens, width), BF), pltpu.VMEM((width, tokens), BF), pltpu.VMEM(own.shape, BF), pltpu.VMEM(oth.shape, BF),
            pltpu.VMEM((tokens, 128), F32), pltpu.VMEM((tokens, 128), F32), pltpu.VMEM((6, tokens, half), BF),
            pltpu.VMEM((tokens, width), F32), sums, sums, sums, p_sums, p_sums, p_sums,
            pltpu.VMEM((groups, width, 384), BF), pltpu.VMEM((half, width), BF),
            pltpu.VMEM((groups, width, 384), BF), pltpu.VMEM((width, 384), F32),
            pltpu.VMEM((1 + stages, *small.shape), F32),
            *route_sems(n, 2), dma((groups + 1,)), dma((groups + 1,)), dma((parts, stages)), dma((parts, stages)),
            dma((parts, stages)), dma((parts, stages)), dma((1 + stages,)), dma((1 + stages,)), dma((8,)),
        ],
        compiler_params=params(collective_id=5, has_side_effects=True),
        cost_estimate=cost(5.3e10, 9e7),
        name="back",
    )(
        head_rows, head_rows, head_rows, probs, gatt, att, x, norm_t, own, oth, gain, small, pg_own, pg_oth, gmid, y
    )


def result_kernel(tcol_ref, z0, z1, z2, mid_ref, sum_q, sum_p, xg_ref, wd_ref, wu_ref, small_ref, out_ref, q_ref, p_ref, xo_ref, do_ref, uo_ref, *smalls):
    rows = gather_rows(tcol_ref[...], (z0[...], z1[...], z2[...]))
    out_ref[...] = (mid_ref[...] + rows.astype(BF).astype(F32)).astype(BF)
    for c in range(3):
        for k in range(sum_q.shape[0]):
            q_ref[c, :, k * 128:(k + 1) * 128] = sum_q[k, :, c * 128:(c + 1) * 128].astype(F32)
    half = sum_p.shape[2]
    for b in range(sum_p.shape[0]):
        p_ref[:, b * half:(b + 1) * half] = sum_p[b].astype(F32)
    xo_ref[...] = xg_ref[...]
    do_ref[...] = wd_ref[...].astype(F32)
    uo_ref[...] = wu_ref[...].astype(F32)
    for k, small in enumerate(smalls):
        small[...] = small_ref[k:k + 1, :].reshape(small.shape)


def result_call(tcol, zs, middle, sum_q, sum_p, xg, wd, wu, small):
    tokens, width = middle.shape
    half = sum_p.shape[1]
    groups = half // 128
    hid = wd.shape[0]
    rows = zs[0].shape[0]
    steps = 8
    tb, qb, pb, wb = tokens // steps, width // steps, half // steps, hid // steps
    sds = jax.ShapeDtypeStruct
    sum_q = sum_q.reshape(groups, width, 384)
    sum_p = sum_p.reshape(width // half, half, half)

    def rows_of(size, cols):
        return pl.BlockSpec((size, cols), lambda i: (i, 0))

    return pl.pallas_call(
        result_kernel,
        grid=(steps,),
        in_specs=[
            rows_of(tb, 128), *[whole((rows, width))] * 3, rows_of(tb, width),
            pl.BlockSpec((groups, qb, 384), lambda i: (0, i, 0)),
            pl.BlockSpec((width // half, pb, half), lambda i: (0, i, 0)), rows_of(tb, width), rows_of(wb, width),
            rows_of(wb, width), whole(small.shape),
        ],
        out_specs=[
            rows_of(tb, width), pl.BlockSpec((3, qb, half), lambda i: (0, i, 0)), rows_of(pb, width),
            rows_of(tb, width), rows_of(wb, width), rows_of(wb, width), *[whole((width,))] * 5,
        ],
        out_shape=[
            sds((tokens, width), BF), sds((3, width, half), F32), sds((half, width), F32), sds((tokens, width), F32),
            sds((hid, width), F32), sds((hid, width), F32), *[sds((width,), F32)] * 5,
        ],
        compiler_params=params(),
        cost_estimate=cost(6 * tokens * rows * width, 6e7),
        name="results",
    )(tcol, *zs, middle, sum_q, sum_p, xg, wd, wu, small)


def on_device(
    tokens, cotangent, segment_ids, expert_ids, qkv_weight, proj_weight, proj_bias, pre_gain, pre_shift,
    mid_gain, mid_shift, up_weight, up_bias, down_weight, down_bias,
):
    n = lax.axis_size("expert")
    count, width = tokens.shape
    cc = 3 * count // (2 * n) // CHUNKS

    def swap(v):
        return lax.ppermute(v, "dp", [(0, 1), (1, 0)])

    down_own, up_own = down_weight[0], up_weight[0]
    up, down = (up_own, swap(up_own)), (down_own, swap(down_own))
    bias = (up_bias, swap(up_bias))
    vectors = (pre_gain, pre_shift, proj_bias, mid_gain, mid_shift)

    tcol, norm_t, head_rows, att, att_t, probs, middle, mid_slots, cot_rows, qkv_oth, proj_oth = front_call(
        n, cc, expert_ids.reshape(1, count), cotangent, tokens, segment_ids, vectors, qkv_weight, proj_weight)
    acts, ghs, ub, y, dx, arrived, gm0 = expert_call(n, cc, mid_slots, cot_rows, up, down, bias, down_bias)
    down_grad, up_grad, upbias_grad, downbias_grad, gm1, gm2 = wgrad_call(n, cc, acts, ghs, cot_rows, arrived, ub, dx)

    gmid, gatt, pg_own, pg_oth, small, z0 = middle_back_call(
        n, cc, tcol, (gm0, gm1, gm2), middle, cotangent, mid_gain, proj_weight, proj_oth, att_t, y)
    input_grad, small, sum_q, sum_p, z1, z2 = back_call(
        n, cc, head_rows, probs, gatt, att, tokens, norm_t, qkv_weight, qkv_oth, gmid, pre_gain, small, pg_own, pg_oth, y)
    output, qkv_grad, proj_grad, input_grad, down_grad, up_grad, pregain, preshift, midgain, midshift, projbias = result_call(
        tcol, (z0, z1, z2), middle, sum_q, sum_p, input_grad, down_grad, up_grad, small)
    return (
        output, input_grad, qkv_grad, proj_grad, projbias, pregain, preshift, midgain, midshift,
        up_grad[None], upbias_grad, down_grad[None], downbias_grad,
    )


def solution(mesh):
    token = P(("dp", "expert"), None)
    in_specs = (
        token, token, token, token, P(None, None, "dp"), P("dp", None), P(), P(), P(), P(), P(),
        P("expert", "dp", None), P("expert", "dp"), P("expert", "dp", None), P("expert", None),
    )
    out_specs = (
        token, token, P(None, None, "dp"), P("dp", None), P(), P(), P(), P(), P(),
        P("expert", "dp", None), P("expert", "dp"), P("expert", "dp", None), P("expert", None),
    )
    return jax.shard_map(on_device, mesh=mesh, in_specs=in_specs, out_specs=out_specs, check_vma=False)
```
